32 devices in a mesh: region: 8 (over z, y), local: 4 (over x, core).
Axes of the slice: x: 2, y: 2, z: 4, core: 2. Of those that a mesh axis runs over, the one named last changes fastest.
Arguments:
- atm_flux: bfloat16 [12, 131072], P(None, ('region', 'local')), may hold values from -6 to 6
- cell_map: int32 [32, 4096], P(('region', 'local')), may hold values from 0 to 4095, each once within a row
- neighbours: int32 [4, 131072], P(None, ('region', 'local')), may hold values from 0 to 4095
- coef_x: float32 [4, 131072], P(None, ('region', 'local')), may hold values from -3 to 3
- coef_y: float32 [4, 131072], P(None, ('region', 'local')), may hold values from -3 to 3
- send_list: int32 [32, 4, 4], P(('region', 'local')), may hold values from 0 to 31, as said below
- cover: int32 [128, 4], P(('region', 'local')), may hold values from 0 to 15, as said below
- cover_count: int32 [128], P(('region', 'local')), may hold values from 1 to 4
- weights: bfloat16 [128, 4, 3, 128, 128], P(('region', 'local')), may hold values from -0.15625 to 0.15625
- ocean_map: int32 [32, 512], P(('region', 'local')), may hold values from 0 to 511, each once within a row
Outputs:
- ocean_flux: float32 [12, 16384], P(None, ('region', 'local'))
The draws below stay inside these ranges and needn't reach their ends.
Inputs may be any that keep to these rules, and one draw needn't show every extreme that they name: `cell_map`: each row is a permutation of one device's cells. `neighbours`: indices of coupler cells on the same device. `send_list`: each row lists 4 different source blocks of the sending device. `cover`: each row lists 4 different slots of what the owner receives from its region. `ocean_map`: each row is a permutation of one device's ocean cells.
All inputs are finite; a program needn't handle non-finite values.
Results may differ from the reference program's by a relative error of at most 0.0024.
Values may be sent and summed in bfloat16 or wider, within the bound.
No kernel may reach another device: no remote copies, remote signals or barrier semaphores. Data moves between devices by JAX's collectives and lax.ppermute only.
A program may use at most 64 MiB of HBM per device.

```python
import jax
import jax.numpy as jnp
from jax import lax

F = 12
BS = 128
OS = 128
NB = 4
K = 4
CAP = 4
A_DEV = 4096
OBLK = 4
NDEV = 32
ABLK = 32
O_DEV = 512
ACELLS = 131072
OBLOCKS = 128
N_REGION = 8
N_LOCAL = 4


def draw_send_list(key, part):
    key = jax.random.fold_in(key, 11)
    base = jnp.broadcast_to(jnp.arange(ABLK, dtype=jnp.int32), (NDEV, N_LOCAL, ABLK))
    shuffled = jax.random.permutation(key, base, axis=2, independent=True)
    return shuffled[:, :, :CAP].astype(jnp.int32)


def draw_cover(key, part):
    key = jax.random.fold_in(key, 23)
    base = jnp.broadcast_to(jnp.arange(N_LOCAL * CAP, dtype=jnp.int32), (OBLOCKS, N_LOCAL * CAP))
    shuffled = jax.random.permutation(key, base, axis=1, independent=True)
    return shuffled[:, :K].astype(jnp.int32)


def place_ends(array, stream_key, least, largest):
    index_at = [jax.random.randint(jax.random.fold_in(stream_key, axis), (), 0, length) for axis, length in enumerate(array.shape)]
    widest = array.shape.index(max(array.shape))
    beside = index_at[:widest] + [(index_at[widest] + 1) % array.shape[widest]] + index_at[widest + 1:]
    return array.at[tuple(index_at)].set(least).at[tuple(beside)].set(largest)


def shard_levels(stream_key, shape, shards, least, top_value):
    loudness, own = 1.0, jax.random.fold_in(stream_key, 6)
    for axis_at, shards_of in shards:
        steps = jnp.exp(jax.random.uniform(jax.random.fold_in(own, axis_at), (shards_of,), jnp.float32, least / len(shards), top_value / len(shards)))
        loudness = loudness * jnp.repeat(steps, shape[axis_at] // shards_of).reshape([-1 if axis == axis_at else 1 for axis in range(len(shape))])
    return loudness


def centred(own_key, shape, deviation, most, pieces=(), kind=jnp.bfloat16):
    values = jax.random.normal(own_key, shape, jnp.float32) * deviation
    if len(pieces) > 0:
        values = shard_levels(own_key, shape, pieces, -0.22, 0.18) * values
    return jnp.clip(values, min=-most, max=most).astype(kind)


def setup_inputs(seed: int = 0) -> dict:
    key_of = jax.random.split(jax.random.key(seed), 11)
    return {
        "atm_flux": centred(key_of[0], (F, ACELLS), 1.0, 6.0, ((1, 32),)),
        "cell_map": jax.vmap(lambda own: jax.random.permutation(own, A_DEV))(jax.random.split(key_of[1], NDEV)).reshape((NDEV, A_DEV)).astype(jnp.int32),
        "neighbours": place_ends(jax.random.randint(key_of[2], (NB, ACELLS), 0, A_DEV), jax.random.fold_in(key_of[2], 1), 0, A_DEV - 1).astype(jnp.int32),
        "coef_x": centred(key_of[3], (NB, ACELLS), 0.5, 3.0, ((1, 32),), jnp.float32),
        "coef_y": centred(key_of[4], (NB, ACELLS), 0.5, 3.0, ((1, 32),), jnp.float32),
        "send_list": draw_send_list(jax.random.fold_in(key_of[10], 71), 0),
        "cover": draw_cover(jax.random.fold_in(key_of[10], 71), 0),
        "cover_count": place_ends(jax.random.randint(key_of[7], (OBLOCKS,), 1, K + 1), jax.random.fold_in(key_of[7], 1), 1, K).astype(jnp.int32),
        "weights": centred(key_of[8], (OBLOCKS, K, 3, OS, BS), (3 * K * BS) ** -0.5, 0.15625, ((0, 32),)),
        "ocean_map": jax.vmap(lambda own: jax.random.permutation(own, O_DEV))(jax.random.split(key_of[9], NDEV)).reshape((NDEV, O_DEV)).astype(jnp.int32),
    }


def reconstruct(values, near_index, weight_x, weight_y):
    nearby = values[:, near_index]
    change = nearby - values[:, None, :]
    slope_x = jnp.sum(weight_x[None] * change, axis=1)
    slope_y = jnp.sum(weight_y[None] * change, axis=1)
    upper = jnp.maximum(values, jnp.max(nearby, axis=1))
    lower = jnp.minimum(values, jnp.min(nearby, axis=1))
    steep = jnp.abs(slope_x) + jnp.abs(slope_y)
    factor = jnp.minimum(1.0, (upper - lower) / jnp.maximum(steep, 1.0))
    return jnp.stack([values, factor * slope_x, factor * slope_y]).astype(jnp.bfloat16)


def reconstruct_packed(packed):
    return reconstruct(packed[0], packed[1], packed[2], packed[3])


def reference(atm_flux, cell_map, neighbours, coef_x, coef_y, send_list, cover, cover_count, weights, ocean_map):
    devices = N_REGION * N_LOCAL
    piece = A_DEV // devices
    source = atm_flux.reshape(F, devices, A_DEV)
    ordered = jnp.take_along_axis(source, cell_map[None], axis=2)
    coupled = ordered.reshape(F, devices, devices, piece).transpose(2, 0, 1, 3)
    coupled = coupled.reshape(devices, F, A_DEV).astype(jnp.float32)
    near_dev = neighbours.reshape(NB, devices, A_DEV).transpose(1, 0, 2)
    along_x = coef_x.reshape(NB, devices, A_DEV).transpose(1, 0, 2)
    along_y = coef_y.reshape(NB, devices, A_DEV).transpose(1, 0, 2)
    recon = lax.map(reconstruct_packed, (coupled, near_dev, along_x, along_y))
    recon = recon.reshape(devices, 3, F, A_DEV // BS, BS)
    cover_dev = cover.reshape(devices, OBLK, K)
    count_dev = cover_count.reshape(devices, OBLK)
    weight_dev = weights.reshape(devices, OBLK, K, 3, OS, BS)

    def remap_one(packed):
        device, covers, counts, block_weights = packed
        region = device // N_LOCAL
        member = device % N_LOCAL
        sender = region * N_LOCAL + covers // CAP
        blocks = send_list[sender, member, covers % CAP]
        chosen = recon[sender, :, :, blocks]
        live = (jnp.arange(K, dtype=jnp.int32)[None, :] < counts[:, None]).astype(jnp.float32)
        chosen = chosen.astype(jnp.float32) * live[:, :, None, None, None]
        result = jnp.einsum("bkmos,bkmfs->fbo", block_weights.astype(jnp.float32), chosen,
                            precision=lax.Precision.HIGHEST)
        return result.reshape(F, OBLK * OS)

    remapped = lax.map(remap_one, (jnp.arange(devices, dtype=jnp.int32), cover_dev, count_dev, weight_dev))
    leaving = jnp.take_along_axis(remapped, ocean_map[:, None, :], axis=2)
    share = O_DEV // N_REGION
    ocean = leaving.reshape(N_REGION, N_LOCAL, F, N_REGION, share).transpose(2, 3, 1, 0, 4)
    return ocean.reshape(F, devices * O_DEV)
```

```python
import functools

import jax
import jax.numpy as jnp
from jax import lax
from jax.experimental import pallas as pl
from jax.experimental.pallas import tpu as pltpu
from jax.sharding import PartitionSpec as P

ROWS = 16
HALF = 8
LANES = 128
DEPTH = 256
PER_ROW = DEPTH // LANES
STEP = 1024
WIDTH = 256
VMEM_LIMIT = 40 * 1024 * 1024


def lookup(table, index):
    row = lax.broadcasted_iota(jnp.int32, (DEPTH, WIDTH), 0).astype(jnp.bfloat16)
    results = []
    for at in range(0, index.shape[1], WIDTH):
        here = index[:, at : at + WIDTH]
        low = (here & (DEPTH - 1)).astype(jnp.bfloat16)
        hot = jnp.where(row == low, jnp.bfloat16(1), jnp.bfloat16(0))
        found = jnp.dot(table, hot, preferred_element_type=jnp.float32)
        high = jnp.broadcast_to(here // DEPTH, (ROWS, WIDTH))
        result = found[:ROWS]
        for part in range(1, table.shape[0] // ROWS):
            result = jnp.where(high == part, found[part * ROWS : (part + 1) * ROWS], result)
        results.append(result)
    return jnp.concatenate(results, axis=1)


def copies_of(sources, targets, sems, first=0):
    return [
        pltpu.make_async_copy(source, target, sems.at[first + at])
        for at, (source, target) in enumerate(zip(sources, targets))
    ]


def message_rows(fields, twins):
    return 2 * fields if twins == 2 else ROWS


def order_kernel(twins, map_hbm, flux_hbm, out_hbm, map_ref, flux_ref, out_ref, table, sems):
    fields, cells = flux_ref.shape
    steps = cells // STEP
    spans = [pl.ds(step * STEP, STEP) for step in range(steps)]
    needed = copies_of([flux_hbm.at[:, span] for span in spans], [flux_ref.at[:, span] for span in spans], sems)
    needed += copies_of((map_hbm,), (map_ref,), sems, 2 * steps)
    for copy in needed:
        copy.start()
    table[...] = jnp.zeros_like(table)
    for copy in needed:
        copy.wait()
    for part in range(cells // DEPTH):
        table[part * ROWS : part * ROWS + fields] = flux_ref[:, part * DEPTH : (part + 1) * DEPTH]
    rows = message_rows(fields, twins)
    written = []
    for step in range(steps):
        found = lookup(table[...], map_ref[:, step * STEP : (step + 1) * STEP])
        pieces = [found[:, at : at + LANES] for at in range(0, STEP, LANES)]
        if twins == 2:
            pieces = [
                jnp.concatenate([pieces[at][:fields], pieces[at ^ 2][:fields]], axis=0) for at in range(len(pieces))
            ]
        for at, piece in enumerate(pieces):
            first = (step * len(pieces) + at) * rows
            out_ref[first : first + rows] = piece.astype(jnp.bfloat16)
        span = pl.ds(step * len(pieces) * rows, len(pieces) * rows)
        written.append(pltpu.make_async_copy(out_ref.at[span], out_hbm.at[span], sems.at[steps + step]))
        written[-1].start()
    for copy in written:
        copy.wait()


def select_kernel(after_ref, list_hbm, near_hbm, x_hbm, y_hbm, *refs):
    selected, (list_ref, near_ref, x_ref, y_ref, sems) = refs[:-5], refs[-5:]
    copies = copies_of((list_hbm, near_hbm, x_hbm, y_hbm), (list_ref, near_ref, x_ref, y_ref), sems)
    for copy in copies:
        copy.start()
    for copy in copies:
        copy.wait()
    me = lax.axis_index("local")
    cap = list_ref.shape[2]
    count = list_ref.shape[1] // len(selected)
    near_count = near_ref.shape[0]
    for twin, stencil_ref in reversed(list(enumerate(selected))):
        for at in range(count * cap):
            block = list_ref[0, me ^ (2 * twin) ^ (at // cap), at % cap]
            columns = pl.ds(pl.multiple_of(block * LANES, LANES), LANES)
            stencil_ref[at, :near_count] = near_ref[:, columns].astype(jnp.float32)
            stencil_ref[at, near_count : 2 * near_count] = x_ref[:, columns]
            stencil_ref[at, 2 * near_count : 3 * near_count] = y_ref[:, columns]
            rest = (ROWS - 3 * near_count, LANES)
            stencil_ref[at, 3 * near_count :] = jnp.broadcast_to(block, rest).astype(jnp.float32)


def fetch_kernel(after_ref, map_hbm, *refs):
    count = (len(refs) - 3) // 2
    sources, moves_ref, targets, (map_ref, sems) = refs[:count], refs[count], refs[count + 1 : -2], refs[-2:]
    (needed,) = copies_of((map_hbm,), (map_ref,), sems, count)
    others = copies_of(sources, targets, sems)
    for copy in [needed] + others:
        copy.start()
    needed.wait()
    moves = lax.broadcasted_iota(jnp.int32, moves_ref.shape, 0) == map_ref[...]
    moves_ref[...] = jnp.where(moves, 1.0, 0.0).astype(jnp.bfloat16)
    for copy in others:
        copy.wait()


def rebuild(near_count, table, stencil, own, shift):
    near = stencil[:near_count].astype(jnp.int32)
    index = jnp.concatenate([near[j : j + 1] for j in range(near_count)], axis=1)
    found = lookup(table, index)
    upper = lower = own
    slope_x = slope_y = jnp.zeros_like(own)
    for j in range(near_count):
        value = found[:, j * LANES : (j + 1) * LANES]
        change = value - own
        slope_x += stencil[near_count + j : near_count + j + 1] * change
        slope_y += stencil[2 * near_count + j : 2 * near_count + j + 1] * change
        upper, lower = jnp.maximum(upper, value), jnp.minimum(lower, value)
    steep = jnp.abs(slope_x) + jnp.abs(slope_y)
    factor = jnp.minimum(1.0, (upper - lower) / jnp.maximum(steep, 1.0))
    results = [own, factor * slope_x, factor * slope_y]
    if shift:
        spare = jnp.zeros((shift, LANES), jnp.float32)
        results = [jnp.concatenate([result[shift:], spare], axis=0) for result in results]
    return results


def own_cells(near_count, table, stencil_ref):
    slots = stencil_ref.shape[0]
    tile = (ROWS, DEPTH)
    column = lax.broadcasted_iota(jnp.int32, tile, 1) - lax.broadcasted_iota(jnp.int32, tile, 0)
    blocks = [stencil_ref[at, 3 * near_count : 3 * near_count + 1].astype(jnp.int32) for at in range(slots)]
    picks = [
        jnp.where(jnp.concatenate([block // PER_ROW * ROWS] * PER_ROW, axis=1) == column, 1.0, 0.0) for block in blocks
    ]
    found = jnp.dot(
        jnp.concatenate(picks, axis=0).astype(jnp.bfloat16), table, preferred_element_type=jnp.float32
    )
    owns = []
    for at, block in enumerate(blocks):
        rows = found[at * ROWS : (at + 1) * ROWS]
        odd = jnp.broadcast_to(block % PER_ROW, (ROWS, LANES))
        owns.append(jnp.where(odd == 1, rows[:, LANES:], rows[:, :LANES]))
    return owns


def outer_kernel(twins, near_count, fields, after_ref, cells_ref, *refs):
    selected, refs = refs[:twins], refs[twins:]
    out_refs, (tables, owns) = refs[:-2], refs[-2:]
    cap = owns.shape[1]
    rows = message_rows(fields, twins)
    for twin in range(twins):
        for block in range(tables.shape[1] // ROWS * PER_ROW):
            part, column = block // PER_ROW, block % PER_ROW * LANES
            first = block * rows + HALF * twin
            tables[twin, part * ROWS : (part + 1) * ROWS, column : column + LANES] = cells_ref[first : first + ROWS]
    for twin, stencil_ref in enumerate(selected):
        for at, own in enumerate(own_cells(near_count, tables[twin], stencil_ref)):
            if at < cap:
                owns[twin, at] = own
                continue
            shift = twin * (fields - HALF)
            results = rebuild(near_count, tables[twin], stencil_ref[at], own, shift)
            for kind, result in enumerate(results):
                out_refs[at // cap - 1][twin, at % cap * len(results) + kind] = result.astype(jnp.bfloat16)


def inner_kernel(near_count, fields, tables, owns, *refs):
    selected, out_ref = refs[:-1], refs[-1]
    for twin, stencil_ref in enumerate(selected):
        for at in range(owns.shape[1]):
            own = owns[twin, at]
            shift = twin * (fields - HALF)
            results = rebuild(near_count, tables[twin], stencil_ref[at], own, shift)
            for kind, result in enumerate(results):
                out_ref[twin, at * len(results) + kind] = result.astype(jnp.bfloat16)


def remap_kernel(packed, fields, cover_ref, count_ref, weight_ref, moves_ref, *refs):
    received, (out_ref, source_ref) = refs[:-2], refs[-2:]
    me = lax.axis_index("local")
    ocean_blocks, slots, kinds = weight_ref.shape[:3]
    cap = source_ref.shape[1] // kinds
    for apart, piece_ref in enumerate(received):
        for twin in range(piece_ref.shape[0]):
            source_ref[me ^ apart ^ (2 * twin)] = piece_ref[twin]
    results = []
    for block in range(ocean_blocks):
        values, weights = [], []
        for slot in range(slots):
            at = cover_ref[block, slot]
            live = slot < count_ref[block]
            for kind in range(kinds):
                value = source_ref[at // cap, at % cap * kinds + kind]
                values.append(jnp.where(live, value, jnp.zeros_like(value)))
                weights.append(weight_ref[block, slot, kind])
        product = lax.dot_general(
            jnp.concatenate(values, axis=1),
            jnp.concatenate(weights, axis=1),
            (((1,), (1,)), ((), ())),
            preferred_element_type=jnp.float32,
        )
        results.append(product)
    remapped = jnp.concatenate(results, axis=1)
    cells = remapped.shape[1]
    coarse = remapped.astype(jnp.bfloat16)
    fine = (remapped - coarse.astype(jnp.float32)).astype(jnp.bfloat16)
    both = jnp.concatenate([coarse, fine], axis=0)
    moved = jnp.dot(both, moves_ref[...], preferred_element_type=jnp.float32)
    moved = moved[:ROWS] + moved[ROWS:]
    if not packed:
        out_ref[...] = moved[:fields]
        return
    half = fields // 2
    rows = out_ref.shape[1]
    listed = listing(out_ref.shape[0])
    side = lax.broadcasted_iota(jnp.int32, (rows, LANES), 1) < LANES // 2
    for pair in range(cells // LANES):
        columns = moved[:, pair * LANES : (pair + 1) * LANES]
        first, second = columns[:rows], columns[half : half + rows]
        out_ref[listed.index(2 * pair)] = jnp.where(side, first, pltpu.roll(second, LANES // 2, 1))
        out_ref[listed.index(2 * pair + 1)] = jnp.where(side, pltpu.roll(first, LANES // 2, 1), second)


def land_kernel(landed_ref, out_ref):
    count = landed_ref.shape[0]
    listed = listing(count)
    half = out_ref.shape[0] // 2
    side = lax.broadcasted_iota(jnp.int32, (half, LANES), 1) < LANES // 2
    for pair in range(count // 2):
        even, odd = landed_ref[listed.index(2 * pair), :half], landed_ref[listed.index(2 * pair + 1), :half]
        columns = pl.ds(pair * LANES, LANES)
        out_ref[:half, columns] = jnp.where(side, even, pltpu.roll(odd, LANES // 2, 1))
        out_ref[half:, columns] = jnp.where(side, pltpu.roll(even, LANES // 2, 1), odd)


def send(array, axis, apart):
    return lax.ppermute(array, axis, [(at, at ^ apart) for at in range(lax.axis_size(axis))])


def listing(count):
    return sorted(range(count), key=lambda at: (abs(2 * at - count + 1), -at))


def swap(pieces, axis):
    groups = [listing(lax.axis_size(axis))]
    pieces = pieces.transpose(1, 0, 2)
    swapped = lax.all_to_all(pieces, axis, split_axis=1, concat_axis=1, axis_index_groups=groups, tiled=True)
    return swapped.transpose(1, 0, 2)


SPACES = {"s": pltpu.SMEM, "v": pltpu.VMEM, "h": pltpu.HBM, "a": pl.ANY}


def call(kernel, outs, memories, scratch=(), out_memory="v", flops=0, moved=0):
    if isinstance(outs, list):
        out_specs = [pl.BlockSpec(memory_space=SPACES[kind]) for kind in (out_memory * len(outs))[: len(outs)]]
    else:
        out_specs = pl.BlockSpec(memory_space=SPACES[out_memory])
    return pl.pallas_call(
        kernel,
        out_shape=outs,
        in_specs=[pl.BlockSpec(memory_space=SPACES[kind]) for kind in memories],
        out_specs=out_specs,
        scratch_shapes=list(scratch),
        cost_estimate=pl.CostEstimate(flops=flops, bytes_accessed=moved, transcendentals=0),
        compiler_params=pltpu.CompilerParams(vmem_limit_bytes=VMEM_LIMIT),
    )


def shards(
    atm_flux,
    cell_map,
    neighbours,
    coef_x,
    coef_y,
    send_list,
    cover,
    cover_count,
    weights,
    ocean_map,
):
    fields, cells = atm_flux.shape
    region_count = lax.axis_size("region")
    local_count = lax.axis_size("local")
    everyone = ("region", "local")
    devices = region_count * local_count
    piece = cells // devices
    blocks = cells // LANES
    table = (cells // DEPTH * ROWS, DEPTH)
    shaped = jax.ShapeDtypeStruct
    twins = 2 if local_count == 4 and piece == LANES else 1
    cap = send_list.shape[2]
    aparts = local_count // twins
    near_count = neighbours.shape[0]
    kinds = weights.shape[2]
    ocean_cells = ocean_map.shape[1]

    def stay(*arrays):
        return [pltpu.with_memory_space_constraint(array, pltpu.HBM) for array in arrays]

    def scratch(array):
        return pltpu.VMEM(array.shape, array.dtype)

    rows = message_rows(fields, twins)
    messages = (blocks * rows, LANES)
    ordered = call(
        functools.partial(order_kernel, twins),
        shaped(messages, jnp.bfloat16),
        "hh",
        [
            scratch(cell_map),
            scratch(atm_flux),
            pltpu.VMEM(messages, jnp.bfloat16),
            pltpu.VMEM(table, jnp.bfloat16),
            pltpu.SemaphoreType.DMA((2 * (cells // STEP) + 1,)),
        ],
        out_memory="h",
    )(*stay(cell_map, atm_flux))

    stencil = shaped((aparts * cap, ROWS, LANES), jnp.float32)
    selected = call(
        select_kernel,
        [stencil] * twins,
        "ahhhh",
        [
            pltpu.SMEM(send_list.shape, send_list.dtype),
            scratch(neighbours),
            scratch(coef_x),
            scratch(coef_y),
            pltpu.SemaphoreType.DMA((4,)),
        ],
        moved=3_000_000,
    )(ordered, *stay(send_list, neighbours, coef_x, coef_y))
    selected = [selected[0]] + [send(array, "local", 2) for array in selected[1:]]

    later = [cover, cover_count, weights]
    moves, cover, cover_count, weights = call(
        fetch_kernel,
        [
            shaped((ocean_cells, ocean_cells), jnp.bfloat16),
            pltpu.SMEM(cover.shape, cover.dtype),
            pltpu.SMEM(cover_count.shape, cover_count.dtype),
            shaped(weights.shape, weights.dtype),
        ],
        "ah" + "h" * len(later),
        [scratch(ocean_map), pltpu.SemaphoreType.DMA((len(later) + 1,))],
        out_memory="vssv",
        moved=3_000_000,
    )(ordered, *stay(ocean_map, *later))

    if piece == LANES:
        coupled = lax.all_to_all(ordered, everyone, split_axis=0, concat_axis=0, tiled=True)
    else:
        outgoing = ordered.reshape(blocks, rows, LANES)[:, :fields].transpose(1, 0, 2).reshape(fields, devices, piece)
        coupled = lax.all_to_all(outgoing, everyone, split_axis=1, concat_axis=1, tiled=True)
        coupled = coupled.reshape(fields, blocks, LANES).transpose(1, 0, 2)
        coupled = jnp.pad(coupled, ((0, 0), (0, rows - fields), (0, 0))).reshape(messages)

    sent = shaped((twins, cap * kinds, ROWS, LANES), jnp.bfloat16)
    tables = shaped((twins,) + table, jnp.bfloat16)
    owns = shaped((twins, cap, ROWS, LANES), jnp.float32)
    work = 2 * twins * cap * table[0] * DEPTH * near_count * LANES
    *outer, tables, owns = call(
        functools.partial(outer_kernel, twins, near_count, fields),
        [sent] * (aparts - 1) + [tables, owns],
        "av" + "v" * twins,
        flops=work * (aparts - 1),
    )(moves, coupled, *selected)
    source = [send(array, "local", 1 + at) for at, array in enumerate(outer)]
    inner = call(
        functools.partial(inner_kernel, near_count, fields),
        sent,
        "vv" + "v" * twins,
        flops=work,
        moved=4_000_000,
    )(tables, owns, *selected)
    source = [inner] + source

    share = ocean_cells // region_count
    packed = share * 2 == LANES
    out_shape = (region_count, ROWS // 2, LANES) if packed else (fields, ocean_cells)
    leaving = call(
        functools.partial(remap_kernel, packed, fields),
        shaped(out_shape, jnp.float32),
        "ssvv" + "v" * aparts,
        [pltpu.VMEM((local_count, cap * kinds, ROWS, LANES), jnp.bfloat16)],
    )(cover, cover_count, weights, moves, *source)
    if packed:
        landed = swap(leaving, "region")
        return call(land_kernel, shaped((fields, ocean_cells), jnp.float32), "v")(landed)
    leaving = leaving.reshape(fields, region_count, share)
    landed = lax.all_to_all(leaving, "region", split_axis=1, concat_axis=1, tiled=True)
    return landed.reshape(fields, ocean_cells)


def solution(mesh):
    return jax.shard_map(
        shards,
        mesh=mesh,
        in_specs=(
            P(None, ("region", "local")),
            P(("region", "local"), None),
            P(None, ("region", "local")),
            P(None, ("region", "local")),
            P(None, ("region", "local")),
            P(("region", "local"), None, None),
            P(("region", "local"), None),
            P(("region", "local")),
            P(("region", "local"), None, None, None, None),
            P(("region", "local"), None),
        ),
        out_specs=P(None, ("region", "local")),
        check_vma=False,
    )
```

```python
import functools

import jax
import jax.numpy as jnp
from jax import lax
from jax.experimental import pallas as pl
from jax.experimental.pallas import tpu as pltpu
from jax.sharding import PartitionSpec as P

ROWS = 16
HALF = 8
LANES = 128
DEPTH = 256
PER_ROW = DEPTH // LANES
STEP = 512
WIDTH = 256
VMEM_LIMIT = 40 * 1024 * 1024


def one_hot(index):
    row = lax.broadcasted_iota(jnp.int32, (DEPTH, index.shape[1]), 0).astype(jnp.bfloat16)
    low = (index & (DEPTH - 1)).astype(jnp.bfloat16)
    return jnp.where(row == low, jnp.bfloat16(1), jnp.bfloat16(0))


def choose(found, high, height):
    high = jnp.broadcast_to(high, (height, found.shape[1]))
    result = found[:height]
    for part in range(1, found.shape[0] // height):
        result = jnp.where(high == part, found[part * height : (part + 1) * height], result)
    return result


def lookup(table, index):
    results = []
    for at in range(0, index.shape[1], WIDTH):
        here = index[:, at : at + WIDTH]
        found = jnp.dot(table, one_hot(here), preferred_element_type=jnp.float32)
        results.append(choose(found, here // DEPTH, ROWS))
    return jnp.concatenate(results, axis=1)


def lookup_dense(table, index, parts):
    results = []
    for at in range(0, index.shape[1], WIDTH):
        here = index[:, at : at + WIDTH]
        found = jnp.dot(table, one_hot(here), preferred_element_type=jnp.float32)
        high = here // DEPTH
        upper = choose(found[: HALF * parts], high, HALF)
        lower = choose(found[HALF * parts :], high // 2, HALF)
        odd = jnp.broadcast_to(high % 2, lower.shape)
        results.append(jnp.concatenate([upper, jnp.where(odd == 1, pltpu.roll(lower, HALF // 2, 0), lower)], axis=0))
    return jnp.concatenate(results, axis=1)


def copies_of(sources, targets, sems, first=0):
    return [
        pltpu.make_async_copy(source, target, sems.at[first + at])
        for at, (source, target) in enumerate(zip(sources, targets))
    ]


def message_rows(fields, twins):
    return 2 * fields if twins == 2 else ROWS


def order_kernel(twins, map_hbm, flux_hbm, out_hbm, map_ref, flux_ref, out_ref, table, sems):
    fields, cells = flux_ref.shape
    steps = cells // STEP
    spans = [pl.ds(at, cells // 4) for at in range(0, cells, cells // 4)]
    needed = copies_of([flux_hbm.at[:, span] for span in spans], [flux_ref.at[:, span] for span in spans], sems)
    needed += copies_of((map_hbm,), (map_ref,), sems, 4)
    for copy in needed:
        copy.start()
    for copy in needed:
        copy.wait()
    parts, rest = cells // DEPTH, fields - HALF
    for part in range(parts):
        columns = slice(part * DEPTH, (part + 1) * DEPTH)
        table[part * HALF : (part + 1) * HALF] = flux_ref[:HALF, columns]
        table[parts * HALF + part * rest : parts * HALF + (part + 1) * rest] = flux_ref[HALF:, columns]
    rows = message_rows(fields, twins)
    written = []
    for step in range(steps):
        found = lookup_dense(table[...], map_ref[:, step * STEP : (step + 1) * STEP], parts)
        pieces = [found[:, at : at + LANES] for at in range(0, STEP, LANES)]
        if twins == 2:
            pieces = [
                jnp.concatenate([pieces[at][:fields], pieces[at ^ 2][:fields]], axis=0) for at in range(len(pieces))
            ]
        for at, piece in enumerate(pieces):
            first = (step * len(pieces) + at) * rows
            out_ref[first : first + rows] = piece.astype(jnp.bfloat16)
        span = pl.ds(step * len(pieces) * rows, len(pieces) * rows)
        written.append(pltpu.make_async_copy(out_ref.at[span], out_hbm.at[span], sems.at[5 + step]))
        written[-1].start()
    for copy in written:
        copy.wait()


def select_kernel(after_ref, list_hbm, near_hbm, x_hbm, y_hbm, *refs):
    selected, (list_ref, near_ref, x_ref, y_ref, sems) = refs[:-5], refs[-5:]
    copies = copies_of((list_hbm, near_hbm, x_hbm, y_hbm), (list_ref, near_ref, x_ref, y_ref), sems)
    for copy in copies:
        copy.start()
    for copy in copies:
        copy.wait()
    me = lax.axis_index("local")
    cap = list_ref.shape[2]
    count = list_ref.shape[1] // len(selected)
    near_count = near_ref.shape[0]
    for twin, stencil_ref in reversed(list(enumerate(selected))):
        for at in range(count * cap):
            block = list_ref[0, me ^ (2 * twin) ^ (at // cap), at % cap]
            columns = pl.ds(pl.multiple_of(block * LANES, LANES), LANES)
            stencil_ref[at, :near_count] = near_ref[:, columns].astype(jnp.float32)
            stencil_ref[at, near_count : 2 * near_count] = x_ref[:, columns]
            stencil_ref[at, 2 * near_count : 3 * near_count] = y_ref[:, columns]
            rest = (ROWS - 3 * near_count, LANES)
            stencil_ref[at, 3 * near_count :] = jnp.broadcast_to(block, rest).astype(jnp.float32)


def fetch_kernel(after_ref, map_hbm, *refs):
    count = (len(refs) - 4) // 2
    sources, (moves_ref, high_ref), targets, (map_ref, sems) = refs[:count], refs[count : count + 2], refs[count + 2 : -2], refs[-2:]
    (needed,) = copies_of((map_hbm,), (map_ref,), sems, count)
    others = copies_of(sources, targets, sems)
    for copy in [needed] + others:
        copy.start()
    needed.wait()
    moves_ref[...] = one_hot(map_ref[...])
    high_ref[...] = map_ref[...] // DEPTH
    for copy in others:
        copy.wait()


def rebuild(near_count, table, stencil, own, shift):
    near = stencil[:near_count].astype(jnp.int32)
    index = jnp.concatenate([near[j : j + 1] for j in range(near_count)], axis=1)
    found = lookup(table, index)
    upper = lower = own
    slope_x = slope_y = jnp.zeros_like(own)
    for j in range(near_count):
        value = found[:, j * LANES : (j + 1) * LANES]
        change = value - own
        slope_x += stencil[near_count + j : near_count + j + 1] * change
        slope_y += stencil[2 * near_count + j : 2 * near_count + j + 1] * change
        upper, lower = jnp.maximum(upper, value), jnp.minimum(lower, value)
    steep = jnp.abs(slope_x) + jnp.abs(slope_y)
    factor = jnp.minimum(1.0, (upper - lower) / jnp.maximum(steep, 1.0))
    results = [own, factor * slope_x, factor * slope_y]
    if shift:
        spare = jnp.zeros((shift, LANES), jnp.float32)
        results = [jnp.concatenate([result[shift:], spare], axis=0) for result in results]
    return results


def own_cells(near_count, table, stencil_ref):
    slots = stencil_ref.shape[0]
    tile = (ROWS, DEPTH)
    column = lax.broadcasted_iota(jnp.int32, tile, 1) - lax.broadcasted_iota(jnp.int32, tile, 0)
    blocks = [stencil_ref[at, 3 * near_count : 3 * near_count + 1].astype(jnp.int32) for at in range(slots)]
    picks = [
        jnp.where(jnp.concatenate([block // PER_ROW * ROWS] * PER_ROW, axis=1) == column, 1.0, 0.0) for block in blocks
    ]
    found = jnp.dot(
        jnp.concatenate(picks, axis=0).astype(jnp.bfloat16), table, preferred_element_type=jnp.float32
    )
    owns = []
    for at, block in enumerate(blocks):
        rows = found[at * ROWS : (at + 1) * ROWS]
        odd = jnp.broadcast_to(block % PER_ROW, (ROWS, LANES))
        owns.append(jnp.where(odd == 1, rows[:, LANES:], rows[:, :LANES]))
    return owns


def outer_kernel(twins, near_count, fields, after_ref, cells_ref, *refs):
    selected, refs = refs[:twins], refs[twins:]
    out_refs, (tables, owns) = refs[:-2], refs[-2:]
    cap = owns.shape[1]
    rows = message_rows(fields, twins)
    for twin in range(twins):
        for block in range(tables.shape[1] // ROWS * PER_ROW):
            part, column = block // PER_ROW, block % PER_ROW * LANES
            first = block * rows + HALF * twin
            tables[twin, part * ROWS : (part + 1) * ROWS, column : column + LANES] = cells_ref[first : first + ROWS]
    for twin, stencil_ref in enumerate(selected):
        for at, own in enumerate(own_cells(near_count, tables[twin], stencil_ref)):
            if at < cap:
                owns[twin, at] = own
                continue
            shift = twin * (fields - HALF)
            results = rebuild(near_count, tables[twin], stencil_ref[at], own, shift)
            for kind, result in enumerate(results):
                out_refs[at // cap - 1][twin, at % cap * len(results) + kind] = result.astype(jnp.bfloat16)


def inner_kernel(near_count, fields, tables, owns, *refs):
    selected, out_ref = refs[:-1], refs[-1]
    for twin, stencil_ref in enumerate(selected):
        for at in range(owns.shape[1]):
            own = owns[twin, at]
            shift = twin * (fields - HALF)
            results = rebuild(near_count, tables[twin], stencil_ref[at], own, shift)
            for kind, result in enumerate(results):
                out_ref[twin, at * len(results) + kind] = result.astype(jnp.bfloat16)


def remap_kernel(packed, fields, cover_ref, count_ref, weight_ref, moves_ref, high_ref, *refs):
    received, (out_ref, source_ref) = refs[:-2], refs[-2:]
    me = lax.axis_index("local")
    ocean_blocks, slots, kinds = weight_ref.shape[:3]
    cap = source_ref.shape[1] // kinds
    for apart, piece_ref in enumerate(received):
        for twin in range(piece_ref.shape[0]):
            source_ref[me ^ apart ^ (2 * twin)] = piece_ref[twin]
    results = []
    for block in range(ocean_blocks):
        values, weights = [], []
        for slot in range(slots):
            at = cover_ref[block, slot]
            live = slot < count_ref[block]
            for kind in range(kinds):
                value = source_ref[at // cap, at % cap * kinds + kind]
                values.append(jnp.where(live, value, jnp.zeros_like(value)))
                weights.append(weight_ref[block, slot, kind])
        product = lax.dot_general(
            jnp.concatenate(values, axis=1),
            jnp.concatenate(weights, axis=1),
            (((1,), (1,)), ((), ())),
            preferred_element_type=jnp.float32,
        )
        results.append(product)
    remapped = jnp.concatenate(results, axis=1)
    cells = remapped.shape[1]
    coarse = remapped.astype(jnp.bfloat16)
    fine = (remapped - coarse.astype(jnp.float32)).astype(jnp.bfloat16)
    table = [part[:, at : at + DEPTH] for at in range(0, cells, DEPTH) for part in (coarse, fine)]
    moved = jnp.dot(jnp.concatenate(table, axis=0), moves_ref[...], preferred_element_type=jnp.float32)
    moved = choose(moved, high_ref[...], 2 * ROWS)
    moved = moved[:ROWS] + moved[ROWS:]
    if not packed:
        out_ref[...] = moved[:fields]
        return
    half = fields // 2
    rows = out_ref.shape[1]
    listed = listing(out_ref.shape[0])
    side = lax.broadcasted_iota(jnp.int32, (rows, LANES), 1) < LANES // 2
    for pair in range(cells // LANES):
        columns = moved[:, pair * LANES : (pair + 1) * LANES]
        first, second = columns[:rows], columns[half : half + rows]
        out_ref[listed.index(2 * pair)] = jnp.where(side, first, pltpu.roll(second, LANES // 2, 1))
        out_ref[listed.index(2 * pair + 1)] = jnp.where(side, pltpu.roll(first, LANES // 2, 1), second)


def land_kernel(landed_ref, out_ref):
    count = landed_ref.shape[0]
    listed = listing(count)
    half = out_ref.shape[0] // 2
    side = lax.broadcasted_iota(jnp.int32, (half, LANES), 1) < LANES // 2
    for pair in range(count // 2):
        even, odd = landed_ref[listed.index(2 * pair), :half], landed_ref[listed.index(2 * pair + 1), :half]
        columns = pl.ds(pair * LANES, LANES)
        out_ref[:half, columns] = jnp.where(side, even, pltpu.roll(odd, LANES // 2, 1))
        out_ref[half:, columns] = jnp.where(side, pltpu.roll(even, LANES // 2, 1), odd)


def send(array, axis, apart):
    return lax.ppermute(array, axis, [(at, at ^ apart) for at in range(lax.axis_size(axis))])


def listing(count):
    return sorted(range(count), key=lambda at: (abs(2 * at - count + 1), -at))


def swap(pieces, axis):
    groups = [listing(lax.axis_size(axis))]
    pieces = pieces.transpose(1, 0, 2)
    swapped = lax.all_to_all(pieces, axis, split_axis=1, concat_axis=1, axis_index_groups=groups, tiled=True)
    return swapped.transpose(1, 0, 2)


SPACES = {"s": pltpu.SMEM, "v": pltpu.VMEM, "h": pltpu.HBM, "a": pl.ANY}


def call(kernel, outs, memories, scratch=(), out_memory="v", flops=0, moved=0):
    if isinstance(outs, list):
        out_specs = [pl.BlockSpec(memory_space=SPACES[kind]) for kind in (out_memory * len(outs))[: len(outs)]]
    else:
        out_specs = pl.BlockSpec(memory_space=SPACES[out_memory])
    return pl.pallas_call(
        kernel,
        out_shape=outs,
        in_specs=[pl.BlockSpec(memory_space=SPACES[kind]) for kind in memories],
        out_specs=out_specs,
        scratch_shapes=list(scratch),
        cost_estimate=pl.CostEstimate(flops=flops, bytes_accessed=moved, transcendentals=0),
        compiler_params=pltpu.CompilerParams(vmem_limit_bytes=VMEM_LIMIT),
    )


def shards(
    atm_flux,
    cell_map,
    neighbours,
    coef_x,
    coef_y,
    send_list,
    cover,
    cover_count,
    weights,
    ocean_map,
):
    fields, cells = atm_flux.shape
    region_count = lax.axis_size("region")
    local_count = lax.axis_size("local")
    everyone = ("region", "local")
    devices = region_count * local_count
    piece = cells // devices
    blocks = cells // LANES
    table = (cells // DEPTH * ROWS, DEPTH)
    shaped = jax.ShapeDtypeStruct
    twins = 2 if local_count == 4 and piece == LANES else 1
    cap = send_list.shape[2]
    aparts = local_count // twins
    near_count = neighbours.shape[0]
    kinds = weights.shape[2]
    ocean_cells = ocean_map.shape[1]

    def stay(*arrays):
        return [pltpu.with_memory_space_constraint(array, pltpu.HBM) for array in arrays]

    def scratch(array):
        return pltpu.VMEM(array.shape, array.dtype)

    rows = message_rows(fields, twins)
    messages = (blocks * rows, LANES)
    ordered = call(
        functools.partial(order_kernel, twins),
        shaped(messages, jnp.bfloat16),
        "hh",
        [
            scratch(cell_map),
            scratch(atm_flux),
            pltpu.VMEM(messages, jnp.bfloat16),
            pltpu.VMEM((cells // DEPTH * fields, DEPTH), jnp.bfloat16),
            pltpu.SemaphoreType.DMA((cells // STEP + 5,)),
        ],
        out_memory="h",
    )(*stay(cell_map, atm_flux))

    stencil = shaped((aparts * cap, ROWS, LANES), jnp.float32)
    selected = call(
        select_kernel,
        [stencil] * twins,
        "ahhhh",
        [
            pltpu.SMEM(send_list.shape, send_list.dtype),
            scratch(neighbours),
            scratch(coef_x),
            scratch(coef_y),
            pltpu.SemaphoreType.DMA((4,)),
        ],
        moved=3_000_000,
    )(ordered, *stay(send_list, neighbours, coef_x, coef_y))
    selected = [selected[0]] + [send(array, "local", 2) for array in selected[1:]]

    later = [cover, cover_count, weights]
    moves, high, cover, cover_count, weights = call(
        fetch_kernel,
        [
            shaped((DEPTH, ocean_cells), jnp.bfloat16),
            shaped(ocean_map.shape, ocean_map.dtype),
            pltpu.SMEM(cover.shape, cover.dtype),
            pltpu.SMEM(cover_count.shape, cover_count.dtype),
            shaped(weights.shape, weights.dtype),
        ],
        "ah" + "h" * len(later),
        [scratch(ocean_map), pltpu.SemaphoreType.DMA((len(later) + 1,))],
        out_memory="vvssv",
        moved=3_000_000,
    )(ordered, *stay(ocean_map, *later))

    if piece == LANES:
        coupled = lax.all_to_all(ordered, everyone, split_axis=0, concat_axis=0, tiled=True)
    else:
        outgoing = ordered.reshape(blocks, rows, LANES)[:, :fields].transpose(1, 0, 2).reshape(fields, devices, piece)
        coupled = lax.all_to_all(outgoing, everyone, split_axis=1, concat_axis=1, tiled=True)
        coupled = coupled.reshape(fields, blocks, LANES).transpose(1, 0, 2)
        coupled = jnp.pad(coupled, ((0, 0), (0, rows - fields), (0, 0))).reshape(messages)

    sent = shaped((twins, cap * kinds, ROWS, LANES), jnp.bfloat16)
    tables = shaped((twins,) + table, jnp.bfloat16)
    owns = shaped((twins, cap, ROWS, LANES), jnp.float32)
    work = 2 * twins * cap * table[0] * DEPTH * near_count * LANES
    *outer, tables, owns = call(
        functools.partial(outer_kernel, twins, near_count, fields),
        [sent] * (aparts - 1) + [tables, owns],
        "av" + "v" * twins,
        flops=work * (aparts - 1),
    )(moves, coupled, *selected)
    source = [send(array, "local", 1 + at) for at, array in enumerate(outer)]
    inner = call(
        functools.partial(inner_kernel, near_count, fields),
        sent,
        "vv" + "v" * twins,
        flops=work,
        moved=4_000_000,
    )(tables, owns, *selected)
    source = [inner] + source

    share = ocean_cells // region_count
    packed = share * 2 == LANES
    out_shape = (region_count, ROWS // 2, LANES) if packed else (fields, ocean_cells)
    leaving = call(
        functools.partial(remap_kernel, packed, fields),
        shaped(out_shape, jnp.float32),
        "ssvvv" + "v" * aparts,
        [pltpu.VMEM((local_count, cap * kinds, ROWS, LANES), jnp.bfloat16)],
    )(cover, cover_count, weights, moves, high, *source)
    if packed:
        landed = swap(leaving, "region")
        return call(land_kernel, shaped((fields, ocean_cells), jnp.float32), "v")(landed)
    leaving = leaving.reshape(fields, region_count, share)
    landed = lax.all_to_all(leaving, "region", split_axis=1, concat_axis=1, tiled=True)
    return landed.reshape(fields, ocean_cells)


def solution(mesh):
    return jax.shard_map(
        shards,
        mesh=mesh,
        in_specs=(
            P(None, ("region", "local")),
            P(("region", "local"), None),
            P(None, ("region", "local")),
            P(None, ("region", "local")),
            P(None, ("region", "local")),
            P(("region", "local"), None, None),
            P(("region", "local"), None),
            P(("region", "local")),
            P(("region", "local"), None, None, None, None),
            P(("region", "local"), None),
        ),
        out_specs=P(None, ("region", "local")),
        check_vma=False,
    )
```

```python
import functools

import jax
import jax.numpy as jnp
from jax import lax
from jax.experimental import pallas as pl
from jax.experimental.pallas import tpu as pltpu
from jax.sharding import PartitionSpec as P

ROWS = 16
HALF = 8
LANES = 128
DEPTH = 256
PER_ROW = DEPTH // LANES
STEP = 512
WIDTH = 256
VMEM_LIMIT = 40 * 1024 * 1024


def one_hot(index):
    row = lax.broadcasted_iota(jnp.int32, (DEPTH, index.shape[1]), 0).astype(jnp.bfloat16)
    low = (index & (DEPTH - 1)).astype(jnp.bfloat16)
    return jnp.where(row == low, jnp.bfloat16(1), jnp.bfloat16(0))


def choose(found, high, height):
    high = jnp.broadcast_to(high, (height, found.shape[1]))
    result = found[:height]
    for part in range(1, found.shape[0] // height):
        result = jnp.where(high == part, found[part * height : (part + 1) * height], result)
    return result


def lookup(table, index, parts):
    results = []
    for at in range(0, index.shape[1], WIDTH):
        here = index[:, at : at + WIDTH]
        found = jnp.dot(table, one_hot(here), preferred_element_type=jnp.float32)
        high = here // DEPTH
        upper = choose(found[: HALF * parts], high, HALF)
        lower = choose(found[HALF * parts :], high // 2, HALF)
        odd = jnp.broadcast_to(high % 2, lower.shape)
        results.append(jnp.concatenate([upper, jnp.where(odd == 1, pltpu.roll(lower, HALF // 2, 0), lower)], axis=0))
    return jnp.concatenate(results, axis=1)


def copies_of(sources, targets, sems, first=0):
    return [
        pltpu.make_async_copy(source, target, sems.at[first + at])
        for at, (source, target) in enumerate(zip(sources, targets))
    ]


def message_rows(fields, twins):
    return 2 * fields if twins == 2 else ROWS


def joined(own, twin):
    first = lax.broadcasted_iota(jnp.int32, (HALF, LANES), 0) < HALF // 2
    middle = jnp.where(first, own[HALF:], pltpu.roll(twin[HALF:], HALF // 2, 0))
    return jnp.concatenate([own[:HALF], middle, twin[:HALF]], axis=0)


def order_kernel(twins, map_hbm, flux_hbm, out_hbm, map_ref, flux_ref, out_ref, table, sems):
    fields, cells = flux_ref.shape
    steps = cells // STEP
    spans = [pl.ds(at, cells // 4) for at in range(0, cells, cells // 4)]
    needed = copies_of([flux_hbm.at[:, span] for span in spans], [flux_ref.at[:, span] for span in spans], sems)
    needed += copies_of((map_hbm,), (map_ref,), sems, 4)
    for copy in needed:
        copy.start()
    for copy in needed:
        copy.wait()
    parts, rest = cells // DEPTH, fields - HALF
    for part in range(parts):
        columns = slice(part * DEPTH, (part + 1) * DEPTH)
        table[part * HALF : (part + 1) * HALF] = flux_ref[:HALF, columns]
        table[parts * HALF + part * rest : parts * HALF + (part + 1) * rest] = flux_ref[HALF:, columns]
    rows = message_rows(fields, twins)
    written = []
    for step in range(steps):
        found = lookup(table[...], map_ref[:, step * STEP : (step + 1) * STEP], parts)
        pieces = [found[:, at : at + LANES] for at in range(0, STEP, LANES)]
        if twins == 2:
            pieces = [joined(pieces[at], pieces[at ^ 2]) for at in range(len(pieces))]
        for at, piece in enumerate(pieces):
            first = (step * len(pieces) + at) * rows
            out_ref[first : first + rows] = piece.astype(jnp.bfloat16)
        span = pl.ds(step * len(pieces) * rows, len(pieces) * rows)
        written.append(pltpu.make_async_copy(out_ref.at[span], out_hbm.at[span], sems.at[5 + step]))
        written[-1].start()
    for copy in written:
        copy.wait()


def select_kernel(after_ref, list_hbm, near_hbm, x_hbm, y_hbm, *refs):
    selected, (list_ref, near_ref, x_ref, y_ref, sems) = refs[:-5], refs[-5:]
    copies = copies_of((list_hbm, near_hbm, x_hbm, y_hbm), (list_ref, near_ref, x_ref, y_ref), sems)
    for copy in copies:
        copy.start()
    for copy in copies:
        copy.wait()
    me = lax.axis_index("local")
    cap = list_ref.shape[2]
    count = list_ref.shape[1] // len(selected)
    near_count = near_ref.shape[0]
    for twin, stencil_ref in reversed(list(enumerate(selected))):
        for at in range(count * cap):
            block = list_ref[0, me ^ (2 * twin) ^ (at // cap), at % cap]
            columns = pl.ds(pl.multiple_of(block * LANES, LANES), LANES)
            stencil_ref[at, :near_count] = near_ref[:, columns].astype(jnp.float32)
            stencil_ref[at, near_count : 2 * near_count] = x_ref[:, columns]
            stencil_ref[at, 2 * near_count : 3 * near_count] = y_ref[:, columns]
            rest = (ROWS - 3 * near_count, LANES)
            stencil_ref[at, 3 * near_count :] = jnp.broadcast_to(block, rest).astype(jnp.float32)


def fetch_kernel(after_ref, map_hbm, *refs):
    count = (len(refs) - 4) // 2
    sources, (moves_ref, high_ref), targets, (map_ref, sems) = refs[:count], refs[count : count + 2], refs[count + 2 : -2], refs[-2:]
    (needed,) = copies_of((map_hbm,), (map_ref,), sems, count)
    others = copies_of(sources, targets, sems)
    for copy in [needed] + others:
        copy.start()
    needed.wait()
    moves_ref[...] = one_hot(map_ref[...])
    high_ref[...] = map_ref[...] // DEPTH
    for copy in others:
        copy.wait()


def rebuild(near_count, table, stencil, own):
    near = stencil[:near_count].astype(jnp.int32)
    index = jnp.concatenate([near[j : j + 1] for j in range(near_count)], axis=1)
    parts = table.shape[0] // ROWS
    found = lookup(table[: parts * (HALF + HALF // 2)], index, parts)
    upper = lower = own
    slope_x = slope_y = jnp.zeros_like(own)
    for j in range(near_count):
        value = found[:, j * LANES : (j + 1) * LANES]
        change = value - own
        slope_x += stencil[near_count + j : near_count + j + 1] * change
        slope_y += stencil[2 * near_count + j : 2 * near_count + j + 1] * change
        upper, lower = jnp.maximum(upper, value), jnp.minimum(lower, value)
    steep = jnp.abs(slope_x) + jnp.abs(slope_y)
    factor = jnp.minimum(1.0, (upper - lower) / jnp.maximum(steep, 1.0))
    return [own, factor * slope_x, factor * slope_y]


def own_cells(near_count, table, stencil_ref):
    slots = stencil_ref.shape[0]
    tile = (ROWS, table.shape[0])
    row = lax.broadcasted_iota(jnp.int32, tile, 0)
    upper = row < HALF
    stride = jnp.where(upper, HALF, HALF // 2)
    column = lax.broadcasted_iota(jnp.int32, tile, 1) - jnp.where(upper, row, HALF * (table.shape[0] // ROWS - 1) + row)
    blocks = [stencil_ref[at, 3 * near_count : 3 * near_count + 1].astype(jnp.int32) for at in range(slots)]
    picks = []
    for block in blocks:
        part = jnp.concatenate([block // PER_ROW] * (table.shape[0] // LANES), axis=1)
        picks.append(jnp.where(part * stride == column, 1.0, 0.0))
    found = jnp.dot(
        jnp.concatenate(picks, axis=0).astype(jnp.bfloat16), table, preferred_element_type=jnp.float32
    )
    owns = []
    for at, block in enumerate(blocks):
        rows = found[at * ROWS : (at + 1) * ROWS]
        odd = jnp.broadcast_to(block % PER_ROW, (ROWS, LANES))
        owns.append(jnp.where(odd == 1, rows[:, LANES:], rows[:, :LANES]))
    return owns


def outer_kernel(twins, near_count, fields, after_ref, cells_ref, *refs):
    selected, refs = refs[:twins], refs[twins:]
    out_refs, (tables, owns) = refs[:-2], refs[-2:]
    cap = owns.shape[1]
    rows = message_rows(fields, twins)
    parts, rest = tables.shape[1] // ROWS, fields - HALF
    for twin in range(twins):
        tables[twin, parts * fields :] = jnp.zeros((parts * (ROWS - fields), DEPTH), jnp.bfloat16)
        for block in range(parts * PER_ROW):
            part, column = block // PER_ROW, slice(block % PER_ROW * LANES, (block % PER_ROW + 1) * LANES)
            upper, lower = block * rows + twin * 2 * HALF, block * rows + HALF + twin * rest
            tables[twin, part * HALF : (part + 1) * HALF, column] = cells_ref[upper : upper + HALF]
            at = parts * HALF + part * rest
            tables[twin, at : at + rest, column] = cells_ref[lower : lower + rest]
    for twin, stencil_ref in enumerate(selected):
        for at, own in enumerate(own_cells(near_count, tables[twin], stencil_ref)):
            if at < cap:
                owns[twin, at] = own
                continue
            results = rebuild(near_count, tables[twin], stencil_ref[at], own)
            for kind, result in enumerate(results):
                out_refs[at // cap - 1][twin, at % cap * len(results) + kind] = result.astype(jnp.bfloat16)


def inner_kernel(near_count, fields, tables, owns, *refs):
    selected, out_ref = refs[:-1], refs[-1]
    for twin, stencil_ref in enumerate(selected):
        for at in range(owns.shape[1]):
            own = owns[twin, at]
            results = rebuild(near_count, tables[twin], stencil_ref[at], own)
            for kind, result in enumerate(results):
                out_ref[twin, at * len(results) + kind] = result.astype(jnp.bfloat16)


def remap_kernel(packed, fields, cover_ref, count_ref, weight_ref, moves_ref, high_ref, *refs):
    received, (out_ref, source_ref) = refs[:-2], refs[-2:]
    me = lax.axis_index("local")
    ocean_blocks, slots, kinds = weight_ref.shape[:3]
    cap = source_ref.shape[1] // kinds
    for apart, piece_ref in enumerate(received):
        for twin in range(piece_ref.shape[0]):
            source_ref[me ^ apart ^ (2 * twin)] = piece_ref[twin]
    results = []
    for first in range(0, ocean_blocks, 2):
        values, weights = [], []
        for block in (first, first + 1):
            tiles = []
            for slot in range(slots):
                at = cover_ref[block, slot]
                live = slot < count_ref[block]
                for kind in range(kinds):
                    value = source_ref[at // cap, at % cap * kinds + kind]
                    tiles.append(jnp.where(live, value, jnp.zeros_like(value)))
            values.append(jnp.concatenate(tiles, axis=1))
            tiles = [weight_ref[block, slot, kind] for slot in range(slots) for kind in range(kinds)]
            weights.append(jnp.concatenate(tiles, axis=1))
        product = lax.dot_general(
            jnp.concatenate(values, axis=0),
            jnp.concatenate(weights, axis=0),
            (((1,), (1,)), ((), ())),
            preferred_element_type=jnp.float32,
        )
        half = product.shape[1] // 2
        results += [product[:ROWS, :half], product[ROWS:, half:]]
    remapped = jnp.concatenate(results, axis=1)
    cells = remapped.shape[1]
    coarse = remapped.astype(jnp.bfloat16)
    fine = (remapped - coarse.astype(jnp.float32)).astype(jnp.bfloat16)
    table = [part[:, at : at + DEPTH] for at in range(0, cells, DEPTH) for part in (coarse, fine)]
    moved = jnp.dot(jnp.concatenate(table, axis=0), moves_ref[...], preferred_element_type=jnp.float32)
    moved = choose(moved, high_ref[...], 2 * ROWS)
    moved = moved[:ROWS] + moved[ROWS:]
    if not packed:
        out_ref[...] = moved[:fields]
        return
    half = fields // 2
    rows = out_ref.shape[1]
    listed = listing(out_ref.shape[0])
    side = lax.broadcasted_iota(jnp.int32, (rows, LANES), 1) < LANES // 2
    for pair in range(cells // LANES):
        columns = moved[:, pair * LANES : (pair + 1) * LANES]
        first, second = columns[:rows], columns[half : half + rows]
        out_ref[listed.index(2 * pair)] = jnp.where(side, first, pltpu.roll(second, LANES // 2, 1))
        out_ref[listed.index(2 * pair + 1)] = jnp.where(side, pltpu.roll(first, LANES // 2, 1), second)


def land_kernel(landed_ref, out_ref):
    count = landed_ref.shape[0]
    listed = listing(count)
    half = out_ref.shape[0] // 2
    side = lax.broadcasted_iota(jnp.int32, (half, LANES), 1) < LANES // 2
    for pair in range(count // 2):
        even, odd = landed_ref[listed.index(2 * pair), :half], landed_ref[listed.index(2 * pair + 1), :half]
        columns = pl.ds(pair * LANES, LANES)
        out_ref[:half, columns] = jnp.where(side, even, pltpu.roll(odd, LANES // 2, 1))
        out_ref[half:, columns] = jnp.where(side, pltpu.roll(even, LANES // 2, 1), odd)


def send(array, axis, apart):
    return lax.ppermute(array, axis, [(at, at ^ apart) for at in range(lax.axis_size(axis))])


def listing(count):
    return sorted(range(count), key=lambda at: (abs(2 * at - count + 1), -at))


def swap(pieces, axis):
    groups = [listing(lax.axis_size(axis))]
    pieces = pieces.transpose(1, 0, 2)
    swapped = lax.all_to_all(pieces, axis, split_axis=1, concat_axis=1, axis_index_groups=groups, tiled=True)
    return swapped.transpose(1, 0, 2)


SPACES = {"s": pltpu.SMEM, "v": pltpu.VMEM, "h": pltpu.HBM, "a": pl.ANY}


def call(kernel, outs, memories, scratch=(), out_memory="v", flops=0, moved=0):
    if isinstance(outs, list):
        out_specs = [pl.BlockSpec(memory_space=SPACES[kind]) for kind in (out_memory * len(outs))[: len(outs)]]
    else:
        out_specs = pl.BlockSpec(memory_space=SPACES[out_memory])
    return pl.pallas_call(
        kernel,
        out_shape=outs,
        in_specs=[pl.BlockSpec(memory_space=SPACES[kind]) for kind in memories],
        out_specs=out_specs,
        scratch_shapes=list(scratch),
        cost_estimate=pl.CostEstimate(flops=flops, bytes_accessed=moved, transcendentals=0),
        compiler_params=pltpu.CompilerParams(vmem_limit_bytes=VMEM_LIMIT),
    )


def shards(
    atm_flux,
    cell_map,
    neighbours,
    coef_x,
    coef_y,
    send_list,
    cover,
    cover_count,
    weights,
    ocean_map,
):
    fields, cells = atm_flux.shape
    region_count = lax.axis_size("region")
    local_count = lax.axis_size("local")
    everyone = ("region", "local")
    devices = region_count * local_count
    piece = cells // devices
    blocks = cells // LANES
    table = (cells // DEPTH * ROWS, DEPTH)
    shaped = jax.ShapeDtypeStruct
    twins = 2 if local_count == 4 and piece == LANES else 1
    cap = send_list.shape[2]
    aparts = local_count // twins
    near_count = neighbours.shape[0]
    kinds = weights.shape[2]
    ocean_cells = ocean_map.shape[1]

    def stay(*arrays):
        return [pltpu.with_memory_space_constraint(array, pltpu.HBM) for array in arrays]

    def scratch(array):
        return pltpu.VMEM(array.shape, array.dtype)

    rows = message_rows(fields, twins)
    messages = (blocks * rows, LANES)
    ordered = call(
        functools.partial(order_kernel, twins),
        shaped(messages, jnp.bfloat16),
        "hh",
        [
            scratch(cell_map),
            scratch(atm_flux),
            pltpu.VMEM(messages, jnp.bfloat16),
            pltpu.VMEM((cells // DEPTH * fields, DEPTH), jnp.bfloat16),
            pltpu.SemaphoreType.DMA((cells // STEP + 5,)),
        ],
        out_memory="h",
    )(*stay(cell_map, atm_flux))

    stencil = shaped((aparts * cap, ROWS, LANES), jnp.float32)
    selected = call(
        select_kernel,
        [stencil] * twins,
        "ahhhh",
        [
            pltpu.SMEM(send_list.shape, send_list.dtype),
            scratch(neighbours),
            scratch(coef_x),
            scratch(coef_y),
            pltpu.SemaphoreType.DMA((4,)),
        ],
        moved=3_000_000,
    )(ordered, *stay(send_list, neighbours, coef_x, coef_y))
    selected = [selected[0]] + [send(array, "local", 2) for array in selected[1:]]

    later = [cover, cover_count, weights]
    moves, high, cover, cover_count, weights = call(
        fetch_kernel,
        [
            shaped((DEPTH, ocean_cells), jnp.bfloat16),
            shaped(ocean_map.shape, ocean_map.dtype),
            pltpu.SMEM(cover.shape, cover.dtype),
            pltpu.SMEM(cover_count.shape, cover_count.dtype),
            shaped(weights.shape, weights.dtype),
        ],
        "ah" + "h" * len(later),
        [scratch(ocean_map), pltpu.SemaphoreType.DMA((len(later) + 1,))],
        out_memory="vvssv",
        moved=3_000_000,
    )(ordered, *stay(ocean_map, *later))

    if piece == LANES:
        coupled = lax.all_to_all(ordered, everyone, split_axis=0, concat_axis=0, tiled=True)
    else:
        outgoing = ordered.reshape(blocks, rows, LANES)[:, :fields].transpose(1, 0, 2).reshape(fields, devices, piece)
        coupled = lax.all_to_all(outgoing, everyone, split_axis=1, concat_axis=1, tiled=True)
        coupled = coupled.reshape(fields, blocks, LANES).transpose(1, 0, 2)
        coupled = jnp.pad(coupled, ((0, 0), (0, rows - fields), (0, 0))).reshape(messages)

    sent = shaped((twins, cap * kinds, ROWS, LANES), jnp.bfloat16)
    tables = shaped((twins,) + table, jnp.bfloat16)
    owns = shaped((twins, cap, ROWS, LANES), jnp.float32)
    work = 2 * twins * cap * table[0] * DEPTH * near_count * LANES
    *outer, tables, owns = call(
        functools.partial(outer_kernel, twins, near_count, fields),
        [sent] * (aparts - 1) + [tables, owns],
        "av" + "v" * twins,
        flops=work * (aparts - 1),
    )(moves, coupled, *selected)
    source = [send(array, "local", 1 + at) for at, array in enumerate(outer)]
    inner = call(
        functools.partial(inner_kernel, near_count, fields),
        sent,
        "vv" + "v" * twins,
        flops=work,
        moved=4_000_000,
    )(tables, owns, *selected)
    source = [inner] + source

    share = ocean_cells // region_count
    packed = share * 2 == LANES
    out_shape = (region_count, ROWS // 2, LANES) if packed else (fields, ocean_cells)
    leaving = call(
        functools.partial(remap_kernel, packed, fields),
        shaped(out_shape, jnp.float32),
        "ssvvv" + "v" * aparts,
        [pltpu.VMEM((local_count, cap * kinds, ROWS, LANES), jnp.bfloat16)],
    )(cover, cover_count, weights, moves, high, *source)
    if packed:
        landed = swap(leaving, "region")
        return call(land_kernel, shaped((fields, ocean_cells), jnp.float32), "v")(landed)
    leaving = leaving.reshape(fields, region_count, share)
    landed = lax.all_to_all(leaving, "region", split_axis=1, concat_axis=1, tiled=True)
    return landed.reshape(fields, ocean_cells)


def solution(mesh):
    return jax.shard_map(
        shards,
        mesh=mesh,
        in_specs=(
            P(None, ("region", "local")),
            P(("region", "local"), None),
            P(None, ("region", "local")),
            P(None, ("region", "local")),
            P(None, ("region", "local")),
            P(("region", "local"), None, None),
            P(("region", "local"), None),
            P(("region", "local")),
            P(("region", "local"), None, None, None, None),
            P(("region", "local"), None),
        ),
        out_specs=P(None, ("region", "local")),
        check_vma=False,
    )
```

```python
import functools

import jax
import jax.numpy as jnp
from jax import lax
from jax.experimental import pallas as pl
from jax.experimental.pallas import tpu as pltpu
from jax.sharding import PartitionSpec as P

ROWS = 16
HALF = 8
LANES = 128
DEPTH = 256
PER_ROW = DEPTH // LANES
STEP = 512
WIDTH = 256
VMEM_LIMIT = 40 * 1024 * 1024


def row_numbers(width):
    return lax.broadcasted_iota(jnp.int32, (DEPTH, width), 0).astype(jnp.bfloat16)


def one_hot(row, index):
    low = (index & (DEPTH - 1)).astype(jnp.bfloat16)
    return jnp.where(row == low, jnp.bfloat16(1), jnp.bfloat16(0))


def choose(found, high, height):
    high = jnp.broadcast_to(high, (height, found.shape[1]))
    result = found[:height]
    for part in range(1, found.shape[0] // height):
        result = jnp.where(high == part, found[part * height : (part + 1) * height], result)
    return result


def lookup(table, row_ref, index):
    results = []
    for at in range(0, index.shape[1], WIDTH):
        here = index[:, at : at + WIDTH]
        found = jnp.dot(table, one_hot(row_ref[...], here), preferred_element_type=jnp.float32)
        results.append(choose(found, here // DEPTH, ROWS))
    return jnp.concatenate(results, axis=1)


def lookup_dense(table, row_ref, index, parts):
    results = []
    for at in range(0, index.shape[1], WIDTH):
        here = index[:, at : at + WIDTH]
        found = jnp.dot(table, one_hot(row_ref[...], here), preferred_element_type=jnp.float32)
        high = here // DEPTH
        upper = choose(found[: HALF * parts], high, HALF)
        lower = choose(found[HALF * parts :], high // 2, HALF)
        odd = jnp.broadcast_to(high % 2, lower.shape)
        results.append(jnp.concatenate([upper, jnp.where(odd == 1, pltpu.roll(lower, HALF // 2, 0), lower)], axis=0))
    return jnp.concatenate(results, axis=1)


def copies_of(sources, targets, sems, first=0):
    return [
        pltpu.make_async_copy(source, target, sems.at[first + at])
        for at, (source, target) in enumerate(zip(sources, targets))
    ]


def message_rows(fields, twins):
    return 2 * fields if twins == 2 else ROWS


def order_kernel(twins, map_hbm, flux_hbm, out_hbm, map_ref, flux_ref, out_ref, table, row_ref, sems):
    fields, cells = flux_ref.shape
    steps = cells // STEP
    spans = [pl.ds(at, cells // 4) for at in range(0, cells, cells // 4)]
    needed = copies_of([flux_hbm.at[:, span] for span in spans], [flux_ref.at[:, span] for span in spans], sems)
    needed += copies_of((map_hbm,), (map_ref,), sems, 4)
    for copy in needed:
        copy.start()
    row_ref[...] = row_numbers(WIDTH)
    for copy in needed:
        copy.wait()
    parts, rest = cells // DEPTH, fields - HALF
    for part in range(parts):
        columns = slice(part * DEPTH, (part + 1) * DEPTH)
        table[part * HALF : (part + 1) * HALF] = flux_ref[:HALF, columns]
        table[parts * HALF + part * rest : parts * HALF + (part + 1) * rest] = flux_ref[HALF:, columns]
    rows = message_rows(fields, twins)
    written = []
    for step in range(steps):
        found = lookup_dense(table[...], row_ref, map_ref[:, step * STEP : (step + 1) * STEP], parts)
        pieces = [found[:, at : at + LANES] for at in range(0, STEP, LANES)]
        if twins == 2:
            pieces = [
                jnp.concatenate([pieces[at][:fields], pieces[at ^ 2][:fields]], axis=0) for at in range(len(pieces))
            ]
        for at, piece in enumerate(pieces):
            first = (step * len(pieces) + at) * rows
            out_ref[first : first + rows] = piece.astype(jnp.bfloat16)
        span = pl.ds(step * len(pieces) * rows, len(pieces) * rows)
        written.append(pltpu.make_async_copy(out_ref.at[span], out_hbm.at[span], sems.at[5 + step]))
        written[-1].start()
    for copy in written:
        copy.wait()


def select_kernel(after_ref, list_hbm, near_hbm, x_hbm, y_hbm, *refs):
    selected, (list_ref, near_ref, x_ref, y_ref, sems) = refs[:-5], refs[-5:]
    copies = copies_of((list_hbm, near_hbm, x_hbm, y_hbm), (list_ref, near_ref, x_ref, y_ref), sems)
    for copy in copies:
        copy.start()
    for copy in copies:
        copy.wait()
    me = lax.axis_index("local")
    cap = list_ref.shape[2]
    count = list_ref.shape[1] // len(selected)
    near_count = near_ref.shape[0]
    for twin, stencil_ref in reversed(list(enumerate(selected))):
        for at in range(count * cap):
            block = list_ref[0, me ^ (2 * twin) ^ (at // cap), at % cap]
            columns = pl.ds(pl.multiple_of(block * LANES, LANES), LANES)
            stencil_ref[at, :near_count] = near_ref[:, columns].astype(jnp.float32)
            stencil_ref[at, near_count : 2 * near_count] = x_ref[:, columns]
            stencil_ref[at, 2 * near_count : 3 * near_count] = y_ref[:, columns]
            rest = (ROWS - 3 * near_count, LANES)
            stencil_ref[at, 3 * near_count :] = jnp.broadcast_to(block, rest).astype(jnp.float32)


def fetch_kernel(after_ref, map_hbm, *refs):
    count = (len(refs) - 5) // 2
    sources, (row_ref, moves_ref, high_ref) = refs[:count], refs[count : count + 3]
    targets, (map_ref, sems) = refs[count + 3 : -2], refs[-2:]
    (needed,) = copies_of((map_hbm,), (map_ref,), sems, count)
    others = copies_of(sources, targets, sems)
    for copy in [needed] + others:
        copy.start()
    needed.wait()
    row_ref[...] = row_numbers(WIDTH)
    moves_ref[...] = one_hot(row_numbers(map_ref.shape[1]), map_ref[...])
    high_ref[...] = map_ref[...] // DEPTH
    for copy in others:
        copy.wait()


def rebuild(near_count, table, row_ref, stencil, own, shift):
    near = stencil[:near_count].astype(jnp.int32)
    index = jnp.concatenate([near[j : j + 1] for j in range(near_count)], axis=1)
    found = lookup(table, row_ref, index)
    upper = lower = own
    slope_x = slope_y = jnp.zeros_like(own)
    for j in range(near_count):
        value = found[:, j * LANES : (j + 1) * LANES]
        change = value - own
        slope_x += stencil[near_count + j : near_count + j + 1] * change
        slope_y += stencil[2 * near_count + j : 2 * near_count + j + 1] * change
        upper, lower = jnp.maximum(upper, value), jnp.minimum(lower, value)
    steep = jnp.abs(slope_x) + jnp.abs(slope_y)
    factor = jnp.minimum(1.0, (upper - lower) / jnp.maximum(steep, 1.0))
    results = [own, factor * slope_x, factor * slope_y]
    if shift:
        spare = jnp.zeros((shift, LANES), jnp.float32)
        results = [jnp.concatenate([result[shift:], spare], axis=0) for result in results]
    return results


def own_cells(near_count, table, stencil_ref):
    slots = stencil_ref.shape[0]
    tile = (ROWS, DEPTH)
    column = lax.broadcasted_iota(jnp.int32, tile, 1) - lax.broadcasted_iota(jnp.int32, tile, 0)
    blocks = [stencil_ref[at, 3 * near_count : 3 * near_count + 1].astype(jnp.int32) for at in range(slots)]
    picks = [
        jnp.where(jnp.concatenate([block // PER_ROW * ROWS] * PER_ROW, axis=1) == column, 1.0, 0.0) for block in blocks
    ]
    found = jnp.dot(
        jnp.concatenate(picks, axis=0).astype(jnp.bfloat16), table, preferred_element_type=jnp.float32
    )
    owns = []
    for at, block in enumerate(blocks):
        rows = found[at * ROWS : (at + 1) * ROWS]
        odd = jnp.broadcast_to(block % PER_ROW, (ROWS, LANES))
        owns.append(jnp.where(odd == 1, rows[:, LANES:], rows[:, :LANES]))
    return owns


def outer_kernel(twins, near_count, fields, row_ref, cells_ref, *refs):
    selected, refs = refs[:twins], refs[twins:]
    out_refs, (tables, owns) = refs[:-2], refs[-2:]
    cap = owns.shape[1]
    rows = message_rows(fields, twins)
    for twin in range(twins):
        for block in range(tables.shape[1] // ROWS * PER_ROW):
            part, column = block // PER_ROW, block % PER_ROW * LANES
            first = block * rows + HALF * twin
            tables[twin, part * ROWS : (part + 1) * ROWS, column : column + LANES] = cells_ref[first : first + ROWS]
    for twin, stencil_ref in enumerate(selected):
        for at, own in enumerate(own_cells(near_count, tables[twin], stencil_ref)):
            if at < cap:
                owns[twin, at] = own
                continue
            shift = twin * (fields - HALF)
            results = rebuild(near_count, tables[twin], row_ref, stencil_ref[at], own, shift)
            for kind, result in enumerate(results):
                out_refs[at // cap - 1][twin, at % cap * len(results) + kind] = result.astype(jnp.bfloat16)


def inner_kernel(near_count, fields, row_ref, tables, owns, *refs):
    selected, out_ref = refs[:-1], refs[-1]
    for twin, stencil_ref in enumerate(selected):
        for at in range(owns.shape[1]):
            own = owns[twin, at]
            shift = twin * (fields - HALF)
            results = rebuild(near_count, tables[twin], row_ref, stencil_ref[at], own, shift)
            for kind, result in enumerate(results):
                out_ref[twin, at * len(results) + kind] = result.astype(jnp.bfloat16)


def remap_kernel(packed, fields, cover_ref, count_ref, weight_ref, moves_ref, high_ref, *refs):
    received, (out_ref, source_ref) = refs[:-2], refs[-2:]
    me = lax.axis_index("local")
    ocean_blocks, slots, kinds = weight_ref.shape[:3]
    cap = source_ref.shape[1] // kinds
    for apart, piece_ref in enumerate(received):
        for twin in range(piece_ref.shape[0]):
            source_ref[me ^ apart ^ (2 * twin)] = piece_ref[twin]
    results = []
    for block in range(ocean_blocks):
        values, weights = [], []
        for slot in range(slots):
            at = cover_ref[block, slot]
            live = slot < count_ref[block]
            for kind in range(kinds):
                value = source_ref[at // cap, at % cap * kinds + kind]
                values.append(jnp.where(live, value, jnp.zeros_like(value)))
                weights.append(weight_ref[block, slot, kind])
        product = lax.dot_general(
            jnp.concatenate(values, axis=1),
            jnp.concatenate(weights, axis=1),
            (((1,), (1,)), ((), ())),
            preferred_element_type=jnp.float32,
        )
        results.append(product)
    remapped = jnp.concatenate(results, axis=1)
    cells = remapped.shape[1]
    coarse = remapped.astype(jnp.bfloat16)
    fine = (remapped - coarse.astype(jnp.float32)).astype(jnp.bfloat16)
    table = [part[:, at : at + DEPTH] for at in range(0, cells, DEPTH) for part in (coarse, fine)]
    moved = jnp.dot(jnp.concatenate(table, axis=0), moves_ref[...], preferred_element_type=jnp.float32)
    moved = choose(moved, high_ref[...], 2 * ROWS)
    moved = moved[:ROWS] + moved[ROWS:]
    if not packed:
        out_ref[...] = moved[:fields]
        return
    half = fields // 2
    rows = out_ref.shape[1]
    listed = listing(out_ref.shape[0])
    side = lax.broadcasted_iota(jnp.int32, (rows, LANES), 1) < LANES // 2
    for pair in range(cells // LANES):
        columns = moved[:, pair * LANES : (pair + 1) * LANES]
        first, second = columns[:rows], columns[half : half + rows]
        out_ref[listed.index(2 * pair)] = jnp.where(side, first, pltpu.roll(second, LANES // 2, 1))
        out_ref[listed.index(2 * pair + 1)] = jnp.where(side, pltpu.roll(first, LANES // 2, 1), second)


def land_kernel(landed_ref, out_ref):
    count = landed_ref.shape[0]
    listed = listing(count)
    half = out_ref.shape[0] // 2
    side = lax.broadcasted_iota(jnp.int32, (half, LANES), 1) < LANES // 2
    for pair in range(count // 2):
        even, odd = landed_ref[listed.index(2 * pair), :half], landed_ref[listed.index(2 * pair + 1), :half]
        columns = pl.ds(pair * LANES, LANES)
        out_ref[:half, columns] = jnp.where(side, even, pltpu.roll(odd, LANES // 2, 1))
        out_ref[half:, columns] = jnp.where(side, pltpu.roll(even, LANES // 2, 1), odd)


def send(array, axis, apart):
    return lax.ppermute(array, axis, [(at, at ^ apart) for at in range(lax.axis_size(axis))])


def listing(count):
    return sorted(range(count), key=lambda at: (abs(2 * at - count + 1), -at))


def swap(pieces, axis):
    groups = [listing(lax.axis_size(axis))]
    pieces = pieces.transpose(1, 0, 2)
    swapped = lax.all_to_all(pieces, axis, split_axis=1, concat_axis=1, axis_index_groups=groups, tiled=True)
    return swapped.transpose(1, 0, 2)


SPACES = {"s": pltpu.SMEM, "v": pltpu.VMEM, "h": pltpu.HBM, "a": pl.ANY}


def call(kernel, outs, memories, scratch=(), out_memory="v", flops=0, moved=0):
    if isinstance(outs, list):
        out_specs = [pl.BlockSpec(memory_space=SPACES[kind]) for kind in (out_memory * len(outs))[: len(outs)]]
    else:
        out_specs = pl.BlockSpec(memory_space=SPACES[out_memory])
    return pl.pallas_call(
        kernel,
        out_shape=outs,
        in_specs=[pl.BlockSpec(memory_space=SPACES[kind]) for kind in memories],
        out_specs=out_specs,
        scratch_shapes=list(scratch),
        cost_estimate=pl.CostEstimate(flops=flops, bytes_accessed=moved, transcendentals=0),
        compiler_params=pltpu.CompilerParams(vmem_limit_bytes=VMEM_LIMIT),
    )


def shards(
    atm_flux,
    cell_map,
    neighbours,
    coef_x,
    coef_y,
    send_list,
    cover,
    cover_count,
    weights,
    ocean_map,
):
    fields, cells = atm_flux.shape
    region_count = lax.axis_size("region")
    local_count = lax.axis_size("local")
    everyone = ("region", "local")
    devices = region_count * local_count
    piece = cells // devices
    blocks = cells // LANES
    table = (cells // DEPTH * ROWS, DEPTH)
    shaped = jax.ShapeDtypeStruct
    twins = 2 if local_count == 4 and piece == LANES else 1
    cap = send_list.shape[2]
    aparts = local_count // twins
    near_count = neighbours.shape[0]
    kinds = weights.shape[2]
    ocean_cells = ocean_map.shape[1]

    def stay(*arrays):
        return [pltpu.with_memory_space_constraint(array, pltpu.HBM) for array in arrays]

    def scratch(array):
        return pltpu.VMEM(array.shape, array.dtype)

    rows = message_rows(fields, twins)
    messages = (blocks * rows, LANES)
    ordered = call(
        functools.partial(order_kernel, twins),
        shaped(messages, jnp.bfloat16),
        "hh",
        [
            scratch(cell_map),
            scratch(atm_flux),
            pltpu.VMEM(messages, jnp.bfloat16),
            pltpu.VMEM((cells // DEPTH * fields, DEPTH), jnp.bfloat16),
            pltpu.VMEM((DEPTH, WIDTH), jnp.bfloat16),
            pltpu.SemaphoreType.DMA((cells // STEP + 5,)),
        ],
        out_memory="h",
    )(*stay(cell_map, atm_flux))

    stencil = shaped((aparts * cap, ROWS, LANES), jnp.float32)
    selected = call(
        select_kernel,
        [stencil] * twins,
        "ahhhh",
        [
            pltpu.SMEM(send_list.shape, send_list.dtype),
            scratch(neighbours),
            scratch(coef_x),
            scratch(coef_y),
            pltpu.SemaphoreType.DMA((4,)),
        ],
        moved=3_000_000,
    )(ordered, *stay(send_list, neighbours, coef_x, coef_y))
    selected = [selected[0]] + [send(array, "local", 2) for array in selected[1:]]

    later = [cover, cover_count, weights]
    row, moves, high, cover, cover_count, weights = call(
        fetch_kernel,
        [
            shaped((DEPTH, WIDTH), jnp.bfloat16),
            shaped((DEPTH, ocean_cells), jnp.bfloat16),
            shaped(ocean_map.shape, ocean_map.dtype),
            pltpu.SMEM(cover.shape, cover.dtype),
            pltpu.SMEM(cover_count.shape, cover_count.dtype),
            shaped(weights.shape, weights.dtype),
        ],
        "ah" + "h" * len(later),
        [scratch(ocean_map), pltpu.SemaphoreType.DMA((len(later) + 1,))],
        out_memory="vvvssv",
        moved=3_000_000,
    )(ordered, *stay(ocean_map, *later))

    if piece == LANES:
        coupled = lax.all_to_all(ordered, everyone, split_axis=0, concat_axis=0, tiled=True)
    else:
        outgoing = ordered.reshape(blocks, rows, LANES)[:, :fields].transpose(1, 0, 2).reshape(fields, devices, piece)
        coupled = lax.all_to_all(outgoing, everyone, split_axis=1, concat_axis=1, tiled=True)
        coupled = coupled.reshape(fields, blocks, LANES).transpose(1, 0, 2)
        coupled = jnp.pad(coupled, ((0, 0), (0, rows - fields), (0, 0))).reshape(messages)

    sent = shaped((twins, cap * kinds, ROWS, LANES), jnp.bfloat16)
    tables = shaped((twins,) + table, jnp.bfloat16)
    owns = shaped((twins, cap, ROWS, LANES), jnp.float32)
    work = 2 * twins * cap * table[0] * DEPTH * near_count * LANES
    *outer, tables, owns = call(
        functools.partial(outer_kernel, twins, near_count, fields),
        [sent] * (aparts - 1) + [tables, owns],
        "vv" + "v" * twins,
        flops=work * (aparts - 1),
    )(row, coupled, *selected)
    source = [send(array, "local", 1 + at) for at, array in enumerate(outer)]
    inner = call(
        functools.partial(inner_kernel, near_count, fields),
        sent,
        "vvv" + "v" * twins,
        flops=work,
        moved=4_000_000,
    )(row, tables, owns, *selected)
    source = [inner] + source

    share = ocean_cells // region_count
    packed = share * 2 == LANES
    out_shape = (region_count, ROWS // 2, LANES) if packed else (fields, ocean_cells)
    leaving = call(
        functools.partial(remap_kernel, packed, fields),
        shaped(out_shape, jnp.float32),
        "ssvvv" + "v" * aparts,
        [pltpu.VMEM((local_count, cap * kinds, ROWS, LANES), jnp.bfloat16)],
    )(cover, cover_count, weights, moves, high, *source)
    if packed:
        landed = swap(leaving, "region")
        return call(land_kernel, shaped((fields, ocean_cells), jnp.float32), "v")(landed)
    leaving = leaving.reshape(fields, region_count, share)
    landed = lax.all_to_all(leaving, "region", split_axis=1, concat_axis=1, tiled=True)
    return landed.reshape(fields, ocean_cells)


def solution(mesh):
    return jax.shard_map(
        shards,
        mesh=mesh,
        in_specs=(
            P(None, ("region", "local")),
            P(("region", "local"), None),
            P(None, ("region", "local")),
            P(None, ("region", "local")),
            P(None, ("region", "local")),
            P(("region", "local"), None, None),
            P(("region", "local"), None),
            P(("region", "local")),
            P(("region", "local"), None, None, None, None),
            P(("region", "local"), None),
        ),
        out_specs=P(None, ("region", "local")),
        check_vma=False,
    )
```

```python
import functools

import jax
import jax.numpy as jnp
from jax import lax
from jax.experimental import pallas as pl
from jax.experimental.pallas import tpu as pltpu
from jax.sharding import PartitionSpec as P

ROWS = 16
HALF = 8
LANES = 128
DEPTH = 256
PER_ROW = DEPTH // LANES
STEP = 512
WIDTH = 256
VMEM_LIMIT = 40 * 1024 * 1024


def one_hot(index):
    row = lax.broadcasted_iota(jnp.int32, (DEPTH, index.shape[1]), 0).astype(jnp.int16)
    low = (index & (DEPTH - 1)).astype(jnp.int16)
    return jnp.where(row == low, jnp.bfloat16(1), jnp.bfloat16(0))


def choose(found, high, height):
    high = jnp.broadcast_to(high, (height, found.shape[1]))
    result = found[:height]
    for part in range(1, found.shape[0] // height):
        result = jnp.where(high == part, found[part * height : (part + 1) * height], result)
    return result


def lookup(table, index):
    results = []
    for at in range(0, index.shape[1], WIDTH):
        here = index[:, at : at + WIDTH]
        found = jnp.dot(table, one_hot(here), preferred_element_type=jnp.float32)
        results.append(choose(found, here // DEPTH, ROWS))
    return jnp.concatenate(results, axis=1)


def lookup_dense(table, index, parts):
    results = []
    for at in range(0, index.shape[1], WIDTH):
        here = index[:, at : at + WIDTH]
        found = jnp.dot(table, one_hot(here), preferred_element_type=jnp.float32)
        high = here // DEPTH
        upper = choose(found[: HALF * parts], high, HALF)
        lower = choose(found[HALF * parts :], high // 2, HALF)
        odd = jnp.broadcast_to(high % 2, lower.shape)
        results.append(jnp.concatenate([upper, jnp.where(odd == 1, pltpu.roll(lower, HALF // 2, 0), lower)], axis=0))
    return jnp.concatenate(results, axis=1)


def copies_of(sources, targets, sems, first=0):
    return [
        pltpu.make_async_copy(source, target, sems.at[first + at])
        for at, (source, target) in enumerate(zip(sources, targets))
    ]


def message_rows(fields, twins):
    return 2 * fields if twins == 2 else ROWS


def order_kernel(twins, map_hbm, flux_hbm, out_hbm, map_ref, flux_ref, out_ref, table, sems):
    fields, cells = flux_ref.shape
    steps = cells // STEP
    spans = [pl.ds(at, cells // 4) for at in range(0, cells, cells // 4)]
    needed = copies_of([flux_hbm.at[:, span] for span in spans], [flux_ref.at[:, span] for span in spans], sems)
    needed += copies_of((map_hbm,), (map_ref,), sems, 4)
    for copy in needed:
        copy.start()
    for copy in needed:
        copy.wait()
    parts, rest = cells // DEPTH, fields - HALF
    for part in range(parts):
        columns = slice(part * DEPTH, (part + 1) * DEPTH)
        table[part * HALF : (part + 1) * HALF] = flux_ref[:HALF, columns]
        table[parts * HALF + part * rest : parts * HALF + (part + 1) * rest] = flux_ref[HALF:, columns]
    rows = message_rows(fields, twins)
    written = []
    for step in range(steps):
        found = lookup_dense(table[...], map_ref[:, step * STEP : (step + 1) * STEP], parts)
        pieces = [found[:, at : at + LANES] for at in range(0, STEP, LANES)]
        if twins == 2:
            pieces = [
                jnp.concatenate([pieces[at][:fields], pieces[at ^ 2][:fields]], axis=0) for at in range(len(pieces))
            ]
        for at, piece in enumerate(pieces):
            first = (step * len(pieces) + at) * rows
            out_ref[first : first + rows] = piece.astype(jnp.bfloat16)
        span = pl.ds(step * len(pieces) * rows, len(pieces) * rows)
        written.append(pltpu.make_async_copy(out_ref.at[span], out_hbm.at[span], sems.at[5 + step]))
        written[-1].start()
    for copy in written:
        copy.wait()


def select_kernel(after_ref, list_hbm, near_hbm, x_hbm, y_hbm, *refs):
    selected, (list_ref, near_ref, x_ref, y_ref, sems) = refs[:-5], refs[-5:]
    copies = copies_of((list_hbm, near_hbm, x_hbm, y_hbm), (list_ref, near_ref, x_ref, y_ref), sems)
    for copy in copies:
        copy.start()
    for copy in copies:
        copy.wait()
    me = lax.axis_index("local")
    cap = list_ref.shape[2]
    count = list_ref.shape[1] // len(selected)
    near_count = near_ref.shape[0]
    for twin, stencil_ref in reversed(list(enumerate(selected))):
        for at in range(count * cap):
            block = list_ref[0, me ^ (2 * twin) ^ (at // cap), at % cap]
            columns = pl.ds(pl.multiple_of(block * LANES, LANES), LANES)
            stencil_ref[at, :near_count] = near_ref[:, columns].astype(jnp.float32)
            stencil_ref[at, near_count : 2 * near_count] = x_ref[:, columns]
            stencil_ref[at, 2 * near_count : 3 * near_count] = y_ref[:, columns]
            rest = (ROWS - 3 * near_count, LANES)
            stencil_ref[at, 3 * near_count :] = jnp.broadcast_to(block, rest).astype(jnp.float32)


def fetch_kernel(after_ref, map_hbm, *refs):
    count = (len(refs) - 4) // 2
    sources, (moves_ref, high_ref), targets, (map_ref, sems) = refs[:count], refs[count : count + 2], refs[count + 2 : -2], refs[-2:]
    (needed,) = copies_of((map_hbm,), (map_ref,), sems, count)
    others = copies_of(sources, targets, sems)
    for copy in [needed] + others:
        copy.start()
    needed.wait()
    moves_ref[...] = one_hot(map_ref[...])
    high_ref[...] = map_ref[...] // DEPTH
    for copy in others:
        copy.wait()


def rebuild(near_count, table, stencil, own, shift):
    near = stencil[:near_count].astype(jnp.int32)
    index = jnp.concatenate([near[j : j + 1] for j in range(near_count)], axis=1)
    found = lookup(table, index)
    upper = lower = own
    slope_x = slope_y = jnp.zeros_like(own)
    for j in range(near_count):
        value = found[:, j * LANES : (j + 1) * LANES]
        change = value - own
        slope_x += stencil[near_count + j : near_count + j + 1] * change
        slope_y += stencil[2 * near_count + j : 2 * near_count + j + 1] * change
        upper, lower = jnp.maximum(upper, value), jnp.minimum(lower, value)
    steep = jnp.abs(slope_x) + jnp.abs(slope_y)
    factor = jnp.minimum(1.0, (upper - lower) / jnp.maximum(steep, 1.0))
    results = [own, factor * slope_x, factor * slope_y]
    if shift:
        spare = jnp.zeros((shift, LANES), jnp.float32)
        results = [jnp.concatenate([result[shift:], spare], axis=0) for result in results]
    return results


def own_cells(near_count, table, stencil_ref):
    slots = stencil_ref.shape[0]
    tile = (ROWS, DEPTH)
    column = lax.broadcasted_iota(jnp.int32, tile, 1) - lax.broadcasted_iota(jnp.int32, tile, 0)
    blocks = [stencil_ref[at, 3 * near_count : 3 * near_count + 1].astype(jnp.int32) for at in range(slots)]
    picks = [
        jnp.where(jnp.concatenate([block // PER_ROW * ROWS] * PER_ROW, axis=1) == column, 1.0, 0.0) for block in blocks
    ]
    found = jnp.dot(
        jnp.concatenate(picks, axis=0).astype(jnp.bfloat16), table, preferred_element_type=jnp.float32
    )
    owns = []
    for at, block in enumerate(blocks):
        rows = found[at * ROWS : (at + 1) * ROWS]
        odd = jnp.broadcast_to(block % PER_ROW, (ROWS, LANES))
        owns.append(jnp.where(odd == 1, rows[:, LANES:], rows[:, :LANES]))
    return owns


def outer_kernel(twins, near_count, fields, after_ref, cells_ref, *refs):
    selected, refs = refs[:twins], refs[twins:]
    out_refs, (tables, owns) = refs[:-2], refs[-2:]
    cap = owns.shape[1]
    rows = message_rows(fields, twins)
    for twin in range(twins):
        for block in range(tables.shape[1] // ROWS * PER_ROW):
            part, column = block // PER_ROW, block % PER_ROW * LANES
            first = block * rows + HALF * twin
            tables[twin, part * ROWS : (part + 1) * ROWS, column : column + LANES] = cells_ref[first : first + ROWS]
    for twin, stencil_ref in enumerate(selected):
        for at, own in enumerate(own_cells(near_count, tables[twin], stencil_ref)):
            if at < cap:
                owns[twin, at] = own
                continue
            shift = twin * (fields - HALF)
            results = rebuild(near_count, tables[twin], stencil_ref[at], own, shift)
            for kind, result in enumerate(results):
                out_refs[at // cap - 1][twin, at % cap * len(results) + kind] = result.astype(jnp.bfloat16)


def inner_kernel(near_count, fields, tables, owns, *refs):
    selected, out_ref = refs[:-1], refs[-1]
    for twin, stencil_ref in enumerate(selected):
        for at in range(owns.shape[1]):
            own = owns[twin, at]
            shift = twin * (fields - HALF)
            results = rebuild(near_count, tables[twin], stencil_ref[at], own, shift)
            for kind, result in enumerate(results):
                out_ref[twin, at * len(results) + kind] = result.astype(jnp.bfloat16)


def remap_kernel(packed, fields, cover_ref, count_ref, weight_ref, moves_ref, high_ref, *refs):
    received, (out_ref, source_ref) = refs[:-2], refs[-2:]
    me = lax.axis_index("local")
    ocean_blocks, slots, kinds = weight_ref.shape[:3]
    cap = source_ref.shape[1] // kinds
    for apart, piece_ref in enumerate(received):
        for twin in range(piece_ref.shape[0]):
            source_ref[me ^ apart ^ (2 * twin)] = piece_ref[twin]
    results = []
    for block in range(ocean_blocks):
        values, weights = [], []
        for slot in range(slots):
            at = cover_ref[block, slot]
            live = slot < count_ref[block]
            for kind in range(kinds):
                value = source_ref[at // cap, at % cap * kinds + kind]
                values.append(jnp.where(live, value, jnp.zeros_like(value)))
                weights.append(weight_ref[block, slot, kind])
        product = lax.dot_general(
            jnp.concatenate(values, axis=1),
            jnp.concatenate(weights, axis=1),
            (((1,), (1,)), ((), ())),
            preferred_element_type=jnp.float32,
        )
        results.append(product)
    remapped = jnp.concatenate(results, axis=1)
    cells = remapped.shape[1]
    coarse = remapped.astype(jnp.bfloat16)
    fine = (remapped - coarse.astype(jnp.float32)).astype(jnp.bfloat16)
    table = [part[:, at : at + DEPTH] for at in range(0, cells, DEPTH) for part in (coarse, fine)]
    moved = jnp.dot(jnp.concatenate(table, axis=0), moves_ref[...], preferred_element_type=jnp.float32)
    moved = choose(moved, high_ref[...], 2 * ROWS)
    moved = moved[:ROWS] + moved[ROWS:]
    if not packed:
        out_ref[...] = moved[:fields]
        return
    half = fields // 2
    rows = out_ref.shape[1]
    listed = listing(out_ref.shape[0])
    side = lax.broadcasted_iota(jnp.int32, (rows, LANES), 1) < LANES // 2
    for pair in range(cells // LANES):
        columns = moved[:, pair * LANES : (pair + 1) * LANES]
        first, second = columns[:rows], columns[half : half + rows]
        out_ref[listed.index(2 * pair)] = jnp.where(side, first, pltpu.roll(second, LANES // 2, 1))
        out_ref[listed.index(2 * pair + 1)] = jnp.where(side, pltpu.roll(first, LANES // 2, 1), second)


def land_kernel(landed_ref, out_ref):
    count = landed_ref.shape[0]
    listed = listing(count)
    half = out_ref.shape[0] // 2
    side = lax.broadcasted_iota(jnp.int32, (half, LANES), 1) < LANES // 2
    for pair in range(count // 2):
        even, odd = landed_ref[listed.index(2 * pair), :half], landed_ref[listed.index(2 * pair + 1), :half]
        columns = pl.ds(pair * LANES, LANES)
        out_ref[:half, columns] = jnp.where(side, even, pltpu.roll(odd, LANES // 2, 1))
        out_ref[half:, columns] = jnp.where(side, pltpu.roll(even, LANES // 2, 1), odd)


def send(array, axis, apart):
    return lax.ppermute(array, axis, [(at, at ^ apart) for at in range(lax.axis_size(axis))])


def listing(count):
    return sorted(range(count), key=lambda at: (abs(2 * at - count + 1), -at))


def swap(pieces, axis):
    groups = [listing(lax.axis_size(axis))]
    pieces = pieces.transpose(1, 0, 2)
    swapped = lax.all_to_all(pieces, axis, split_axis=1, concat_axis=1, axis_index_groups=groups, tiled=True)
    return swapped.transpose(1, 0, 2)


SPACES = {"s": pltpu.SMEM, "v": pltpu.VMEM, "h": pltpu.HBM, "a": pl.ANY}


def call(kernel, outs, memories, scratch=(), out_memory="v", flops=0, moved=0):
    if isinstance(outs, list):
        out_specs = [pl.BlockSpec(memory_space=SPACES[kind]) for kind in (out_memory * len(outs))[: len(outs)]]
    else:
        out_specs = pl.BlockSpec(memory_space=SPACES[out_memory])
    return pl.pallas_call(
        kernel,
        out_shape=outs,
        in_specs=[pl.BlockSpec(memory_space=SPACES[kind]) for kind in memories],
        out_specs=out_specs,
        scratch_shapes=list(scratch),
        cost_estimate=pl.CostEstimate(flops=flops, bytes_accessed=moved, transcendentals=0),
        compiler_params=pltpu.CompilerParams(vmem_limit_bytes=VMEM_LIMIT),
    )


def shards(
    atm_flux,
    cell_map,
    neighbours,
    coef_x,
    coef_y,
    send_list,
    cover,
    cover_count,
    weights,
    ocean_map,
):
    fields, cells = atm_flux.shape
    region_count = lax.axis_size("region")
    local_count = lax.axis_size("local")
    everyone = ("region", "local")
    devices = region_count * local_count
    piece = cells // devices
    blocks = cells // LANES
    table = (cells // DEPTH * ROWS, DEPTH)
    shaped = jax.ShapeDtypeStruct
    twins = 2 if local_count == 4 and piece == LANES else 1
    cap = send_list.shape[2]
    aparts = local_count // twins
    near_count = neighbours.shape[0]
    kinds = weights.shape[2]
    ocean_cells = ocean_map.shape[1]

    def stay(*arrays):
        return [pltpu.with_memory_space_constraint(array, pltpu.HBM) for array in arrays]

    def scratch(array):
        return pltpu.VMEM(array.shape, array.dtype)

    rows = message_rows(fields, twins)
    messages = (blocks * rows, LANES)
    ordered = call(
        functools.partial(order_kernel, twins),
        shaped(messages, jnp.bfloat16),
        "hh",
        [
            scratch(cell_map),
            scratch(atm_flux),
            pltpu.VMEM(messages, jnp.bfloat16),
            pltpu.VMEM((cells // DEPTH * fields, DEPTH), jnp.bfloat16),
            pltpu.SemaphoreType.DMA((cells // STEP + 5,)),
        ],
        out_memory="h",
    )(*stay(cell_map, atm_flux))

    stencil = shaped((aparts * cap, ROWS, LANES), jnp.float32)
    selected = call(
        select_kernel,
        [stencil] * twins,
        "ahhhh",
        [
            pltpu.SMEM(send_list.shape, send_list.dtype),
            scratch(neighbours),
            scratch(coef_x),
            scratch(coef_y),
            pltpu.SemaphoreType.DMA((4,)),
        ],
        moved=3_000_000,
    )(ordered, *stay(send_list, neighbours, coef_x, coef_y))
    selected = [selected[0]] + [send(array, "local", 2) for array in selected[1:]]

    later = [cover, cover_count, weights]
    moves, high, cover, cover_count, weights = call(
        fetch_kernel,
        [
            shaped((DEPTH, ocean_cells), jnp.bfloat16),
            shaped(ocean_map.shape, ocean_map.dtype),
            pltpu.SMEM(cover.shape, cover.dtype),
            pltpu.SMEM(cover_count.shape, cover_count.dtype),
            shaped(weights.shape, weights.dtype),
        ],
        "ah" + "h" * len(later),
        [scratch(ocean_map), pltpu.SemaphoreType.DMA((len(later) + 1,))],
        out_memory="vvssv",
        moved=3_000_000,
    )(ordered, *stay(ocean_map, *later))

    if piece == LANES:
        coupled = lax.all_to_all(ordered, everyone, split_axis=0, concat_axis=0, tiled=True)
    else:
        outgoing = ordered.reshape(blocks, rows, LANES)[:, :fields].transpose(1, 0, 2).reshape(fields, devices, piece)
        coupled = lax.all_to_all(outgoing, everyone, split_axis=1, concat_axis=1, tiled=True)
        coupled = coupled.reshape(fields, blocks, LANES).transpose(1, 0, 2)
        coupled = jnp.pad(coupled, ((0, 0), (0, rows - fields), (0, 0))).reshape(messages)

    sent = shaped((twins, cap * kinds, ROWS, LANES), jnp.bfloat16)
    tables = shaped((twins,) + table, jnp.bfloat16)
    owns = shaped((twins, cap, ROWS, LANES), jnp.float32)
    work = 2 * twins * cap * table[0] * DEPTH * near_count * LANES
    *outer, tables, owns = call(
        functools.partial(outer_kernel, twins, near_count, fields),
        [sent] * (aparts - 1) + [tables, owns],
        "av" + "v" * twins,
        flops=work * (aparts - 1),
    )(moves, coupled, *selected)
    source = [send(array, "local", 1 + at) for at, array in enumerate(outer)]
    inner = call(
        functools.partial(inner_kernel, near_count, fields),
        sent,
        "vv" + "v" * twins,
        flops=work,
        moved=4_000_000,
    )(tables, owns, *selected)
    source = [inner] + source

    share = ocean_cells // region_count
    packed = share * 2 == LANES
    out_shape = (region_count, ROWS // 2, LANES) if packed else (fields, ocean_cells)
    leaving = call(
        functools.partial(remap_kernel, packed, fields),
        shaped(out_shape, jnp.float32),
        "ssvvv" + "v" * aparts,
        [pltpu.VMEM((local_count, cap * kinds, ROWS, LANES), jnp.bfloat16)],
    )(cover, cover_count, weights, moves, high, *source)
    if packed:
        landed = swap(leaving, "region")
        return call(land_kernel, shaped((fields, ocean_cells), jnp.float32), "v")(landed)
    leaving = leaving.reshape(fields, region_count, share)
    landed = lax.all_to_all(leaving, "region", split_axis=1, concat_axis=1, tiled=True)
    return landed.reshape(fields, ocean_cells)


def solution(mesh):
    return jax.shard_map(
        shards,
        mesh=mesh,
        in_specs=(
            P(None, ("region", "local")),
            P(("region", "local"), None),
            P(None, ("region", "local")),
            P(None, ("region", "local")),
            P(None, ("region", "local")),
            P(("region", "local"), None, None),
            P(("region", "local"), None),
            P(("region", "local")),
            P(("region", "local"), None, None, None, None),
            P(("region", "local"), None),
        ),
        out_specs=P(None, ("region", "local")),
        check_vma=False,
    )
```

```python
import functools

import jax
import jax.numpy as jnp
from jax import lax
from jax.experimental import pallas as pl
from jax.experimental.pallas import tpu as pltpu
from jax.sharding import PartitionSpec as P

ROWS = 16
HALF = 8
LANES = 128
DEPTH = 256
PER_ROW = DEPTH // LANES
STEP = 1024
WIDTH = 256
VMEM_LIMIT = 40 * 1024 * 1024


def one_hot(index):
    row = lax.broadcasted_iota(jnp.int32, (DEPTH, index.shape[1]), 0).astype(jnp.bfloat16)
    low = (index & (DEPTH - 1)).astype(jnp.bfloat16)
    return jnp.where(row == low, jnp.bfloat16(1), jnp.bfloat16(0))


def choose(found, high, height):
    high = jnp.broadcast_to(high, (height, found.shape[1]))
    result = found[:height]
    for part in range(1, found.shape[0] // height):
        result = jnp.where(high == part, found[part * height : (part + 1) * height], result)
    return result


def lookup(table, index):
    results = []
    for at in range(0, index.shape[1], WIDTH):
        here = index[:, at : at + WIDTH]
        found = jnp.dot(table, one_hot(here), preferred_element_type=jnp.float32)
        results.append(choose(found, here // DEPTH, ROWS))
    return jnp.concatenate(results, axis=1)


def lookup_dense(table, index, parts):
    results = []
    for at in range(0, index.shape[1], WIDTH):
        here = index[:, at : at + WIDTH]
        found = jnp.dot(table, one_hot(here), preferred_element_type=jnp.float32)
        high = here // DEPTH
        upper = choose(found[: HALF * parts], high, HALF)
        lower = choose(found[HALF * parts :], high // 2, HALF)
        odd = jnp.broadcast_to(high % 2, lower.shape)
        results.append(jnp.concatenate([upper, jnp.where(odd == 1, pltpu.roll(lower, HALF // 2, 0), lower)], axis=0))
    return jnp.concatenate(results, axis=1)


def copies_of(sources, targets, sems, first=0):
    return [
        pltpu.make_async_copy(source, target, sems.at[first + at])
        for at, (source, target) in enumerate(zip(sources, targets))
    ]


def message_rows(fields, twins):
    return 2 * fields if twins == 2 else ROWS


def order_kernel(twins, map_hbm, flux_hbm, out_hbm, map_ref, flux_ref, out_ref, table, sems):
    fields, cells = flux_ref.shape
    steps = cells // STEP
    needed = copies_of((map_hbm, flux_hbm), (map_ref, flux_ref), sems)
    for copy in needed:
        copy.start()
    for copy in needed:
        copy.wait()
    parts, rest = cells // DEPTH, fields - HALF
    for part in range(parts):
        columns = slice(part * DEPTH, (part + 1) * DEPTH)
        table[part * HALF : (part + 1) * HALF] = flux_ref[:HALF, columns]
        table[parts * HALF + part * rest : parts * HALF + (part + 1) * rest] = flux_ref[HALF:, columns]
    rows = message_rows(fields, twins)
    written = []
    for step in range(steps):
        found = lookup_dense(table[...], map_ref[:, step * STEP : (step + 1) * STEP], parts)
        pieces = [found[:, at : at + LANES] for at in range(0, STEP, LANES)]
        if twins == 2:
            pieces = [
                jnp.concatenate([pieces[at][:fields], pieces[at ^ 2][:fields]], axis=0) for at in range(len(pieces))
            ]
        for at, piece in enumerate(pieces):
            first = (step * len(pieces) + at) * rows
            out_ref[first : first + rows] = piece.astype(jnp.bfloat16)
        span = pl.ds(step * len(pieces) * rows, len(pieces) * rows)
        written.append(pltpu.make_async_copy(out_ref.at[span], out_hbm.at[span], sems.at[2 + step]))
        written[-1].start()
    for copy in written:
        copy.wait()


def select_kernel(after_ref, list_hbm, near_hbm, x_hbm, y_hbm, *refs):
    selected, (list_ref, near_ref, x_ref, y_ref, sems) = refs[:-5], refs[-5:]
    copies = copies_of((list_hbm, near_hbm, x_hbm, y_hbm), (list_ref, near_ref, x_ref, y_ref), sems)
    for copy in copies:
        copy.start()
    for copy in copies:
        copy.wait()
    me = lax.axis_index("local")
    cap = list_ref.shape[2]
    count = list_ref.shape[1] // len(selected)
    near_count = near_ref.shape[0]
    for twin, stencil_ref in reversed(list(enumerate(selected))):
        for at in range(count * cap):
            block = list_ref[0, me ^ (2 * twin) ^ (at // cap), at % cap]
            columns = pl.ds(pl.multiple_of(block * LANES, LANES), LANES)
            stencil_ref[at, :near_count] = near_ref[:, columns].astype(jnp.float32)
            stencil_ref[at, near_count : 2 * near_count] = x_ref[:, columns]
            stencil_ref[at, 2 * near_count : 3 * near_count] = y_ref[:, columns]
            rest = (ROWS - 3 * near_count, LANES)
            stencil_ref[at, 3 * near_count :] = jnp.broadcast_to(block, rest).astype(jnp.float32)


def fetch_kernel(after_ref, map_hbm, *refs):
    count = (len(refs) - 4) // 2
    sources, (moves_ref, high_ref), targets, (map_ref, sems) = refs[:count], refs[count : count + 2], refs[count + 2 : -2], refs[-2:]
    (needed,) = copies_of((map_hbm,), (map_ref,), sems, count)
    others = copies_of(sources, targets, sems)
    for copy in [needed] + others:
        copy.start()
    needed.wait()
    moves_ref[...] = one_hot(map_ref[...])
    high_ref[...] = map_ref[...] // DEPTH
    for copy in others:
        copy.wait()


def rebuild(near_count, table, stencil, own, shift):
    near = stencil[:near_count].astype(jnp.int32)
    index = jnp.concatenate([near[j : j + 1] for j in range(near_count)], axis=1)
    found = lookup(table, index)
    upper = lower = own
    slope_x = slope_y = jnp.zeros_like(own)
    for j in range(near_count):
        value = found[:, j * LANES : (j + 1) * LANES]
        change = value - own
        slope_x += stencil[near_count + j : near_count + j + 1] * change
        slope_y += stencil[2 * near_count + j : 2 * near_count + j + 1] * change
        upper, lower = jnp.maximum(upper, value), jnp.minimum(lower, value)
    steep = jnp.abs(slope_x) + jnp.abs(slope_y)
    factor = jnp.minimum(1.0, (upper - lower) / jnp.maximum(steep, 1.0))
    results = [own, factor * slope_x, factor * slope_y]
    if shift:
        spare = jnp.zeros((shift, LANES), jnp.float32)
        results = [jnp.concatenate([result[shift:], spare], axis=0) for result in results]
    return results


def own_cells(near_count, table, stencil_ref):
    slots = stencil_ref.shape[0]
    tile = (ROWS, DEPTH)
    column = lax.broadcasted_iota(jnp.int32, tile, 1) - lax.broadcasted_iota(jnp.int32, tile, 0)
    blocks = [stencil_ref[at, 3 * near_count : 3 * near_count + 1].astype(jnp.int32) for at in range(slots)]
    picks = [
        jnp.where(jnp.concatenate([block // PER_ROW * ROWS] * PER_ROW, axis=1) == column, 1.0, 0.0) for block in blocks
    ]
    found = jnp.dot(
        jnp.concatenate(picks, axis=0).astype(jnp.bfloat16), table, preferred_element_type=jnp.float32
    )
    owns = []
    for at, block in enumerate(blocks):
        rows = found[at * ROWS : (at + 1) * ROWS]
        odd = jnp.broadcast_to(block % PER_ROW, (ROWS, LANES))
        owns.append(jnp.where(odd == 1, rows[:, LANES:], rows[:, :LANES]))
    return owns


def outer_kernel(twins, near_count, fields, after_ref, cells_ref, *refs):
    selected, refs = refs[:twins], refs[twins:]
    out_refs, (tables, owns) = refs[:-2], refs[-2:]
    cap = owns.shape[1]
    rows = message_rows(fields, twins)
    for twin in range(twins):
        for block in range(tables.shape[1] // ROWS * PER_ROW):
            part, column = block // PER_ROW, block % PER_ROW * LANES
            first = block * rows + HALF * twin
            tables[twin, part * ROWS : (part + 1) * ROWS, column : column + LANES] = cells_ref[first : first + ROWS]
    for twin, stencil_ref in enumerate(selected):
        for at, own in enumerate(own_cells(near_count, tables[twin], stencil_ref)):
            if at < cap:
                owns[twin, at] = own
                continue
            shift = twin * (fields - HALF)
            results = rebuild(near_count, tables[twin], stencil_ref[at], own, shift)
            for kind, result in enumerate(results):
                out_refs[at // cap - 1][twin, at % cap * len(results) + kind] = result.astype(jnp.bfloat16)


def inner_kernel(near_count, fields, tables, owns, *refs):
    selected, out_ref = refs[:-1], refs[-1]
    for twin, stencil_ref in enumerate(selected):
        for at in range(owns.shape[1]):
            own = owns[twin, at]
            shift = twin * (fields - HALF)
            results = rebuild(near_count, tables[twin], stencil_ref[at], own, shift)
            for kind, result in enumerate(results):
                out_ref[twin, at * len(results) + kind] = result.astype(jnp.bfloat16)


def remap_kernel(packed, fields, cover_ref, count_ref, weight_ref, moves_ref, high_ref, *refs):
    received, out_ref = refs[:-1], refs[-1]
    me = lax.axis_index("local")
    ocean_blocks, slots, kinds = weight_ref.shape[:3]
    cap = received[0].shape[1] // kinds
    results = []
    for block in range(ocean_blocks):
        values, weights = [], []
        for slot in range(slots):
            at = cover_ref[block, slot]
            live = slot < count_ref[block]
            apart = me ^ (at // cap)
            twin, apart = apart // len(received), apart % len(received)
            for kind in range(kinds):
                value = received[0][twin, at % cap * kinds + kind]
                for other in range(1, len(received)):
                    value = jnp.where(apart == other, received[other][twin, at % cap * kinds + kind], value)
                values.append(jnp.where(live, value, jnp.zeros_like(value)))
                weights.append(weight_ref[block, slot, kind])
        product = lax.dot_general(
            jnp.concatenate(values, axis=1),
            jnp.concatenate(weights, axis=1),
            (((1,), (1,)), ((), ())),
            preferred_element_type=jnp.float32,
        )
        results.append(product)
    remapped = jnp.concatenate(results, axis=1)
    cells = remapped.shape[1]
    coarse = remapped.astype(jnp.bfloat16)
    fine = (remapped - coarse.astype(jnp.float32)).astype(jnp.bfloat16)
    table = [part[:, at : at + DEPTH] for at in range(0, cells, DEPTH) for part in (coarse, fine)]
    moved = jnp.dot(jnp.concatenate(table, axis=0), moves_ref[...], preferred_element_type=jnp.float32)
    moved = choose(moved, high_ref[...], 2 * ROWS)
    moved = moved[:ROWS] + moved[ROWS:]
    if not packed:
        out_ref[...] = moved[:fields]
        return
    half = fields // 2
    rows = out_ref.shape[1]
    listed = listing(out_ref.shape[0])
    side = lax.broadcasted_iota(jnp.int32, (rows, LANES), 1) < LANES // 2
    for pair in range(cells // LANES):
        columns = moved[:, pair * LANES : (pair + 1) * LANES]
        first, second = columns[:rows], columns[half : half + rows]
        out_ref[listed.index(2 * pair)] = jnp.where(side, first, pltpu.roll(second, LANES // 2, 1))
        out_ref[listed.index(2 * pair + 1)] = jnp.where(side, pltpu.roll(first, LANES // 2, 1), second)


def land_kernel(landed_ref, out_ref):
    count = landed_ref.shape[0]
    listed = listing(count)
    half = out_ref.shape[0] // 2
    side = lax.broadcasted_iota(jnp.int32, (half, LANES), 1) < LANES // 2
    for pair in range(count // 2):
        even, odd = landed_ref[listed.index(2 * pair), :half], landed_ref[listed.index(2 * pair + 1), :half]
        columns = pl.ds(pair * LANES, LANES)
        out_ref[:half, columns] = jnp.where(side, even, pltpu.roll(odd, LANES // 2, 1))
        out_ref[half:, columns] = jnp.where(side, pltpu.roll(even, LANES // 2, 1), odd)


def send(array, axis, apart):
    return lax.ppermute(array, axis, [(at, at ^ apart) for at in range(lax.axis_size(axis))])


def listing(count):
    return sorted(range(count), key=lambda at: (abs(2 * at - count + 1), -at))


def swap(pieces, axis):
    groups = [listing(lax.axis_size(axis))]
    pieces = pieces.transpose(1, 0, 2)
    swapped = lax.all_to_all(pieces, axis, split_axis=1, concat_axis=1, axis_index_groups=groups, tiled=True)
    return swapped.transpose(1, 0, 2)


SPACES = {"s": pltpu.SMEM, "v": pltpu.VMEM, "h": pltpu.HBM, "a": pl.ANY}


def call(kernel, outs, memories, scratch=(), out_memory="v", flops=0, moved=0):
    if isinstance(outs, list):
        out_specs = [pl.BlockSpec(memory_space=SPACES[kind]) for kind in (out_memory * len(outs))[: len(outs)]]
    else:
        out_specs = pl.BlockSpec(memory_space=SPACES[out_memory])
    return pl.pallas_call(
        kernel,
        out_shape=outs,
        in_specs=[pl.BlockSpec(memory_space=SPACES[kind]) for kind in memories],
        out_specs=out_specs,
        scratch_shapes=list(scratch),
        cost_estimate=pl.CostEstimate(flops=flops, bytes_accessed=moved, transcendentals=0),
        compiler_params=pltpu.CompilerParams(vmem_limit_bytes=VMEM_LIMIT),
    )


def shards(
    atm_flux,
    cell_map,
    neighbours,
    coef_x,
    coef_y,
    send_list,
    cover,
    cover_count,
    weights,
    ocean_map,
):
    fields, cells = atm_flux.shape
    region_count = lax.axis_size("region")
    local_count = lax.axis_size("local")
    everyone = ("region", "local")
    devices = region_count * local_count
    piece = cells // devices
    blocks = cells // LANES
    table = (cells // DEPTH * ROWS, DEPTH)
    shaped = jax.ShapeDtypeStruct
    twins = 2 if local_count == 4 and piece == LANES else 1
    cap = send_list.shape[2]
    aparts = local_count // twins
    near_count = neighbours.shape[0]
    kinds = weights.shape[2]
    ocean_cells = ocean_map.shape[1]

    def stay(*arrays):
        return [pltpu.with_memory_space_constraint(array, pltpu.HBM) for array in arrays]

    def scratch(array):
        return pltpu.VMEM(array.shape, array.dtype)

    rows = message_rows(fields, twins)
    messages = (blocks * rows, LANES)
    ordered = call(
        functools.partial(order_kernel, twins),
        shaped(messages, jnp.bfloat16),
        "hh",
        [
            scratch(cell_map),
            scratch(atm_flux),
            pltpu.VMEM(messages, jnp.bfloat16),
            pltpu.VMEM((cells // DEPTH * fields, DEPTH), jnp.bfloat16),
            pltpu.SemaphoreType.DMA((cells // STEP + 2,)),
        ],
        out_memory="h",
    )(*stay(cell_map, atm_flux))

    stencil = shaped((aparts * cap, ROWS, LANES), jnp.float32)
    selected = call(
        select_kernel,
        [stencil] * twins,
        "ahhhh",
        [
            pltpu.SMEM(send_list.shape, send_list.dtype),
            scratch(neighbours),
            scratch(coef_x),
            scratch(coef_y),
            pltpu.SemaphoreType.DMA((4,)),
        ],
        moved=3_000_000,
    )(ordered, *stay(send_list, neighbours, coef_x, coef_y))
    selected = [selected[0]] + [send(array, "local", 2) for array in selected[1:]]

    later = [cover, cover_count, weights]
    moves, high, cover, cover_count, weights = call(
        fetch_kernel,
        [
            shaped((DEPTH, ocean_cells), jnp.bfloat16),
            shaped(ocean_map.shape, ocean_map.dtype),
            pltpu.SMEM(cover.shape, cover.dtype),
            pltpu.SMEM(cover_count.shape, cover_count.dtype),
            shaped(weights.shape, weights.dtype),
        ],
        "ah" + "h" * len(later),
        [scratch(ocean_map), pltpu.SemaphoreType.DMA((len(later) + 1,))],
        out_memory="vvssv",
        moved=3_000_000,
    )(ordered, *stay(ocean_map, *later))

    if piece == LANES:
        coupled = lax.all_to_all(ordered, everyone, split_axis=0, concat_axis=0, tiled=True)
    else:
        outgoing = ordered.reshape(blocks, rows, LANES)[:, :fields].transpose(1, 0, 2).reshape(fields, devices, piece)
        coupled = lax.all_to_all(outgoing, everyone, split_axis=1, concat_axis=1, tiled=True)
        coupled = coupled.reshape(fields, blocks, LANES).transpose(1, 0, 2)
        coupled = jnp.pad(coupled, ((0, 0), (0, rows - fields), (0, 0))).reshape(messages)

    sent = shaped((twins, cap * kinds, ROWS, LANES), jnp.bfloat16)
    tables = shaped((twins,) + table, jnp.bfloat16)
    owns = shaped((twins, cap, ROWS, LANES), jnp.float32)
    work = 2 * twins * cap * table[0] * DEPTH * near_count * LANES
    *outer, tables, owns = call(
        functools.partial(outer_kernel, twins, near_count, fields),
        [sent] * (aparts - 1) + [tables, owns],
        "av" + "v" * twins,
        flops=work * (aparts - 1),
    )(moves, coupled, *selected)
    source = [send(array, "local", 1 + at) for at, array in enumerate(outer)]
    inner = call(
        functools.partial(inner_kernel, near_count, fields),
        sent,
        "vv" + "v" * twins,
        flops=work,
        moved=4_000_000,
    )(tables, owns, *selected)
    source = [inner] + source

    share = ocean_cells // region_count
    packed = share * 2 == LANES
    out_shape = (region_count, ROWS // 2, LANES) if packed else (fields, ocean_cells)
    leaving = call(
        functools.partial(remap_kernel, packed, fields),
        shaped(out_shape, jnp.float32),
        "ssvvv" + "v" * aparts,
    )(cover, cover_count, weights, moves, high, *source)
    if packed:
        landed = swap(leaving, "region")
        return call(land_kernel, shaped((fields, ocean_cells), jnp.float32), "v")(landed)
    leaving = leaving.reshape(fields, region_count, share)
    landed = lax.all_to_all(leaving, "region", split_axis=1, concat_axis=1, tiled=True)
    return landed.reshape(fields, ocean_cells)


def solution(mesh):
    return jax.shard_map(
        shards,
        mesh=mesh,
        in_specs=(
            P(None, ("region", "local")),
            P(("region", "local"), None),
            P(None, ("region", "local")),
            P(None, ("region", "local")),
            P(None, ("region", "local")),
            P(("region", "local"), None, None),
            P(("region", "local"), None),
            P(("region", "local")),
            P(("region", "local"), None, None, None, None),
            P(("region", "local"), None),
        ),
        out_specs=P(None, ("region", "local")),
        check_vma=False,
    )
```

```python
import functools

import jax
import jax.numpy as jnp
from jax import lax
from jax.experimental import pallas as pl
from jax.experimental.pallas import tpu as pltpu
from jax.sharding import PartitionSpec as P

ROWS = 16
HALF = 8
LANES = 128
DEPTH = 256
PER_ROW = DEPTH // LANES
STEP = 512
WIDTH = 256
VMEM_LIMIT = 40 * 1024 * 1024


def one_hot(index):
    row = lax.broadcasted_iota(jnp.int32, (DEPTH, index.shape[1]), 0).astype(jnp.bfloat16)
    low = (index & (DEPTH - 1)).astype(jnp.bfloat16)
    return jnp.where(row == low, jnp.bfloat16(1), jnp.bfloat16(0))


def choose(found, high, height):
    high = jnp.broadcast_to(high, (height, found.shape[1]))
    result = found[:height]
    for part in range(1, found.shape[0] // height):
        result = jnp.where(high == part, found[part * height : (part + 1) * height], result)
    return result


def lookup(table, index, hot=None):
    results = []
    for at in range(0, index.shape[1], WIDTH):
        here = index[:, at : at + WIDTH]
        made = one_hot(here) if hot is None else hot[:, at : at + WIDTH]
        found = jnp.dot(table, made, preferred_element_type=jnp.float32)
        results.append(choose(found, here // DEPTH, ROWS))
    return jnp.concatenate(results, axis=1)


def lookup_dense(table, index, parts):
    results = []
    for at in range(0, index.shape[1], WIDTH):
        here = index[:, at : at + WIDTH]
        found = jnp.dot(table, one_hot(here), preferred_element_type=jnp.float32)
        high = here // DEPTH
        upper = choose(found[: HALF * parts], high, HALF)
        lower = choose(found[HALF * parts :], high // 2, HALF)
        odd = jnp.broadcast_to(high % 2, lower.shape)
        results.append(jnp.concatenate([upper, jnp.where(odd == 1, pltpu.roll(lower, HALF // 2, 0), lower)], axis=0))
    return jnp.concatenate(results, axis=1)


def copies_of(sources, targets, sems, first=0):
    return [
        pltpu.make_async_copy(source, target, sems.at[first + at])
        for at, (source, target) in enumerate(zip(sources, targets))
    ]


def message_rows(fields, twins):
    return 2 * fields if twins == 2 else ROWS


def order_kernel(twins, map_hbm, flux_hbm, out_hbm, map_ref, flux_ref, out_ref, table, sems):
    fields, cells = flux_ref.shape
    steps = cells // STEP
    spans = [pl.ds(at, cells // 4) for at in range(0, cells, cells // 4)]
    needed = copies_of([flux_hbm.at[:, span] for span in spans], [flux_ref.at[:, span] for span in spans], sems)
    needed += copies_of((map_hbm,), (map_ref,), sems, 4)
    for copy in needed:
        copy.start()
    for copy in needed:
        copy.wait()
    parts, rest = cells // DEPTH, fields - HALF
    for part in range(parts):
        columns = slice(part * DEPTH, (part + 1) * DEPTH)
        table[part * HALF : (part + 1) * HALF] = flux_ref[:HALF, columns]
        table[parts * HALF + part * rest : parts * HALF + (part + 1) * rest] = flux_ref[HALF:, columns]
    rows = message_rows(fields, twins)
    written = []
    for step in range(steps):
        found = lookup_dense(table[...], map_ref[:, step * STEP : (step + 1) * STEP], parts)
        pieces = [found[:, at : at + LANES] for at in range(0, STEP, LANES)]
        if twins == 2:
            pieces = [
                jnp.concatenate([pieces[at][:fields], pieces[at ^ 2][:fields]], axis=0) for at in range(len(pieces))
            ]
        for at, piece in enumerate(pieces):
            first = (step * len(pieces) + at) * rows
            out_ref[first : first + rows] = piece.astype(jnp.bfloat16)
        span = pl.ds(step * len(pieces) * rows, len(pieces) * rows)
        written.append(pltpu.make_async_copy(out_ref.at[span], out_hbm.at[span], sems.at[5 + step]))
        written[-1].start()
    for copy in written:
        copy.wait()


def select_kernel(twins, after_ref, list_hbm, near_hbm, x_hbm, y_hbm, *refs):
    selected, hots, (list_ref, near_ref, x_ref, y_ref, sems) = refs[:twins], refs[twins:-5], refs[-5:]
    copies = copies_of((list_hbm, near_hbm, x_hbm, y_hbm), (list_ref, near_ref, x_ref, y_ref), sems)
    for copy in copies:
        copy.start()
    for copy in copies:
        copy.wait()
    me = lax.axis_index("local")
    cap = list_ref.shape[2]
    count = list_ref.shape[1] // len(selected)
    near_count = near_ref.shape[0]
    for twin, stencil_ref in reversed(list(enumerate(selected))):
        for at in range(count * cap):
            block = list_ref[0, me ^ (2 * twin) ^ (at // cap), at % cap]
            columns = pl.ds(pl.multiple_of(block * LANES, LANES), LANES)
            stencil_ref[at, :near_count] = near_ref[:, columns].astype(jnp.float32)
            stencil_ref[at, near_count : 2 * near_count] = x_ref[:, columns]
            stencil_ref[at, 2 * near_count : 3 * near_count] = y_ref[:, columns]
            rest = (ROWS - 3 * near_count, LANES)
            stencil_ref[at, 3 * near_count :] = jnp.broadcast_to(block, rest).astype(jnp.float32)
    for hot_ref in hots:
        for at in range(hot_ref.shape[0]):
            near = selected[0][cap + at, :near_count].astype(jnp.int32)
            hot_ref[at] = one_hot(jnp.concatenate([near[j : j + 1] for j in range(near_count)], axis=1))


def fetch_kernel(after_ref, map_hbm, *refs):
    count = (len(refs) - 4) // 2
    sources, (moves_ref, high_ref), targets, (map_ref, sems) = refs[:count], refs[count : count + 2], refs[count + 2 : -2], refs[-2:]
    (needed,) = copies_of((map_hbm,), (map_ref,), sems, count)
    others = copies_of(sources, targets, sems)
    for copy in [needed] + others:
        copy.start()
    needed.wait()
    moves_ref[...] = one_hot(map_ref[...])
    high_ref[...] = map_ref[...] // DEPTH
    for copy in others:
        copy.wait()


def rebuild(near_count, table, stencil, own, shift, hot=None):
    near = stencil[:near_count].astype(jnp.int32)
    index = jnp.concatenate([near[j : j + 1] for j in range(near_count)], axis=1)
    found = lookup(table, index, hot)
    upper = lower = own
    slope_x = slope_y = jnp.zeros_like(own)
    for j in range(near_count):
        value = found[:, j * LANES : (j + 1) * LANES]
        change = value - own
        slope_x += stencil[near_count + j : near_count + j + 1] * change
        slope_y += stencil[2 * near_count + j : 2 * near_count + j + 1] * change
        upper, lower = jnp.maximum(upper, value), jnp.minimum(lower, value)
    steep = jnp.abs(slope_x) + jnp.abs(slope_y)
    factor = jnp.minimum(1.0, (upper - lower) / jnp.maximum(steep, 1.0))
    results = [own, factor * slope_x, factor * slope_y]
    if shift:
        spare = jnp.zeros((shift, LANES), jnp.float32)
        results = [jnp.concatenate([result[shift:], spare], axis=0) for result in results]
    return results


def own_cells(near_count, table, stencil_ref):
    slots = stencil_ref.shape[0]
    tile = (ROWS, DEPTH)
    column = lax.broadcasted_iota(jnp.int32, tile, 1) - lax.broadcasted_iota(jnp.int32, tile, 0)
    blocks = [stencil_ref[at, 3 * near_count : 3 * near_count + 1].astype(jnp.int32) for at in range(slots)]
    picks = [
        jnp.where(jnp.concatenate([block // PER_ROW * ROWS] * PER_ROW, axis=1) == column, 1.0, 0.0) for block in blocks
    ]
    found = jnp.dot(
        jnp.concatenate(picks, axis=0).astype(jnp.bfloat16), table, preferred_element_type=jnp.float32
    )
    owns = []
    for at, block in enumerate(blocks):
        rows = found[at * ROWS : (at + 1) * ROWS]
        odd = jnp.broadcast_to(block % PER_ROW, (ROWS, LANES))
        owns.append(jnp.where(odd == 1, rows[:, LANES:], rows[:, :LANES]))
    return owns


def outer_kernel(twins, near_count, fields, after_ref, cells_ref, *refs):
    selected, refs = refs[:twins], refs[twins:]
    hots, refs = refs[: twins - 1], refs[twins - 1 :]
    out_refs, (tables, owns) = refs[:-2], refs[-2:]
    cap = owns.shape[1]
    rows = message_rows(fields, twins)
    for twin in range(twins):
        for block in range(tables.shape[1] // ROWS * PER_ROW):
            part, column = block // PER_ROW, block % PER_ROW * LANES
            first = block * rows + HALF * twin
            tables[twin, part * ROWS : (part + 1) * ROWS, column : column + LANES] = cells_ref[first : first + ROWS]
    for twin, stencil_ref in enumerate(selected):
        for at, own in enumerate(own_cells(near_count, tables[twin], stencil_ref)):
            if at < cap:
                owns[twin, at] = own
                continue
            shift = twin * (fields - HALF)
            hot = hots[0][at - cap] if hots and twin == 0 else None
            results = rebuild(near_count, tables[twin], stencil_ref[at], own, shift, hot)
            for kind, result in enumerate(results):
                out_refs[at // cap - 1][twin, at % cap * len(results) + kind] = result.astype(jnp.bfloat16)


def inner_kernel(near_count, fields, tables, owns, *refs):
    selected, out_ref = refs[:-1], refs[-1]
    for twin, stencil_ref in enumerate(selected):
        for at in range(owns.shape[1]):
            own = owns[twin, at]
            shift = twin * (fields - HALF)
            results = rebuild(near_count, tables[twin], stencil_ref[at], own, shift)
            for kind, result in enumerate(results):
                out_ref[twin, at * len(results) + kind] = result.astype(jnp.bfloat16)


def remap_kernel(packed, fields, cover_ref, count_ref, weight_ref, moves_ref, high_ref, *refs):
    received, (out_ref, source_ref) = refs[:-2], refs[-2:]
    me = lax.axis_index("local")
    ocean_blocks, slots, kinds = weight_ref.shape[:3]
    cap = source_ref.shape[1] // kinds
    for apart, piece_ref in enumerate(received):
        for twin in range(piece_ref.shape[0]):
            source_ref[me ^ apart ^ (2 * twin)] = piece_ref[twin]
    results = []
    for block in range(ocean_blocks):
        values, weights = [], []
        for slot in range(slots):
            at = cover_ref[block, slot]
            live = slot < count_ref[block]
            for kind in range(kinds):
                value = source_ref[at // cap, at % cap * kinds + kind]
                values.append(jnp.where(live, value, jnp.zeros_like(value)))
                weights.append(weight_ref[block, slot, kind])
        product = lax.dot_general(
            jnp.concatenate(values, axis=1),
            jnp.concatenate(weights, axis=1),
            (((1,), (1,)), ((), ())),
            preferred_element_type=jnp.float32,
        )
        results.append(product)
    remapped = jnp.concatenate(results, axis=1)
    cells = remapped.shape[1]
    coarse = remapped.astype(jnp.bfloat16)
    fine = (remapped - coarse.astype(jnp.float32)).astype(jnp.bfloat16)
    table = [part[:, at : at + DEPTH] for at in range(0, cells, DEPTH) for part in (coarse, fine)]
    moved = jnp.dot(jnp.concatenate(table, axis=0), moves_ref[...], preferred_element_type=jnp.float32)
    moved = choose(moved, high_ref[...], 2 * ROWS)
    moved = moved[:ROWS] + moved[ROWS:]
    if not packed:
        out_ref[...] = moved[:fields]
        return
    half = fields // 2
    rows = out_ref.shape[1]
    listed = listing(out_ref.shape[0])
    side = lax.broadcasted_iota(jnp.int32, (rows, LANES), 1) < LANES // 2
    for pair in range(cells // LANES):
        columns = moved[:, pair * LANES : (pair + 1) * LANES]
        first, second = columns[:rows], columns[half : half + rows]
        out_ref[listed.index(2 * pair)] = jnp.where(side, first, pltpu.roll(second, LANES // 2, 1))
        out_ref[listed.index(2 * pair + 1)] = jnp.where(side, pltpu.roll(first, LANES // 2, 1), second)


def land_kernel(landed_ref, out_ref):
    count = landed_ref.shape[0]
    listed = listing(count)
    half = out_ref.shape[0] // 2
    side = lax.broadcasted_iota(jnp.int32, (half, LANES), 1) < LANES // 2
    for pair in range(count // 2):
        even, odd = landed_ref[listed.index(2 * pair), :half], landed_ref[listed.index(2 * pair + 1), :half]
        columns = pl.ds(pair * LANES, LANES)
        out_ref[:half, columns] = jnp.where(side, even, pltpu.roll(odd, LANES // 2, 1))
        out_ref[half:, columns] = jnp.where(side, pltpu.roll(even, LANES // 2, 1), odd)


def send(array, axis, apart):
    return lax.ppermute(array, axis, [(at, at ^ apart) for at in range(lax.axis_size(axis))])


def listing(count):
    return sorted(range(count), key=lambda at: (abs(2 * at - count + 1), -at))


def swap(pieces, axis):
    groups = [listing(lax.axis_size(axis))]
    pieces = pieces.transpose(1, 0, 2)
    swapped = lax.all_to_all(pieces, axis, split_axis=1, concat_axis=1, axis_index_groups=groups, tiled=True)
    return swapped.transpose(1, 0, 2)


SPACES = {"s": pltpu.SMEM, "v": pltpu.VMEM, "h": pltpu.HBM, "a": pl.ANY}


def call(kernel, outs, memories, scratch=(), out_memory="v", flops=0, moved=0):
    if isinstance(outs, list):
        out_specs = [pl.BlockSpec(memory_space=SPACES[kind]) for kind in (out_memory * len(outs))[: len(outs)]]
    else:
        out_specs = pl.BlockSpec(memory_space=SPACES[out_memory])
    return pl.pallas_call(
        kernel,
        out_shape=outs,
        in_specs=[pl.BlockSpec(memory_space=SPACES[kind]) for kind in memories],
        out_specs=out_specs,
        scratch_shapes=list(scratch),
        cost_estimate=pl.CostEstimate(flops=flops, bytes_accessed=moved, transcendentals=0),
        compiler_params=pltpu.CompilerParams(vmem_limit_bytes=VMEM_LIMIT),
    )


def shards(
    atm_flux,
    cell_map,
    neighbours,
    coef_x,
    coef_y,
    send_list,
    cover,
    cover_count,
    weights,
    ocean_map,
):
    fields, cells = atm_flux.shape
    region_count = lax.axis_size("region")
    local_count = lax.axis_size("local")
    everyone = ("region", "local")
    devices = region_count * local_count
    piece = cells // devices
    blocks = cells // LANES
    table = (cells // DEPTH * ROWS, DEPTH)
    shaped = jax.ShapeDtypeStruct
    twins = 2 if local_count == 4 and piece == LANES else 1
    cap = send_list.shape[2]
    aparts = local_count // twins
    near_count = neighbours.shape[0]
    kinds = weights.shape[2]
    ocean_cells = ocean_map.shape[1]

    def stay(*arrays):
        return [pltpu.with_memory_space_constraint(array, pltpu.HBM) for array in arrays]

    def scratch(array):
        return pltpu.VMEM(array.shape, array.dtype)

    rows = message_rows(fields, twins)
    messages = (blocks * rows, LANES)
    ordered = call(
        functools.partial(order_kernel, twins),
        shaped(messages, jnp.bfloat16),
        "hh",
        [
            scratch(cell_map),
            scratch(atm_flux),
            pltpu.VMEM(messages, jnp.bfloat16),
            pltpu.VMEM((cells // DEPTH * fields, DEPTH), jnp.bfloat16),
            pltpu.SemaphoreType.DMA((cells // STEP + 5,)),
        ],
        out_memory="h",
    )(*stay(cell_map, atm_flux))

    stencil = shaped((aparts * cap, ROWS, LANES), jnp.float32)
    hots = [shaped((cap, DEPTH, near_count * LANES), jnp.bfloat16)] * (twins - 1)
    selected = call(
        functools.partial(select_kernel, twins),
        [stencil] * twins + hots,
        "ahhhh",
        [
            pltpu.SMEM(send_list.shape, send_list.dtype),
            scratch(neighbours),
            scratch(coef_x),
            scratch(coef_y),
            pltpu.SemaphoreType.DMA((4,)),
        ],
        moved=3_000_000,
    )(ordered, *stay(send_list, neighbours, coef_x, coef_y))
    hots = selected[twins:]
    selected = [selected[0]] + [send(array, "local", 2) for array in selected[1:twins]]

    later = [cover, cover_count, weights]
    moves, high, cover, cover_count, weights = call(
        fetch_kernel,
        [
            shaped((DEPTH, ocean_cells), jnp.bfloat16),
            shaped(ocean_map.shape, ocean_map.dtype),
            pltpu.SMEM(cover.shape, cover.dtype),
            pltpu.SMEM(cover_count.shape, cover_count.dtype),
            shaped(weights.shape, weights.dtype),
        ],
        "ah" + "h" * len(later),
        [scratch(ocean_map), pltpu.SemaphoreType.DMA((len(later) + 1,))],
        out_memory="vvssv",
        moved=3_000_000,
    )(ordered, *stay(ocean_map, *later))

    if piece == LANES:
        coupled = lax.all_to_all(ordered, everyone, split_axis=0, concat_axis=0, tiled=True)
    else:
        outgoing = ordered.reshape(blocks, rows, LANES)[:, :fields].transpose(1, 0, 2).reshape(fields, devices, piece)
        coupled = lax.all_to_all(outgoing, everyone, split_axis=1, concat_axis=1, tiled=True)
        coupled = coupled.reshape(fields, blocks, LANES).transpose(1, 0, 2)
        coupled = jnp.pad(coupled, ((0, 0), (0, rows - fields), (0, 0))).reshape(messages)

    sent = shaped((twins, cap * kinds, ROWS, LANES), jnp.bfloat16)
    tables = shaped((twins,) + table, jnp.bfloat16)
    owns = shaped((twins, cap, ROWS, LANES), jnp.float32)
    work = 2 * twins * cap * table[0] * DEPTH * near_count * LANES
    *outer, tables, owns = call(
        functools.partial(outer_kernel, twins, near_count, fields),
        [sent] * (aparts - 1) + [tables, owns],
        "av" + "v" * twins + "v" * len(hots),
        flops=work * (aparts - 1),
    )(moves, coupled, *selected, *hots)
    source = [send(array, "local", 1 + at) for at, array in enumerate(outer)]
    inner = call(
        functools.partial(inner_kernel, near_count, fields),
        sent,
        "vv" + "v" * twins,
        flops=work,
        moved=4_000_000,
    )(tables, owns, *selected)
    source = [inner] + source

    share = ocean_cells // region_count
    packed = share * 2 == LANES
    out_shape = (region_count, ROWS // 2, LANES) if packed else (fields, ocean_cells)
    leaving = call(
        functools.partial(remap_kernel, packed, fields),
        shaped(out_shape, jnp.float32),
        "ssvvv" + "v" * aparts,
        [pltpu.VMEM((local_count, cap * kinds, ROWS, LANES), jnp.bfloat16)],
    )(cover, cover_count, weights, moves, high, *source)
    if packed:
        landed = swap(leaving, "region")
        return call(land_kernel, shaped((fields, ocean_cells), jnp.float32), "v")(landed)
    leaving = leaving.reshape(fields, region_count, share)
    landed = lax.all_to_all(leaving, "region", split_axis=1, concat_axis=1, tiled=True)
    return landed.reshape(fields, ocean_cells)


def solution(mesh):
    return jax.shard_map(
        shards,
        mesh=mesh,
        in_specs=(
            P(None, ("region", "local")),
            P(("region", "local"), None),
            P(None, ("region", "local")),
            P(None, ("region", "local")),
            P(None, ("region", "local")),
            P(("region", "local"), None, None),
            P(("region", "local"), None),
            P(("region", "local")),
            P(("region", "local"), None, None, None, None),
            P(("region", "local"), None),
        ),
        out_specs=P(None, ("region", "local")),
        check_vma=False,
    )
```

```python
import functools

import jax
import jax.numpy as jnp
from jax import lax
from jax.experimental import pallas as pl
from jax.experimental.pallas import tpu as pltpu
from jax.sharding import PartitionSpec as P

ROWS = 16
HALF = 8
LANES = 128
DEPTH = 256
PER_ROW = DEPTH // LANES
STEP = 512
WIDTH = 256
VMEM_LIMIT = 40 * 1024 * 1024


def one_hot(index):
    row = lax.broadcasted_iota(jnp.int32, (DEPTH, index.shape[1]), 0).astype(jnp.bfloat16)
    low = (index & (DEPTH - 1)).astype(jnp.bfloat16)
    return jnp.where(row == low, jnp.bfloat16(1), jnp.bfloat16(0))


def choose(found, high, height):
    high = jnp.broadcast_to(high, (height, found.shape[1]))
    result = found[:height]
    for part in range(1, found.shape[0] // height):
        result = jnp.where(high == part, found[part * height : (part + 1) * height], result)
    return result


def lookup(table, index):
    results = []
    for at in range(0, index.shape[1], WIDTH):
        here = index[:, at : at + WIDTH]
        found = jnp.dot(table, one_hot(here), preferred_element_type=jnp.float32).astype(jnp.bfloat16)
        results.append(choose(found, (here // DEPTH).astype(jnp.int16), ROWS).astype(jnp.float32))
    return jnp.concatenate(results, axis=1)


def lookup_dense(table, index, parts):
    results = []
    for at in range(0, index.shape[1], WIDTH):
        here = index[:, at : at + WIDTH]
        found = jnp.dot(table, one_hot(here), preferred_element_type=jnp.float32)
        high = here // DEPTH
        upper = choose(found[: HALF * parts], high, HALF)
        lower = choose(found[HALF * parts :], high // 2, HALF)
        odd = jnp.broadcast_to(high % 2, lower.shape)
        results.append(jnp.concatenate([upper, jnp.where(odd == 1, pltpu.roll(lower, HALF // 2, 0), lower)], axis=0))
    return jnp.concatenate(results, axis=1)


def copies_of(sources, targets, sems, first=0):
    return [
        pltpu.make_async_copy(source, target, sems.at[first + at])
        for at, (source, target) in enumerate(zip(sources, targets))
    ]


def message_rows(fields, twins):
    return 2 * fields if twins == 2 else ROWS


def order_kernel(twins, map_hbm, flux_hbm, out_hbm, map_ref, flux_ref, out_ref, table, sems):
    fields, cells = flux_ref.shape
    steps = cells // STEP
    spans = [pl.ds(at, cells // 4) for at in range(0, cells, cells // 4)]
    needed = copies_of([flux_hbm.at[:, span] for span in spans], [flux_ref.at[:, span] for span in spans], sems)
    needed += copies_of((map_hbm,), (map_ref,), sems, 4)
    for copy in needed:
        copy.start()
    for copy in needed:
        copy.wait()
    parts, rest = cells // DEPTH, fields - HALF
    for part in range(parts):
        columns = slice(part * DEPTH, (part + 1) * DEPTH)
        table[part * HALF : (part + 1) * HALF] = flux_ref[:HALF, columns]
        table[parts * HALF + part * rest : parts * HALF + (part + 1) * rest] = flux_ref[HALF:, columns]
    rows = message_rows(fields, twins)
    written = []
    for step in range(steps):
        found = lookup_dense(table[...], map_ref[:, step * STEP : (step + 1) * STEP], parts)
        pieces = [found[:, at : at + LANES] for at in range(0, STEP, LANES)]
        if twins == 2:
            pieces = [
                jnp.concatenate([pieces[at][:fields], pieces[at ^ 2][:fields]], axis=0) for at in range(len(pieces))
            ]
        for at, piece in enumerate(pieces):
            first = (step * len(pieces) + at) * rows
            out_ref[first : first + rows] = piece.astype(jnp.bfloat16)
        span = pl.ds(step * len(pieces) * rows, len(pieces) * rows)
        written.append(pltpu.make_async_copy(out_ref.at[span], out_hbm.at[span], sems.at[5 + step]))
        written[-1].start()
    for copy in written:
        copy.wait()


def select_kernel(after_ref, list_hbm, near_hbm, x_hbm, y_hbm, *refs):
    selected, (list_ref, near_ref, x_ref, y_ref, sems) = refs[:-5], refs[-5:]
    copies = copies_of((list_hbm, near_hbm, x_hbm, y_hbm), (list_ref, near_ref, x_ref, y_ref), sems)
    for copy in copies:
        copy.start()
    for copy in copies:
        copy.wait()
    me = lax.axis_index("local")
    cap = list_ref.shape[2]
    count = list_ref.shape[1] // len(selected)
    near_count = near_ref.shape[0]
    for twin, stencil_ref in reversed(list(enumerate(selected))):
        for at in range(count * cap):
            block = list_ref[0, me ^ (2 * twin) ^ (at // cap), at % cap]
            columns = pl.ds(pl.multiple_of(block * LANES, LANES), LANES)
            stencil_ref[at, :near_count] = near_ref[:, columns].astype(jnp.float32)
            stencil_ref[at, near_count : 2 * near_count] = x_ref[:, columns]
            stencil_ref[at, 2 * near_count : 3 * near_count] = y_ref[:, columns]
            rest = (ROWS - 3 * near_count, LANES)
            stencil_ref[at, 3 * near_count :] = jnp.broadcast_to(block, rest).astype(jnp.float32)


def fetch_kernel(after_ref, map_hbm, *refs):
    count = (len(refs) - 4) // 2
    sources, (moves_ref, high_ref), targets, (map_ref, sems) = refs[:count], refs[count : count + 2], refs[count + 2 : -2], refs[-2:]
    (needed,) = copies_of((map_hbm,), (map_ref,), sems, count)
    others = copies_of(sources, targets, sems)
    for copy in [needed] + others:
        copy.start()
    needed.wait()
    moves_ref[...] = one_hot(map_ref[...])
    high_ref[...] = map_ref[...] // DEPTH
    for copy in others:
        copy.wait()


def rebuild(near_count, table, stencil, own, shift):
    near = stencil[:near_count].astype(jnp.int32)
    index = jnp.concatenate([near[j : j + 1] for j in range(near_count)], axis=1)
    found = lookup(table, index)
    upper = lower = own
    slope_x = slope_y = jnp.zeros_like(own)
    for j in range(near_count):
        value = found[:, j * LANES : (j + 1) * LANES]
        change = value - own
        slope_x += stencil[near_count + j : near_count + j + 1] * change
        slope_y += stencil[2 * near_count + j : 2 * near_count + j + 1] * change
        upper, lower = jnp.maximum(upper, value), jnp.minimum(lower, value)
    steep = jnp.abs(slope_x) + jnp.abs(slope_y)
    factor = jnp.minimum(1.0, (upper - lower) / jnp.maximum(steep, 1.0))
    results = [own, factor * slope_x, factor * slope_y]
    if shift:
        spare = jnp.zeros((shift, LANES), jnp.float32)
        results = [jnp.concatenate([result[shift:], spare], axis=0) for result in results]
    return results


def own_cells(near_count, table, stencil_ref):
    slots = stencil_ref.shape[0]
    tile = (ROWS, DEPTH)
    column = lax.broadcasted_iota(jnp.int32, tile, 1) - lax.broadcasted_iota(jnp.int32, tile, 0)
    blocks = [stencil_ref[at, 3 * near_count : 3 * near_count + 1].astype(jnp.int32) for at in range(slots)]
    picks = [
        jnp.where(jnp.concatenate([block // PER_ROW * ROWS] * PER_ROW, axis=1) == column, 1.0, 0.0) for block in blocks
    ]
    found = jnp.dot(
        jnp.concatenate(picks, axis=0).astype(jnp.bfloat16), table, preferred_element_type=jnp.float32
    )
    owns = []
    for at, block in enumerate(blocks):
        rows = found[at * ROWS : (at + 1) * ROWS]
        odd = jnp.broadcast_to(block % PER_ROW, (ROWS, LANES))
        owns.append(jnp.where(odd == 1, rows[:, LANES:], rows[:, :LANES]))
    return owns


def outer_kernel(twins, near_count, fields, after_ref, cells_ref, *refs):
    selected, refs = refs[:twins], refs[twins:]
    out_refs, (tables, owns) = refs[:-2], refs[-2:]
    cap = owns.shape[1]
    rows = message_rows(fields, twins)
    for twin in range(twins):
        for block in range(tables.shape[1] // ROWS * PER_ROW):
            part, column = block // PER_ROW, block % PER_ROW * LANES
            first = block * rows + HALF * twin
            tables[twin, part * ROWS : (part + 1) * ROWS, column : column + LANES] = cells_ref[first : first + ROWS]
    for twin, stencil_ref in enumerate(selected):
        for at, own in enumerate(own_cells(near_count, tables[twin], stencil_ref)):
            if at < cap:
                owns[twin, at] = own
                continue
            shift = twin * (fields - HALF)
            results = rebuild(near_count, tables[twin], stencil_ref[at], own, shift)
            for kind, result in enumerate(results):
                out_refs[at // cap - 1][twin, at % cap * len(results) + kind] = result.astype(jnp.bfloat16)


def inner_kernel(near_count, fields, tables, owns, *refs):
    selected, out_ref = refs[:-1], refs[-1]
    for twin, stencil_ref in enumerate(selected):
        for at in range(owns.shape[1]):
            own = owns[twin, at]
            shift = twin * (fields - HALF)
            results = rebuild(near_count, tables[twin], stencil_ref[at], own, shift)
            for kind, result in enumerate(results):
                out_ref[twin, at * len(results) + kind] = result.astype(jnp.bfloat16)


def remap_kernel(packed, fields, cover_ref, count_ref, weight_ref, moves_ref, high_ref, *refs):
    received, (out_ref, source_ref) = refs[:-2], refs[-2:]
    me = lax.axis_index("local")
    ocean_blocks, slots, kinds = weight_ref.shape[:3]
    cap = source_ref.shape[1] // kinds
    for apart, piece_ref in enumerate(received):
        for twin in range(piece_ref.shape[0]):
            source_ref[me ^ apart ^ (2 * twin)] = piece_ref[twin]
    results = []
    for block in range(ocean_blocks):
        values, weights = [], []
        for slot in range(slots):
            at = cover_ref[block, slot]
            live = slot < count_ref[block]
            for kind in range(kinds):
                value = source_ref[at // cap, at % cap * kinds + kind]
                values.append(jnp.where(live, value, jnp.zeros_like(value)))
                weights.append(weight_ref[block, slot, kind])
        product = lax.dot_general(
            jnp.concatenate(values, axis=1),
            jnp.concatenate(weights, axis=1),
            (((1,), (1,)), ((), ())),
            preferred_element_type=jnp.float32,
        )
        results.append(product)
    remapped = jnp.concatenate(results, axis=1)
    cells = remapped.shape[1]
    coarse = remapped.astype(jnp.bfloat16)
    fine = (remapped - coarse.astype(jnp.float32)).astype(jnp.bfloat16)
    table = [part[:, at : at + DEPTH] for at in range(0, cells, DEPTH) for part in (coarse, fine)]
    moved = jnp.dot(jnp.concatenate(table, axis=0), moves_ref[...], preferred_element_type=jnp.float32)
    moved = choose(moved, high_ref[...], 2 * ROWS)
    moved = moved[:ROWS] + moved[ROWS:]
    if not packed:
        out_ref[...] = moved[:fields]
        return
    half = fields // 2
    rows = out_ref.shape[1]
    listed = listing(out_ref.shape[0])
    side = lax.broadcasted_iota(jnp.int32, (rows, LANES), 1) < LANES // 2
    for pair in range(cells // LANES):
        columns = moved[:, pair * LANES : (pair + 1) * LANES]
        first, second = columns[:rows], columns[half : half + rows]
        out_ref[listed.index(2 * pair)] = jnp.where(side, first, pltpu.roll(second, LANES // 2, 1))
        out_ref[listed.index(2 * pair + 1)] = jnp.where(side, pltpu.roll(first, LANES // 2, 1), second)


def land_kernel(landed_ref, out_ref):
    count = landed_ref.shape[0]
    listed = listing(count)
    half = out_ref.shape[0] // 2
    side = lax.broadcasted_iota(jnp.int32, (half, LANES), 1) < LANES // 2
    for pair in range(count // 2):
        even, odd = landed_ref[listed.index(2 * pair), :half], landed_ref[listed.index(2 * pair + 1), :half]
        columns = pl.ds(pair * LANES, LANES)
        out_ref[:half, columns] = jnp.where(side, even, pltpu.roll(odd, LANES // 2, 1))
        out_ref[half:, columns] = jnp.where(side, pltpu.roll(even, LANES // 2, 1), odd)


def send(array, axis, apart):
    return lax.ppermute(array, axis, [(at, at ^ apart) for at in range(lax.axis_size(axis))])


def listing(count):
    return sorted(range(count), key=lambda at: (abs(2 * at - count + 1), -at))


def swap(pieces, axis):
    groups = [listing(lax.axis_size(axis))]
    pieces = pieces.transpose(1, 0, 2)
    swapped = lax.all_to_all(pieces, axis, split_axis=1, concat_axis=1, axis_index_groups=groups, tiled=True)
    return swapped.transpose(1, 0, 2)


SPACES = {"s": pltpu.SMEM, "v": pltpu.VMEM, "h": pltpu.HBM, "a": pl.ANY}


def call(kernel, outs, memories, scratch=(), out_memory="v", flops=0, moved=0):
    if isinstance(outs, list):
        out_specs = [pl.BlockSpec(memory_space=SPACES[kind]) for kind in (out_memory * len(outs))[: len(outs)]]
    else:
        out_specs = pl.BlockSpec(memory_space=SPACES[out_memory])
    return pl.pallas_call(
        kernel,
        out_shape=outs,
        in_specs=[pl.BlockSpec(memory_space=SPACES[kind]) for kind in memories],
        out_specs=out_specs,
        scratch_shapes=list(scratch),
        cost_estimate=pl.CostEstimate(flops=flops, bytes_accessed=moved, transcendentals=0),
        compiler_params=pltpu.CompilerParams(vmem_limit_bytes=VMEM_LIMIT),
    )


def shards(
    atm_flux,
    cell_map,
    neighbours,
    coef_x,
    coef_y,
    send_list,
    cover,
    cover_count,
    weights,
    ocean_map,
):
    fields, cells = atm_flux.shape
    region_count = lax.axis_size("region")
    local_count = lax.axis_size("local")
    everyone = ("region", "local")
    devices = region_count * local_count
    piece = cells // devices
    blocks = cells // LANES
    table = (cells // DEPTH * ROWS, DEPTH)
    shaped = jax.ShapeDtypeStruct
    twins = 2 if local_count == 4 and piece == LANES else 1
    cap = send_list.shape[2]
    aparts = local_count // twins
    near_count = neighbours.shape[0]
    kinds = weights.shape[2]
    ocean_cells = ocean_map.shape[1]

    def stay(*arrays):
        return [pltpu.with_memory_space_constraint(array, pltpu.HBM) for array in arrays]

    def scratch(array):
        return pltpu.VMEM(array.shape, array.dtype)

    rows = message_rows(fields, twins)
    messages = (blocks * rows, LANES)
    ordered = call(
        functools.partial(order_kernel, twins),
        shaped(messages, jnp.bfloat16),
        "hh",
        [
            scratch(cell_map),
            scratch(atm_flux),
            pltpu.VMEM(messages, jnp.bfloat16),
            pltpu.VMEM((cells // DEPTH * fields, DEPTH), jnp.bfloat16),
            pltpu.SemaphoreType.DMA((cells // STEP + 5,)),
        ],
        out_memory="h",
    )(*stay(cell_map, atm_flux))

    stencil = shaped((aparts * cap, ROWS, LANES), jnp.float32)
    selected = call(
        select_kernel,
        [stencil] * twins,
        "ahhhh",
        [
            pltpu.SMEM(send_list.shape, send_list.dtype),
            scratch(neighbours),
            scratch(coef_x),
            scratch(coef_y),
            pltpu.SemaphoreType.DMA((4,)),
        ],
        moved=3_000_000,
    )(ordered, *stay(send_list, neighbours, coef_x, coef_y))
    selected = [selected[0]] + [send(array, "local", 2) for array in selected[1:]]

    later = [cover, cover_count, weights]
    moves, high, cover, cover_count, weights = call(
        fetch_kernel,
        [
            shaped((DEPTH, ocean_cells), jnp.bfloat16),
            shaped(ocean_map.shape, ocean_map.dtype),
            pltpu.SMEM(cover.shape, cover.dtype),
            pltpu.SMEM(cover_count.shape, cover_count.dtype),
            shaped(weights.shape, weights.dtype),
        ],
        "ah" + "h" * len(later),
        [scratch(ocean_map), pltpu.SemaphoreType.DMA((len(later) + 1,))],
        out_memory="vvssv",
        moved=3_000_000,
    )(ordered, *stay(ocean_map, *later))

    if piece == LANES:
        coupled = lax.all_to_all(ordered, everyone, split_axis=0, concat_axis=0, tiled=True)
    else:
        outgoing = ordered.reshape(blocks, rows, LANES)[:, :fields].transpose(1, 0, 2).reshape(fields, devices, piece)
        coupled = lax.all_to_all(outgoing, everyone, split_axis=1, concat_axis=1, tiled=True)
        coupled = coupled.reshape(fields, blocks, LANES).transpose(1, 0, 2)
        coupled = jnp.pad(coupled, ((0, 0), (0, rows - fields), (0, 0))).reshape(messages)

    sent = shaped((twins, cap * kinds, ROWS, LANES), jnp.bfloat16)
    tables = shaped((twins,) + table, jnp.bfloat16)
    owns = shaped((twins, cap, ROWS, LANES), jnp.float32)
    work = 2 * twins * cap * table[0] * DEPTH * near_count * LANES
    *outer, tables, owns = call(
        functools.partial(outer_kernel, twins, near_count, fields),
        [sent] * (aparts - 1) + [tables, owns],
        "av" + "v" * twins,
        flops=work * (aparts - 1),
    )(moves, coupled, *selected)
    source = [send(array, "local", 1 + at) for at, array in enumerate(outer)]
    inner = call(
        functools.partial(inner_kernel, near_count, fields),
        sent,
        "vv" + "v" * twins,
        flops=work,
        moved=4_000_000,
    )(tables, owns, *selected)
    source = [inner] + source

    share = ocean_cells // region_count
    packed = share * 2 == LANES
    out_shape = (region_count, ROWS // 2, LANES) if packed else (fields, ocean_cells)
    leaving = call(
        functools.partial(remap_kernel, packed, fields),
        shaped(out_shape, jnp.float32),
        "ssvvv" + "v" * aparts,
        [pltpu.VMEM((local_count, cap * kinds, ROWS, LANES), jnp.bfloat16)],
    )(cover, cover_count, weights, moves, high, *source)
    if packed:
        landed = swap(leaving, "region")
        return call(land_kernel, shaped((fields, ocean_cells), jnp.float32), "v")(landed)
    leaving = leaving.reshape(fields, region_count, share)
    landed = lax.all_to_all(leaving, "region", split_axis=1, concat_axis=1, tiled=True)
    return landed.reshape(fields, ocean_cells)


def solution(mesh):
    return jax.shard_map(
        shards,
        mesh=mesh,
        in_specs=(
            P(None, ("region", "local")),
            P(("region", "local"), None),
            P(None, ("region", "local")),
            P(None, ("region", "local")),
            P(None, ("region", "local")),
            P(("region", "local"), None, None),
            P(("region", "local"), None),
            P(("region", "local")),
            P(("region", "local"), None, None, None, None),
            P(("region", "local"), None),
        ),
        out_specs=P(None, ("region", "local")),
        check_vma=False,
    )
```

```python
import functools

import jax
import jax.numpy as jnp
from jax import lax
from jax.experimental import pallas as pl
from jax.experimental.pallas import tpu as pltpu
from jax.sharding import PartitionSpec as P

ROWS = 16
HALF = 8
LANES = 128
DEPTH = 256
PER_ROW = DEPTH // LANES
STEP = 512
WIDTH = 256
VMEM_LIMIT = 40 * 1024 * 1024


def one_hot(index):
    row = lax.broadcasted_iota(jnp.int32, (DEPTH, index.shape[1]), 0).astype(jnp.bfloat16)
    low = (index & (DEPTH - 1)).astype(jnp.bfloat16)
    return jnp.where(row == low, jnp.bfloat16(1), jnp.bfloat16(0))


def choose(found, high, height):
    high = jnp.broadcast_to(high, (height, found.shape[1]))
    result = found[:height]
    for part in range(1, found.shape[0] // height):
        result = jnp.where(high == part, found[part * height : (part + 1) * height], result)
    return result


def lookup(table, index):
    results = []
    for at in range(0, index.shape[1], WIDTH):
        here = index[:, at : at + WIDTH]
        found = jnp.dot(table, one_hot(here), preferred_element_type=jnp.float32)
        results.append(choose(found, here // DEPTH, ROWS))
    return jnp.concatenate(results, axis=1)


def lookup_dense(table, index, parts):
    results = []
    for at in range(0, index.shape[1], WIDTH):
        here = index[:, at : at + WIDTH]
        found = jnp.dot(table, one_hot(here), preferred_element_type=jnp.float32)
        high = here // DEPTH
        upper = choose(found[: HALF * parts], high, HALF)
        lower = choose(found[HALF * parts :], high // 2, HALF)
        odd = jnp.broadcast_to(high % 2, lower.shape)
        results.append(jnp.concatenate([upper, jnp.where(odd == 1, pltpu.roll(lower, HALF // 2, 0), lower)], axis=0))
    return jnp.concatenate(results, axis=1)


def copies_of(sources, targets, sems, first=0):
    return [
        pltpu.make_async_copy(source, target, sems.at[first + at])
        for at, (source, target) in enumerate(zip(sources, targets))
    ]


def message_rows(fields, twins):
    return 2 * fields if twins == 2 else ROWS


def place_of(device, twins):
    return device ^ 1 if twins == 2 else device


def order_kernel(twins, map_hbm, flux_hbm, out_hbm, map_ref, flux_ref, out_ref, table, sems):
    fields, cells = flux_ref.shape
    steps = cells // STEP
    spans = [pl.ds(at, cells // 4) for at in range(0, cells, cells // 4)]
    needed = copies_of([flux_hbm.at[:, span] for span in spans], [flux_ref.at[:, span] for span in spans], sems)
    needed += copies_of((map_hbm,), (map_ref,), sems, 4)
    for copy in needed:
        copy.start()
    for copy in needed:
        copy.wait()
    parts, rest = cells // DEPTH, fields - HALF
    for part in range(parts):
        columns = slice(part * DEPTH, (part + 1) * DEPTH)
        table[part * HALF : (part + 1) * HALF] = flux_ref[:HALF, columns]
        table[parts * HALF + part * rest : parts * HALF + (part + 1) * rest] = flux_ref[HALF:, columns]
    rows = message_rows(fields, twins)
    written = []
    for step in range(steps):
        found = lookup_dense(table[...], map_ref[:, step * STEP : (step + 1) * STEP], parts)
        pieces = [found[:, at : at + LANES] for at in range(0, STEP, LANES)]
        if twins == 2:
            pieces = [
                jnp.concatenate([pieces[at][:fields], pieces[at ^ 2][:fields]], axis=0) for at in range(len(pieces))
            ]
        for at, piece in enumerate(pieces):
            first = place_of(step * len(pieces) + at, twins) * rows
            out_ref[first : first + rows] = piece.astype(jnp.bfloat16)
        span = pl.ds(step * len(pieces) * rows, len(pieces) * rows)
        written.append(pltpu.make_async_copy(out_ref.at[span], out_hbm.at[span], sems.at[5 + step]))
        written[-1].start()
    for copy in written:
        copy.wait()


def select_kernel(after_ref, list_hbm, near_hbm, x_hbm, y_hbm, *refs):
    selected, (list_ref, near_ref, x_ref, y_ref, sems) = refs[:-5], refs[-5:]
    copies = copies_of((list_hbm, near_hbm, x_hbm, y_hbm), (list_ref, near_ref, x_ref, y_ref), sems)
    for copy in copies:
        copy.start()
    for copy in copies:
        copy.wait()
    me = lax.axis_index("local")
    cap = list_ref.shape[2]
    count = list_ref.shape[1] // len(selected)
    near_count = near_ref.shape[0]
    for twin, stencil_ref in reversed(list(enumerate(selected))):
        for at in range(count * cap):
            block = list_ref[0, me ^ (2 * twin) ^ (at // cap), at % cap]
            columns = pl.ds(pl.multiple_of(block * LANES, LANES), LANES)
            stencil_ref[at, :near_count] = near_ref[:, columns].astype(jnp.float32)
            stencil_ref[at, near_count : 2 * near_count] = x_ref[:, columns]
            stencil_ref[at, 2 * near_count : 3 * near_count] = y_ref[:, columns]
            rest = (ROWS - 3 * near_count, LANES)
            stencil_ref[at, 3 * near_count :] = jnp.broadcast_to(block, rest).astype(jnp.float32)


def fetch_kernel(after_ref, map_hbm, *refs):
    count = (len(refs) - 4) // 2
    sources, (moves_ref, high_ref), targets, (map_ref, sems) = refs[:count], refs[count : count + 2], refs[count + 2 : -2], refs[-2:]
    (needed,) = copies_of((map_hbm,), (map_ref,), sems, count)
    others = copies_of(sources, targets, sems)
    for copy in [needed] + others:
        copy.start()
    needed.wait()
    moves_ref[...] = one_hot(map_ref[...])
    high_ref[...] = map_ref[...] // DEPTH
    for copy in others:
        copy.wait()


def rebuild(near_count, table, stencil, own, shift):
    near = stencil[:near_count].astype(jnp.int32)
    index = jnp.concatenate([near[j : j + 1] for j in range(near_count)], axis=1)
    found = lookup(table, index)
    upper = lower = own
    slope_x = slope_y = jnp.zeros_like(own)
    for j in range(near_count):
        value = found[:, j * LANES : (j + 1) * LANES]
        change = value - own
        slope_x += stencil[near_count + j : near_count + j + 1] * change
        slope_y += stencil[2 * near_count + j : 2 * near_count + j + 1] * change
        upper, lower = jnp.maximum(upper, value), jnp.minimum(lower, value)
    steep = jnp.abs(slope_x) + jnp.abs(slope_y)
    factor = jnp.minimum(1.0, (upper - lower) / jnp.maximum(steep, 1.0))
    results = [own, factor * slope_x, factor * slope_y]
    if shift:
        spare = jnp.zeros((shift, LANES), jnp.float32)
        results = [jnp.concatenate([result[shift:], spare], axis=0) for result in results]
    return results


def own_cells(near_count, table, stencil_ref):
    slots = stencil_ref.shape[0]
    tile = (ROWS, DEPTH)
    column = lax.broadcasted_iota(jnp.int32, tile, 1) - lax.broadcasted_iota(jnp.int32, tile, 0)
    blocks = [stencil_ref[at, 3 * near_count : 3 * near_count + 1].astype(jnp.int32) for at in range(slots)]
    picks = [
        jnp.where(jnp.concatenate([block // PER_ROW * ROWS] * PER_ROW, axis=1) == column, 1.0, 0.0) for block in blocks
    ]
    found = jnp.dot(
        jnp.concatenate(picks, axis=0).astype(jnp.bfloat16), table, preferred_element_type=jnp.float32
    )
    owns = []
    for at, block in enumerate(blocks):
        rows = found[at * ROWS : (at + 1) * ROWS]
        odd = jnp.broadcast_to(block % PER_ROW, (ROWS, LANES))
        owns.append(jnp.where(odd == 1, rows[:, LANES:], rows[:, :LANES]))
    return owns


def outer_kernel(twins, near_count, fields, after_ref, cells_ref, *refs):
    selected, refs = refs[:twins], refs[twins:]
    out_refs, (tables, owns) = refs[:-2], refs[-2:]
    cap = owns.shape[1]
    rows = message_rows(fields, twins)
    for twin in range(twins):
        for block in range(tables.shape[1] // ROWS * PER_ROW):
            part, column = block // PER_ROW, block % PER_ROW * LANES
            first = place_of(block, twins) * rows + HALF * twin
            tables[twin, part * ROWS : (part + 1) * ROWS, column : column + LANES] = cells_ref[first : first + ROWS]
    for twin, stencil_ref in enumerate(selected):
        for at, own in enumerate(own_cells(near_count, tables[twin], stencil_ref)):
            if at < cap:
                owns[twin, at] = own
                continue
            shift = twin * (fields - HALF)
            results = rebuild(near_count, tables[twin], stencil_ref[at], own, shift)
            for kind, result in enumerate(results):
                out_refs[at // cap - 1][twin, at % cap * len(results) + kind] = result.astype(jnp.bfloat16)


def inner_kernel(near_count, fields, tables, owns, *refs):
    selected, out_ref = refs[:-1], refs[-1]
    for twin, stencil_ref in enumerate(selected):
        for at in range(owns.shape[1]):
            own = owns[twin, at]
            shift = twin * (fields - HALF)
            results = rebuild(near_count, tables[twin], stencil_ref[at], own, shift)
            for kind, result in enumerate(results):
                out_ref[twin, at * len(results) + kind] = result.astype(jnp.bfloat16)


def remap_kernel(packed, fields, cover_ref, count_ref, weight_ref, moves_ref, high_ref, *refs):
    received, (out_ref, source_ref) = refs[:-2], refs[-2:]
    me = lax.axis_index("local")
    ocean_blocks, slots, kinds = weight_ref.shape[:3]
    cap = source_ref.shape[1] // kinds
    for apart, piece_ref in enumerate(received):
        for twin in range(piece_ref.shape[0]):
            source_ref[me ^ apart ^ (2 * twin)] = piece_ref[twin]
    results = []
    for block in range(ocean_blocks):
        values, weights = [], []
        for slot in range(slots):
            at = cover_ref[block, slot]
            live = slot < count_ref[block]
            for kind in range(kinds):
                value = source_ref[at // cap, at % cap * kinds + kind]
                values.append(jnp.where(live, value, jnp.zeros_like(value)))
                weights.append(weight_ref[block, slot, kind])
        product = lax.dot_general(
            jnp.concatenate(values, axis=1),
            jnp.concatenate(weights, axis=1),
            (((1,), (1,)), ((), ())),
            preferred_element_type=jnp.float32,
        )
        results.append(product)
    remapped = jnp.concatenate(results, axis=1)
    cells = remapped.shape[1]
    coarse = remapped.astype(jnp.bfloat16)
    fine = (remapped - coarse.astype(jnp.float32)).astype(jnp.bfloat16)
    table = [part[:, at : at + DEPTH] for at in range(0, cells, DEPTH) for part in (coarse, fine)]
    moved = jnp.dot(jnp.concatenate(table, axis=0), moves_ref[...], preferred_element_type=jnp.float32)
    moved = choose(moved, high_ref[...], 2 * ROWS)
    moved = moved[:ROWS] + moved[ROWS:]
    if not packed:
        out_ref[...] = moved[:fields]
        return
    half = fields // 2
    rows = out_ref.shape[1]
    listed = listing(out_ref.shape[0])
    side = lax.broadcasted_iota(jnp.int32, (rows, LANES), 1) < LANES // 2
    for pair in range(cells // LANES):
        columns = moved[:, pair * LANES : (pair + 1) * LANES]
        first, second = columns[:rows], columns[half : half + rows]
        out_ref[listed.index(2 * pair)] = jnp.where(side, first, pltpu.roll(second, LANES // 2, 1))
        out_ref[listed.index(2 * pair + 1)] = jnp.where(side, pltpu.roll(first, LANES // 2, 1), second)


def land_kernel(landed_ref, out_ref):
    count = landed_ref.shape[0]
    listed = listing(count)
    half = out_ref.shape[0] // 2
    side = lax.broadcasted_iota(jnp.int32, (half, LANES), 1) < LANES // 2
    for pair in range(count // 2):
        even, odd = landed_ref[listed.index(2 * pair), :half], landed_ref[listed.index(2 * pair + 1), :half]
        columns = pl.ds(pair * LANES, LANES)
        out_ref[:half, columns] = jnp.where(side, even, pltpu.roll(odd, LANES // 2, 1))
        out_ref[half:, columns] = jnp.where(side, pltpu.roll(even, LANES // 2, 1), odd)


def send(array, axis, apart):
    return lax.ppermute(array, axis, [(at, at ^ apart) for at in range(lax.axis_size(axis))])


def listing(count):
    return sorted(range(count), key=lambda at: (abs(2 * at - count + 1), -at))


def swap(pieces, axis):
    groups = [listing(lax.axis_size(axis))]
    pieces = pieces.transpose(1, 0, 2)
    swapped = lax.all_to_all(pieces, axis, split_axis=1, concat_axis=1, axis_index_groups=groups, tiled=True)
    return swapped.transpose(1, 0, 2)


SPACES = {"s": pltpu.SMEM, "v": pltpu.VMEM, "h": pltpu.HBM, "a": pl.ANY}


def call(kernel, outs, memories, scratch=(), out_memory="v", flops=0, moved=0):
    if isinstance(outs, list):
        out_specs = [pl.BlockSpec(memory_space=SPACES[kind]) for kind in (out_memory * len(outs))[: len(outs)]]
    else:
        out_specs = pl.BlockSpec(memory_space=SPACES[out_memory])
    return pl.pallas_call(
        kernel,
        out_shape=outs,
        in_specs=[pl.BlockSpec(memory_space=SPACES[kind]) for kind in memories],
        out_specs=out_specs,
        scratch_shapes=list(scratch),
        cost_estimate=pl.CostEstimate(flops=flops, bytes_accessed=moved, transcendentals=0),
        compiler_params=pltpu.CompilerParams(vmem_limit_bytes=VMEM_LIMIT),
    )


def shards(
    atm_flux,
    cell_map,
    neighbours,
    coef_x,
    coef_y,
    send_list,
    cover,
    cover_count,
    weights,
    ocean_map,
):
    fields, cells = atm_flux.shape
    region_count = lax.axis_size("region")
    local_count = lax.axis_size("local")
    everyone = ("region", "local")
    devices = region_count * local_count
    piece = cells // devices
    blocks = cells // LANES
    table = (cells // DEPTH * ROWS, DEPTH)
    shaped = jax.ShapeDtypeStruct
    twins = 2 if local_count == 4 and piece == LANES else 1
    cap = send_list.shape[2]
    aparts = local_count // twins
    near_count = neighbours.shape[0]
    kinds = weights.shape[2]
    ocean_cells = ocean_map.shape[1]

    def stay(*arrays):
        return [pltpu.with_memory_space_constraint(array, pltpu.HBM) for array in arrays]

    def scratch(array):
        return pltpu.VMEM(array.shape, array.dtype)

    rows = message_rows(fields, twins)
    messages = (blocks * rows, LANES)
    ordered = call(
        functools.partial(order_kernel, twins),
        shaped(messages, jnp.bfloat16),
        "hh",
        [
            scratch(cell_map),
            scratch(atm_flux),
            pltpu.VMEM(messages, jnp.bfloat16),
            pltpu.VMEM((cells // DEPTH * fields, DEPTH), jnp.bfloat16),
            pltpu.SemaphoreType.DMA((cells // STEP + 5,)),
        ],
        out_memory="h",
    )(*stay(cell_map, atm_flux))

    stencil = shaped((aparts * cap, ROWS, LANES), jnp.float32)
    selected = call(
        select_kernel,
        [stencil] * twins,
        "ahhhh",
        [
            pltpu.SMEM(send_list.shape, send_list.dtype),
            scratch(neighbours),
            scratch(coef_x),
            scratch(coef_y),
            pltpu.SemaphoreType.DMA((4,)),
        ],
        moved=3_000_000,
    )(ordered, *stay(send_list, neighbours, coef_x, coef_y))
    selected = [selected[0]] + [send(array, "local", 2) for array in selected[1:]]

    later = [cover, cover_count, weights]
    moves, high, cover, cover_count, weights = call(
        fetch_kernel,
        [
            shaped((DEPTH, ocean_cells), jnp.bfloat16),
            shaped(ocean_map.shape, ocean_map.dtype),
            pltpu.SMEM(cover.shape, cover.dtype),
            pltpu.SMEM(cover_count.shape, cover_count.dtype),
            shaped(weights.shape, weights.dtype),
        ],
        "ah" + "h" * len(later),
        [scratch(ocean_map), pltpu.SemaphoreType.DMA((len(later) + 1,))],
        out_memory="vvssv",
        moved=3_000_000,
    )(ordered, *stay(ocean_map, *later))

    if piece == LANES:
        listed = [place_of(device, twins) for device in range(devices)]
        coupled = lax.all_to_all(
            ordered, everyone, split_axis=0, concat_axis=0, axis_index_groups=[listed], tiled=True
        )
    else:
        outgoing = ordered.reshape(blocks, rows, LANES)[:, :fields].transpose(1, 0, 2).reshape(fields, devices, piece)
        coupled = lax.all_to_all(outgoing, everyone, split_axis=1, concat_axis=1, tiled=True)
        coupled = coupled.reshape(fields, blocks, LANES).transpose(1, 0, 2)
        coupled = jnp.pad(coupled, ((0, 0), (0, rows - fields), (0, 0))).reshape(messages)

    sent = shaped((twins, cap * kinds, ROWS, LANES), jnp.bfloat16)
    tables = shaped((twins,) + table, jnp.bfloat16)
    owns = shaped((twins, cap, ROWS, LANES), jnp.float32)
    work = 2 * twins * cap * table[0] * DEPTH * near_count * LANES
    *outer, tables, owns = call(
        functools.partial(outer_kernel, twins, near_count, fields),
        [sent] * (aparts - 1) + [tables, owns],
        "av" + "v" * twins,
        flops=work * (aparts - 1),
    )(moves, coupled, *selected)
    source = [send(array, "local", 1 + at) for at, array in enumerate(outer)]
    inner = call(
        functools.partial(inner_kernel, near_count, fields),
        sent,
        "vv" + "v" * twins,
        flops=work,
        moved=4_000_000,
    )(tables, owns, *selected)
    source = [inner] + source

    share = ocean_cells // region_count
    packed = share * 2 == LANES
    out_shape = (region_count, ROWS // 2, LANES) if packed else (fields, ocean_cells)
    leaving = call(
        functools.partial(remap_kernel, packed, fields),
        shaped(out_shape, jnp.float32),
        "ssvvv" + "v" * aparts,
        [pltpu.VMEM((local_count, cap * kinds, ROWS, LANES), jnp.bfloat16)],
    )(cover, cover_count, weights, moves, high, *source)
    if packed:
        landed = swap(leaving, "region")
        return call(land_kernel, shaped((fields, ocean_cells), jnp.float32), "v")(landed)
    leaving = leaving.reshape(fields, region_count, share)
    landed = lax.all_to_all(leaving, "region", split_axis=1, concat_axis=1, tiled=True)
    return landed.reshape(fields, ocean_cells)


def solution(mesh):
    return jax.shard_map(
        shards,
        mesh=mesh,
        in_specs=(
            P(None, ("region", "local")),
            P(("region", "local"), None),
            P(None, ("region", "local")),
            P(None, ("region", "local")),
            P(None, ("region", "local")),
            P(("region", "local"), None, None),
            P(("region", "local"), None),
            P(("region", "local")),
            P(("region", "local"), None, None, None, None),
            P(("region", "local"), None),
        ),
        out_specs=P(None, ("region", "local")),
        check_vma=False,
    )
```

```python
import functools

import jax
import jax.numpy as jnp
from jax import lax
from jax.experimental import pallas as pl
from jax.experimental.pallas import tpu as pltpu
from jax.sharding import PartitionSpec as P

ROWS = 16
HALF = 8
LANES = 128
DEPTH = 256
PER_ROW = DEPTH // LANES
STEP = 512
WIDTH = 256
VMEM_LIMIT = 40 * 1024 * 1024


def one_hot(index):
    row = lax.broadcasted_iota(jnp.int32, (DEPTH, index.shape[1]), 0).astype(jnp.bfloat16)
    low = (index & (DEPTH - 1)).astype(jnp.bfloat16)
    return jnp.where(row == low, jnp.bfloat16(1), jnp.bfloat16(0))


def choose(found, high, height):
    high = jnp.broadcast_to(high, (height, found.shape[1]))
    result = found[:height]
    for part in range(1, found.shape[0] // height):
        result = jnp.where(high == part, found[part * height : (part + 1) * height], result)
    return result


def lookup(table, index):
    results = []
    for at in range(0, index.shape[1], WIDTH):
        here = index[:, at : at + WIDTH]
        found = jnp.dot(table, one_hot(here), preferred_element_type=jnp.float32)
        results.append(choose(found, here // DEPTH, ROWS))
    return jnp.concatenate(results, axis=1)


def lookup_dense(table, index, parts):
    results = []
    for at in range(0, index.shape[1], WIDTH):
        here = index[:, at : at + WIDTH]
        found = jnp.dot(table, one_hot(here), preferred_element_type=jnp.float32)
        high = here // DEPTH
        upper = choose(found[: HALF * parts], high, HALF)
        lower = choose(found[HALF * parts :], high // 2, HALF)
        odd = jnp.broadcast_to(high % 2, lower.shape)
        results.append(jnp.concatenate([upper, jnp.where(odd == 1, pltpu.roll(lower, HALF // 2, 0), lower)], axis=0))
    return jnp.concatenate(results, axis=1)


def copies_of(sources, targets, sems, first=0):
    return [
        pltpu.make_async_copy(source, target, sems.at[first + at])
        for at, (source, target) in enumerate(zip(sources, targets))
    ]


def message_rows(fields, twins):
    return 2 * fields if twins == 2 else ROWS


def place_of(device, twins):
    return device ^ 4 if twins == 2 else device


def order_kernel(twins, map_hbm, flux_hbm, out_hbm, map_ref, flux_ref, out_ref, table, sems):
    fields, cells = flux_ref.shape
    steps = cells // STEP
    spans = [pl.ds(at, cells // 4) for at in range(0, cells, cells // 4)]
    needed = copies_of([flux_hbm.at[:, span] for span in spans], [flux_ref.at[:, span] for span in spans], sems)
    needed += copies_of((map_hbm,), (map_ref,), sems, 4)
    for copy in needed:
        copy.start()
    for copy in needed:
        copy.wait()
    parts, rest = cells // DEPTH, fields - HALF
    for part in range(parts):
        columns = slice(part * DEPTH, (part + 1) * DEPTH)
        table[part * HALF : (part + 1) * HALF] = flux_ref[:HALF, columns]
        table[parts * HALF + part * rest : parts * HALF + (part + 1) * rest] = flux_ref[HALF:, columns]
    rows = message_rows(fields, twins)
    written = []
    for step in range(steps):
        found = lookup_dense(table[...], map_ref[:, step * STEP : (step + 1) * STEP], parts)
        pieces = [found[:, at : at + LANES] for at in range(0, STEP, LANES)]
        if twins == 2:
            pieces = [
                jnp.concatenate([pieces[at][:fields], pieces[at ^ 2][:fields]], axis=0) for at in range(len(pieces))
            ]
        for at, piece in enumerate(pieces):
            first = place_of(step * len(pieces) + at, twins) * rows
            out_ref[first : first + rows] = piece.astype(jnp.bfloat16)
        span = pl.ds(place_of(step * len(pieces), twins) * rows, len(pieces) * rows)
        written.append(pltpu.make_async_copy(out_ref.at[span], out_hbm.at[span], sems.at[5 + step]))
        written[-1].start()
    for copy in written:
        copy.wait()


def select_kernel(after_ref, list_hbm, near_hbm, x_hbm, y_hbm, *refs):
    selected, (list_ref, near_ref, x_ref, y_ref, sems) = refs[:-5], refs[-5:]
    copies = copies_of((list_hbm, near_hbm, x_hbm, y_hbm), (list_ref, near_ref, x_ref, y_ref), sems)
    for copy in copies:
        copy.start()
    for copy in copies:
        copy.wait()
    me = lax.axis_index("local")
    cap = list_ref.shape[2]
    count = list_ref.shape[1] // len(selected)
    near_count = near_ref.shape[0]
    for twin, stencil_ref in reversed(list(enumerate(selected))):
        for at in range(count * cap):
            block = list_ref[0, me ^ (2 * twin) ^ (at // cap), at % cap]
            columns = pl.ds(pl.multiple_of(block * LANES, LANES), LANES)
            stencil_ref[at, :near_count] = near_ref[:, columns].astype(jnp.float32)
            stencil_ref[at, near_count : 2 * near_count] = x_ref[:, columns]
            stencil_ref[at, 2 * near_count : 3 * near_count] = y_ref[:, columns]
            rest = (ROWS - 3 * near_count, LANES)
            stencil_ref[at, 3 * near_count :] = jnp.broadcast_to(block, rest).astype(jnp.float32)


def fetch_kernel(after_ref, map_hbm, *refs):
    count = (len(refs) - 4) // 2
    sources, (moves_ref, high_ref), targets, (map_ref, sems) = refs[:count], refs[count : count + 2], refs[count + 2 : -2], refs[-2:]
    (needed,) = copies_of((map_hbm,), (map_ref,), sems, count)
    others = copies_of(sources, targets, sems)
    for copy in [needed] + others:
        copy.start()
    needed.wait()
    moves_ref[...] = one_hot(map_ref[...])
    high_ref[...] = map_ref[...] // DEPTH
    for copy in others:
        copy.wait()


def rebuild(near_count, table, stencil, own, shift):
    near = stencil[:near_count].astype(jnp.int32)
    index = jnp.concatenate([near[j : j + 1] for j in range(near_count)], axis=1)
    found = lookup(table, index)
    upper = lower = own
    slope_x = slope_y = jnp.zeros_like(own)
    for j in range(near_count):
        value = found[:, j * LANES : (j + 1) * LANES]
        change = value - own
        slope_x += stencil[near_count + j : near_count + j + 1] * change
        slope_y += stencil[2 * near_count + j : 2 * near_count + j + 1] * change
        upper, lower = jnp.maximum(upper, value), jnp.minimum(lower, value)
    steep = jnp.abs(slope_x) + jnp.abs(slope_y)
    factor = jnp.minimum(1.0, (upper - lower) / jnp.maximum(steep, 1.0))
    results = [own, factor * slope_x, factor * slope_y]
    if shift:
        spare = jnp.zeros((shift, LANES), jnp.float32)
        results = [jnp.concatenate([result[shift:], spare], axis=0) for result in results]
    return results


def own_cells(near_count, table, stencil_ref):
    slots = stencil_ref.shape[0]
    tile = (ROWS, DEPTH)
    column = lax.broadcasted_iota(jnp.int32, tile, 1) - lax.broadcasted_iota(jnp.int32, tile, 0)
    blocks = [stencil_ref[at, 3 * near_count : 3 * near_count + 1].astype(jnp.int32) for at in range(slots)]
    picks = [
        jnp.where(jnp.concatenate([block // PER_ROW * ROWS] * PER_ROW, axis=1) == column, 1.0, 0.0) for block in blocks
    ]
    found = jnp.dot(
        jnp.concatenate(picks, axis=0).astype(jnp.bfloat16), table, preferred_element_type=jnp.float32
    )
    owns = []
    for at, block in enumerate(blocks):
        rows = found[at * ROWS : (at + 1) * ROWS]
        odd = jnp.broadcast_to(block % PER_ROW, (ROWS, LANES))
        owns.append(jnp.where(odd == 1, rows[:, LANES:], rows[:, :LANES]))
    return owns


def outer_kernel(twins, near_count, fields, after_ref, cells_ref, *refs):
    selected, refs = refs[:twins], refs[twins:]
    out_refs, (tables, owns) = refs[:-2], refs[-2:]
    cap = owns.shape[1]
    rows = message_rows(fields, twins)
    for twin in range(twins):
        for block in range(tables.shape[1] // ROWS * PER_ROW):
            part, column = block // PER_ROW, block % PER_ROW * LANES
            first = place_of(block, twins) * rows + HALF * twin
            tables[twin, part * ROWS : (part + 1) * ROWS, column : column + LANES] = cells_ref[first : first + ROWS]
    for twin, stencil_ref in enumerate(selected):
        for at, own in enumerate(own_cells(near_count, tables[twin], stencil_ref)):
            if at < cap:
                owns[twin, at] = own
                continue
            shift = twin * (fields - HALF)
            results = rebuild(near_count, tables[twin], stencil_ref[at], own, shift)
            for kind, result in enumerate(results):
                out_refs[at // cap - 1][twin, at % cap * len(results) + kind] = result.astype(jnp.bfloat16)


def inner_kernel(near_count, fields, tables, owns, *refs):
    selected, out_ref = refs[:-1], refs[-1]
    for twin, stencil_ref in enumerate(selected):
        for at in range(owns.shape[1]):
            own = owns[twin, at]
            shift = twin * (fields - HALF)
            results = rebuild(near_count, tables[twin], stencil_ref[at], own, shift)
            for kind, result in enumerate(results):
                out_ref[twin, at * len(results) + kind] = result.astype(jnp.bfloat16)


def remap_kernel(packed, fields, cover_ref, count_ref, weight_ref, moves_ref, high_ref, *refs):
    received, (out_ref, source_ref) = refs[:-2], refs[-2:]
    me = lax.axis_index("local")
    ocean_blocks, slots, kinds = weight_ref.shape[:3]
    cap = source_ref.shape[1] // kinds
    for apart, piece_ref in enumerate(received):
        for twin in range(piece_ref.shape[0]):
            source_ref[me ^ apart ^ (2 * twin)] = piece_ref[twin]
    results = []
    for block in range(ocean_blocks):
        values, weights = [], []
        for slot in range(slots):
            at = cover_ref[block, slot]
            live = slot < count_ref[block]
            for kind in range(kinds):
                value = source_ref[at // cap, at % cap * kinds + kind]
                values.append(jnp.where(live, value, jnp.zeros_like(value)))
                weights.append(weight_ref[block, slot, kind])
        product = lax.dot_general(
            jnp.concatenate(values, axis=1),
            jnp.concatenate(weights, axis=1),
            (((1,), (1,)), ((), ())),
            preferred_element_type=jnp.float32,
        )
        results.append(product)
    remapped = jnp.concatenate(results, axis=1)
    cells = remapped.shape[1]
    coarse = remapped.astype(jnp.bfloat16)
    fine = (remapped - coarse.astype(jnp.float32)).astype(jnp.bfloat16)
    table = [part[:, at : at + DEPTH] for at in range(0, cells, DEPTH) for part in (coarse, fine)]
    moved = jnp.dot(jnp.concatenate(table, axis=0), moves_ref[...], preferred_element_type=jnp.float32)
    moved = choose(moved, high_ref[...], 2 * ROWS)
    moved = moved[:ROWS] + moved[ROWS:]
    if not packed:
        out_ref[...] = moved[:fields]
        return
    half = fields // 2
    rows = out_ref.shape[1]
    listed = listing(out_ref.shape[0])
    side = lax.broadcasted_iota(jnp.int32, (rows, LANES), 1) < LANES // 2
    for pair in range(cells // LANES):
        columns = moved[:, pair * LANES : (pair + 1) * LANES]
        first, second = columns[:rows], columns[half : half + rows]
        out_ref[listed.index(2 * pair)] = jnp.where(side, first, pltpu.roll(second, LANES // 2, 1))
        out_ref[listed.index(2 * pair + 1)] = jnp.where(side, pltpu.roll(first, LANES // 2, 1), second)


def land_kernel(landed_ref, out_ref):
    count = landed_ref.shape[0]
    listed = listing(count)
    half = out_ref.shape[0] // 2
    side = lax.broadcasted_iota(jnp.int32, (half, LANES), 1) < LANES // 2
    for pair in range(count // 2):
        even, odd = landed_ref[listed.index(2 * pair), :half], landed_ref[listed.index(2 * pair + 1), :half]
        columns = pl.ds(pair * LANES, LANES)
        out_ref[:half, columns] = jnp.where(side, even, pltpu.roll(odd, LANES // 2, 1))
        out_ref[half:, columns] = jnp.where(side, pltpu.roll(even, LANES // 2, 1), odd)


def send(array, axis, apart):
    return lax.ppermute(array, axis, [(at, at ^ apart) for at in range(lax.axis_size(axis))])


def listing(count):
    return sorted(range(count), key=lambda at: (abs(2 * at - count + 1), -at))


def swap(pieces, axis):
    groups = [listing(lax.axis_size(axis))]
    pieces = pieces.transpose(1, 0, 2)
    swapped = lax.all_to_all(pieces, axis, split_axis=1, concat_axis=1, axis_index_groups=groups, tiled=True)
    return swapped.transpose(1, 0, 2)


SPACES = {"s": pltpu.SMEM, "v": pltpu.VMEM, "h": pltpu.HBM, "a": pl.ANY}


def call(kernel, outs, memories, scratch=(), out_memory="v", flops=0, moved=0):
    if isinstance(outs, list):
        out_specs = [pl.BlockSpec(memory_space=SPACES[kind]) for kind in (out_memory * len(outs))[: len(outs)]]
    else:
        out_specs = pl.BlockSpec(memory_space=SPACES[out_memory])
    return pl.pallas_call(
        kernel,
        out_shape=outs,
        in_specs=[pl.BlockSpec(memory_space=SPACES[kind]) for kind in memories],
        out_specs=out_specs,
        scratch_shapes=list(scratch),
        cost_estimate=pl.CostEstimate(flops=flops, bytes_accessed=moved, transcendentals=0),
        compiler_params=pltpu.CompilerParams(vmem_limit_bytes=VMEM_LIMIT),
    )


def shards(
    atm_flux,
    cell_map,
    neighbours,
    coef_x,
    coef_y,
    send_list,
    cover,
    cover_count,
    weights,
    ocean_map,
):
    fields, cells = atm_flux.shape
    region_count = lax.axis_size("region")
    local_count = lax.axis_size("local")
    everyone = ("region", "local")
    devices = region_count * local_count
    piece = cells // devices
    blocks = cells // LANES
    table = (cells // DEPTH * ROWS, DEPTH)
    shaped = jax.ShapeDtypeStruct
    twins = 2 if local_count == 4 and piece == LANES else 1
    cap = send_list.shape[2]
    aparts = local_count // twins
    near_count = neighbours.shape[0]
    kinds = weights.shape[2]
    ocean_cells = ocean_map.shape[1]

    def stay(*arrays):
        return [pltpu.with_memory_space_constraint(array, pltpu.HBM) for array in arrays]

    def scratch(array):
        return pltpu.VMEM(array.shape, array.dtype)

    rows = message_rows(fields, twins)
    messages = (blocks * rows, LANES)
    ordered = call(
        functools.partial(order_kernel, twins),
        shaped(messages, jnp.bfloat16),
        "hh",
        [
            scratch(cell_map),
            scratch(atm_flux),
            pltpu.VMEM(messages, jnp.bfloat16),
            pltpu.VMEM((cells // DEPTH * fields, DEPTH), jnp.bfloat16),
            pltpu.SemaphoreType.DMA((cells // STEP + 5,)),
        ],
        out_memory="h",
    )(*stay(cell_map, atm_flux))

    stencil = shaped((aparts * cap, ROWS, LANES), jnp.float32)
    selected = call(
        select_kernel,
        [stencil] * twins,
        "ahhhh",
        [
            pltpu.SMEM(send_list.shape, send_list.dtype),
            scratch(neighbours),
            scratch(coef_x),
            scratch(coef_y),
            pltpu.SemaphoreType.DMA((4,)),
        ],
        moved=3_000_000,
    )(ordered, *stay(send_list, neighbours, coef_x, coef_y))
    selected = [selected[0]] + [send(array, "local", 2) for array in selected[1:]]

    later = [cover, cover_count, weights]
    moves, high, cover, cover_count, weights = call(
        fetch_kernel,
        [
            shaped((DEPTH, ocean_cells), jnp.bfloat16),
            shaped(ocean_map.shape, ocean_map.dtype),
            pltpu.SMEM(cover.shape, cover.dtype),
            pltpu.SMEM(cover_count.shape, cover_count.dtype),
            shaped(weights.shape, weights.dtype),
        ],
        "ah" + "h" * len(later),
        [scratch(ocean_map), pltpu.SemaphoreType.DMA((len(later) + 1,))],
        out_memory="vvssv",
        moved=3_000_000,
    )(ordered, *stay(ocean_map, *later))

    if piece == LANES:
        listed = [place_of(device, twins) for device in range(devices)]
        coupled = lax.all_to_all(
            ordered, everyone, split_axis=0, concat_axis=0, axis_index_groups=[listed], tiled=True
        )
    else:
        outgoing = ordered.reshape(blocks, rows, LANES)[:, :fields].transpose(1, 0, 2).reshape(fields, devices, piece)
        coupled = lax.all_to_all(outgoing, everyone, split_axis=1, concat_axis=1, tiled=True)
        coupled = coupled.reshape(fields, blocks, LANES).transpose(1, 0, 2)
        coupled = jnp.pad(coupled, ((0, 0), (0, rows - fields), (0, 0))).reshape(messages)

    sent = shaped((twins, cap * kinds, ROWS, LANES), jnp.bfloat16)
    tables = shaped((twins,) + table, jnp.bfloat16)
    owns = shaped((twins, cap, ROWS, LANES), jnp.float32)
    work = 2 * twins * cap * table[0] * DEPTH * near_count * LANES
    *outer, tables, owns = call(
        functools.partial(outer_kernel, twins, near_count, fields),
        [sent] * (aparts - 1) + [tables, owns],
        "av" + "v" * twins,
        flops=work * (aparts - 1),
    )(moves, coupled, *selected)
    source = [send(array, "local", 1 + at) for at, array in enumerate(outer)]
    inner = call(
        functools.partial(inner_kernel, near_count, fields),
        sent,
        "vv" + "v" * twins,
        flops=work,
        moved=4_000_000,
    )(tables, owns, *selected)
    source = [inner] + source

    share = ocean_cells // region_count
    packed = share * 2 == LANES
    out_shape = (region_count, ROWS // 2, LANES) if packed else (fields, ocean_cells)
    leaving = call(
        functools.partial(remap_kernel, packed, fields),
        shaped(out_shape, jnp.float32),
        "ssvvv" + "v" * aparts,
        [pltpu.VMEM((local_count, cap * kinds, ROWS, LANES), jnp.bfloat16)],
    )(cover, cover_count, weights, moves, high, *source)
    if packed:
        landed = swap(leaving, "region")
        return call(land_kernel, shaped((fields, ocean_cells), jnp.float32), "v")(landed)
    leaving = leaving.reshape(fields, region_count, share)
    landed = lax.all_to_all(leaving, "region", split_axis=1, concat_axis=1, tiled=True)
    return landed.reshape(fields, ocean_cells)


def solution(mesh):
    return jax.shard_map(
        shards,
        mesh=mesh,
        in_specs=(
            P(None, ("region", "local")),
            P(("region", "local"), None),
            P(None, ("region", "local")),
            P(None, ("region", "local")),
            P(None, ("region", "local")),
            P(("region", "local"), None, None),
            P(("region", "local"), None),
            P(("region", "local")),
            P(("region", "local"), None, None, None, None),
            P(("region", "local"), None),
        ),
        out_specs=P(None, ("region", "local")),
        check_vma=False,
    )
```
